32 devices in a mesh: copy: 2 (over y), dp: 4 (over x, core), fsdp: 4 (over z).
Axes of the slice: x: 2, y: 2, z: 4, core: 2. Of those that a mesh axis runs over, the one named last changes fastest.
Arguments:
- queries: bfloat16 [2, 16, 256, 2560], P('copy', ('dp', 'fsdp')), may hold values from -25 to 25
- keys: bfloat16 [2, 16, 256, 2560], P('copy', ('dp', 'fsdp')), may hold values from -25 to 25
- values: bfloat16 [2, 16, 256, 2560], P('copy', ('dp', 'fsdp')), may hold values from -6 to 6
- residual: bfloat16 [2, 16, 256, 2560], P('copy', ('dp', 'fsdp')), may hold values from -6 to 6
- event_ids: int32 [16, 256], P(('dp', 'fsdp')), may hold values from 0 to 1023
- lengths: int32 [16], replicated, may hold values from 8 to 256, as said below
- type_weight: float32 [1024], replicated, may hold values from 0.25 to 4
- w_out: bfloat16 [2, 2560, 2560], P('copy', 'fsdp'), may hold values from -0.125 to 0.125
- gain: float32 [2, 2560], P('copy'), may hold values from 0.5 to 1.5
Outputs:
- loss: float32 [2, 16], P('copy', ('dp', 'fsdp'))
- d_queries: bfloat16 [2, 16, 256, 2560], P('copy', ('dp', 'fsdp'))
- d_keys: bfloat16 [2, 16, 256, 2560], P('copy', ('dp', 'fsdp'))
- d_values: bfloat16 [2, 16, 256, 2560], P('copy', ('dp', 'fsdp'))
- d_wo: float32 [2, 2560, 2560], P('copy', 'fsdp')
The draws below stay inside these ranges and needn't reach their ends.
Inputs may be any that keep to these rules, and one draw needn't show every extreme that they name: `lengths`: every history has at least 8 valid events and some history has all 256.
All inputs are finite; a program needn't handle non-finite values.
Results may differ from the reference program's by a relative error of at most 0.02.
Values may be sent and summed in bfloat16 or wider, within the bound.
No kernel may reach another device: no remote copies, remote signals or barrier semaphores. Data moves between devices by JAX's collectives and lax.ppermute only.
A program may use at most 128 MiB of HBM per device.

```python
import math
import jax
import jax.numpy as jnp
import numpy as np
from jax import lax

D = 2560
H = 20
DH = 128
L = 256
TYPES = 1024
HD = 2560
HISTS = 16


def drawn_pair(key):
    query_key = jax.random.fold_in(key, 11)
    key_key = jax.random.fold_in(key, 12)
    shape = (2, HISTS, L, H, DH)
    query_draw = jnp.clip(jax.random.normal(query_key, shape, jnp.float32), -6.0, 6.0)
    key_draw = jnp.clip(jax.random.normal(key_key, shape, jnp.float32), -6.0, 6.0)
    return (query_draw.reshape(2, HISTS, L, HD), key_draw.reshape(2, HISTS, L, HD))


def draw_queries(key, part):
    return drawn_pair(key)[0].astype(jnp.bfloat16)


def draw_keys(key, part):
    return drawn_pair(key)[1].astype(jnp.bfloat16)


def draw_lengths(key, part):
    drawn = jax.random.randint(jax.random.fold_in(key, 21), (HISTS,), 8, L + 1, dtype=jnp.int32)
    return drawn.at[0].set(L)


def set_ends(values, stream_key, smallest, largest):
    spot = [jax.random.randint(jax.random.fold_in(stream_key, axis), (), 0, length) for axis, length in enumerate(values.shape)]
    longest = values.shape.index(max(values.shape))
    next_to = spot[:longest] + [(spot[longest] + 1) % values.shape[longest]] + spot[longest + 1:]
    return values.at[tuple(spot)].set(smallest).at[tuple(next_to)].set(largest)


def block_levels(stream_key, dims, split, low, largest):
    def one(axis_at, blocks):
        steps = jax.random.uniform(jax.random.fold_in(jax.random.fold_in(stream_key, 6), axis_at), (blocks,), jnp.float32, low / len(split), largest / len(split))
        return jnp.repeat(jnp.exp(steps), dims[axis_at] // blocks).reshape((-1,) + (1,) * (len(dims) - axis_at - 1))

    level = one(*split[0])
    for cut in split[1:]:
        level = level * one(*cut)
    return level


def rank_bounds(amount, skew):
    portions = [(1 << 20) // math.isqrt(standing ** skew) + 1 for standing in range(1, amount + 1)]
    scale = 1 + sum(portions) // (1 << 30)
    return np.cumsum(np.array([max(1, weight // scale) for weight in portions]))


def ranked(stream_key, extent, number_of, lean):
    listing = rank_bounds(number_of, lean)
    ticket = jax.random.randint(jax.random.fold_in(stream_key, 1), extent, 0, int(listing[number_of - 1]))
    rank = jnp.searchsorted(jnp.asarray(listing, jnp.int32), ticket, side="right")
    return jax.random.permutation(jax.random.fold_in(stream_key, 2), number_of)[rank].astype(jnp.int32)


def bell_draw(own_key, shape, deviation, limit, pieces=(), kind=jnp.bfloat16):
    result = deviation * jax.random.normal(own_key, shape, jnp.float32)
    if pieces:
        result = result * block_levels(own_key, shape, pieces, -0.22, 0.18)
    return jnp.clip(result, -limit, limit).astype(kind)


def setup_inputs(seed: int = 0) -> dict:
    arg_keys = jax.random.split(jax.random.key(seed), 10)
    return {
        "queries": draw_queries(jax.random.fold_in(arg_keys[9], 71), 0),
        "keys": draw_keys(jax.random.fold_in(arg_keys[9], 71), 0),
        "values": bell_draw(arg_keys[2], (2, HISTS, L, HD), 1.0, 6.0, ((0, 2), (1, 16))),
        "residual": bell_draw(arg_keys[3], (2, HISTS, L, D), 1.0, 6.0, ((0, 2), (1, 16))),
        "event_ids": set_ends(ranked(arg_keys[4], (HISTS, L), TYPES, 2), jax.random.fold_in(arg_keys[4], 3), 0, TYPES - 1).astype(jnp.int32),
        "lengths": draw_lengths(jax.random.fold_in(arg_keys[9], 71), 0),
        "type_weight": jnp.clip(jnp.exp(jax.random.uniform(arg_keys[6], (TYPES,), jnp.float32, math.log(0.25), math.log(4.0))), 0.25, 4.0),
        "w_out": bell_draw(arg_keys[7], (2, HD, D), HD ** -0.5, 0.125, ((0, 2), (1, 4))),
        "gain": jnp.clip(1.0 + 0.1 * jax.random.normal(arg_keys[8], (2, D), jnp.float32), 0.5, 1.5),
    }


def attention_forward(queries, keys, values, residual, w_out, gain, length):
    query_heads = queries.reshape(L, H, DH).astype(jnp.float32)
    key_heads = keys.reshape(L, H, DH).astype(jnp.float32)
    value_heads = values.reshape(L, H, DH).astype(jnp.float32)
    scores = jnp.einsum('qhd,khd->hqk', query_heads, key_heads) / jnp.sqrt(jnp.float32(DH))
    rows = jnp.arange(L, dtype=jnp.int32)[:, None]
    cols = jnp.arange(L, dtype=jnp.int32)[None, :]
    valid = (cols <= rows) & (cols < length)
    scores = jnp.where(valid[None], scores, jnp.float32(-1e+30))
    probs = jax.nn.softmax(scores, axis=-1)
    probs_b = probs.astype(jnp.bfloat16)
    attn = jnp.einsum('hqk,khd->qhd', probs_b.astype(jnp.float32), value_heads).reshape(L, HD).astype(jnp.bfloat16)
    hidden = residual.astype(jnp.float32) + jnp.dot(attn, w_out, preferred_element_type=jnp.float32)
    inv = lax.rsqrt(lax.optimization_barrier(jnp.mean(hidden * hidden, axis=-1, keepdims=True)) + 1e-06)
    normed = hidden * inv
    feat = normed * gain[None, :]
    return (probs, probs_b, attn, inv, normed, feat)

def attention_backward(queries, keys, values, w_out, gain, probs, probs_b, attn, inv, normed, feat, partner, tok_w, count):
    diff = feat - partner.astype(jnp.float32)
    loss = jnp.sum(tok_w * lax.optimization_barrier(jnp.sum(diff * diff, axis=-1))) / (D * count)
    dfeat = 2.0 * tok_w[:, None] * diff / (D * count)
    scaled = dfeat * gain[None, :]
    d_hidden = (inv * (scaled - normed * lax.optimization_barrier(jnp.mean(normed * scaled, axis=-1, keepdims=True)))).astype(jnp.bfloat16)
    partial_value = jnp.dot(attn.T, d_hidden, preferred_element_type=jnp.float32).astype(jnp.bfloat16).astype(jnp.float32)
    d_attn = jnp.dot(d_hidden, w_out.T, preferred_element_type=jnp.float32).astype(jnp.bfloat16)
    d_heads = d_attn.reshape(L, H, DH).astype(jnp.float32)
    query_heads = queries.reshape(L, H, DH).astype(jnp.float32)
    key_heads = keys.reshape(L, H, DH).astype(jnp.float32)
    value_heads = values.reshape(L, H, DH).astype(jnp.float32)
    d_values = jnp.einsum('hqk,qhd->khd', probs_b.astype(jnp.float32), d_heads).reshape(L, HD).astype(jnp.bfloat16)
    dprob = jnp.einsum('qhd,khd->hqk', d_heads, value_heads)
    delta = lax.optimization_barrier(jnp.sum(dprob * probs, axis=-1, keepdims=True))
    ds = (probs * (dprob - delta) / jnp.sqrt(jnp.float32(DH))).astype(jnp.bfloat16).astype(jnp.float32)
    d_queries = jnp.einsum('hqk,khd->qhd', ds, key_heads).reshape(L, HD).astype(jnp.bfloat16)
    d_keys = jnp.einsum('hqk,qhd->khd', ds, query_heads).reshape(L, HD).astype(jnp.bfloat16)
    return (loss, d_queries, d_keys, d_values, partial_value)

def reference(queries, keys, values, residual, event_ids, lengths, type_weight, w_out, gain):
    count = jnp.sum(lengths).astype(jnp.float32)
    forward = jax.vmap(attention_forward, in_axes=(0, 0, 0, 0, 0, 0, None))
    backward = jax.vmap(attention_backward, in_axes=(0, 0, 0, 0, 0, 0, 0, 0, 0, 0, 0, 0, None, None))

    def one_history(carry, index):
        q_hist = queries[:, index]
        k_hist = keys[:, index]
        v_hist = values[:, index]
        x_hist = residual[:, index]
        length = lengths[index]
        probs, probs_b, attn, inv, normed, feat = forward(q_hist, k_hist, v_hist, x_hist, w_out, gain, length)
        partner = feat.astype(jnp.bfloat16)[::-1]
        live = jnp.arange(L, dtype=jnp.int32) < length
        tok_w = jnp.where(live, type_weight[event_ids[index]], jnp.float32(0.0))
        loss, d_q, d_k, d_v, partial_value = backward(q_hist, k_hist, v_hist, w_out, gain, probs, probs_b, attn, inv, normed, feat, partner, tok_w, count)
        return (carry + partial_value, (loss, d_q, d_k, d_v))
    start = jnp.zeros((2, HD, D), jnp.float32)
    d_wo, (loss, d_q, d_k, d_v) = lax.scan(one_history, start, jnp.arange(HISTS, dtype=jnp.int32))
    return (jnp.transpose(loss, (1, 0)), jnp.transpose(d_q, (1, 0, 2, 3)), jnp.transpose(d_k, (1, 0, 2, 3)), jnp.transpose(d_v, (1, 0, 2, 3)), d_wo)
```

```python
import jax
import jax.numpy as jnp
from jax import lax
from jax.experimental import pallas as pl
from jax.experimental.pallas import tpu as pltpu
from jax.sharding import PartitionSpec as P

DH = 128
LANES = 128
NEG = -1e30


def swap(value, axis, bit):
    return lax.ppermute(value, axis, [(i, i ^ bit) for i in range(lax.axis_size(axis))])


def bits_of(size):
    return [1 << j for j in range(size.bit_length() - 1)]


def ring_shift(value, axis):
    size = lax.axis_size(axis)
    return lax.ppermute(value, axis, [(i, (i + 1) % size) for i in range(size)])


def head_probs(query, key, valid):
    scores = lax.dot_general(query, key, (((1,), (1,)), ((), ())), preferred_element_type=jnp.float32)
    scores = jnp.where(valid, scores * (DH**-0.5), NEG)
    top = jnp.max(scores, axis=-1, keepdims=True)
    exps = jnp.exp(scores - top)
    return exps * (1.0 / jnp.sum(exps, axis=-1, keepdims=True))


def valid_mask(seq, length):
    rows = lax.broadcasted_iota(jnp.int32, (seq, seq), 0)
    cols = lax.broadcasted_iota(jnp.int32, (seq, seq), 1)
    return (cols <= rows) & (cols < length)


def forward_kernel(length_ref, q_ref, k_ref, v_ref, out_ref):
    seq, wide = q_ref.shape
    valid = valid_mask(seq, length_ref[0])
    for head in range(wide // DH):
        at = slice(head * DH, (head + 1) * DH)
        probs = head_probs(q_ref[:, at], k_ref[:, at], valid).astype(jnp.bfloat16)
        out_ref[:, at] = jnp.dot(probs, v_ref[:, at], preferred_element_type=jnp.float32).astype(out_ref.dtype)


def backward_kernel(length_ref, q_ref, k_ref, v_ref, one_ref, two_ref, dq_ref, dk_ref, dv_ref):
    seq, wide = q_ref.shape
    valid = valid_mask(seq, length_ref[0])
    for head in range(wide // DH):
        at = slice(head * DH, (head + 1) * DH)
        query, key, value = q_ref[:, at], k_ref[:, at], v_ref[:, at]
        probs = head_probs(query, key, valid)
        d_attn = (one_ref[:, at].astype(jnp.float32) + two_ref[:, at].astype(jnp.float32)).astype(jnp.bfloat16)
        dv_ref[:, at] = lax.dot_general(
            probs.astype(jnp.bfloat16), d_attn, (((0,), (0,)), ((), ())), preferred_element_type=jnp.float32
        ).astype(dv_ref.dtype)
        dprob = lax.dot_general(d_attn, value, (((1,), (1,)), ((), ())), preferred_element_type=jnp.float32)
        delta = jnp.sum(dprob * probs, axis=-1, keepdims=True)
        ds = (probs * (dprob - delta) * (DH**-0.5)).astype(jnp.bfloat16)
        dq_ref[:, at] = jnp.dot(ds, key, preferred_element_type=jnp.float32).astype(dq_ref.dtype)
        dk_ref[:, at] = lax.dot_general(
            ds, query, (((0,), (0,)), ((), ())), preferred_element_type=jnp.float32
        ).astype(dk_ref.dtype)


def group_width(heads_width):
    heads = heads_width // DH
    return DH * max(g for g in (4, 2, 1) if heads % g == 0)


def attention_call(kernel, length, arrays, outs, products):
    seq, wide = arrays[0].shape
    group = group_width(wide)
    block = pl.BlockSpec((seq, group), lambda i, *_: (0, i))
    shape = jax.ShapeDtypeStruct((seq, wide), jnp.bfloat16)
    return pl.pallas_call(
        kernel,
        grid_spec=pltpu.PrefetchScalarGridSpec(
            num_scalar_prefetch=1,
            grid=(wide // group,),
            in_specs=[block] * len(arrays),
            out_specs=[block] * outs,
        ),
        out_shape=[shape] * outs,
        cost_estimate=pl.CostEstimate(
            flops=products * 2 * seq * seq * wide,
            bytes_accessed=2 * seq * wide * (len(arrays) + outs),
            transcendentals=seq * seq * wide // DH,
        ),
        compiler_params=pltpu.CompilerParams(vmem_limit_bytes=32 << 20),
    )(length.reshape(1), *arrays)


def chunks_of(wide):
    lanes = -(-wide // LANES)
    first = min(wide, -(-lanes * 3 // 5) * LANES)
    return [(0, first), (first, wide)] if first < wide else [(0, wide)]


def body(queries, keys, values, residual, event_ids, lengths, type_weight, w_out, gain):
    seq, heads_width = queries.shape[2:]
    width = residual.shape[3]
    parts = lax.axis_size("fsdp")
    team = lax.axis_size("dp")
    bits = bits_of(team)
    shard_rows = w_out.shape[1]
    part = lax.axis_index("fsdp")
    member = lax.axis_index("dp")
    own = lax.axis_index(("dp", "fsdp"))
    length = lengths[own]
    count = jnp.sum(lengths).astype(jnp.float32)
    wide = width // team
    chunks = chunks_of(wide)

    weights = []
    for low, high in chunks:
        block = lax.dynamic_slice(w_out[0], (0, member * wide + low), (shard_rows, high - low))
        whole = jnp.zeros((heads_width, high - low), block.dtype)
        whole = lax.dynamic_update_slice(whole, block, (part * shard_rows, 0))
        for step in range(1, parts):
            block = ring_shift(block, "fsdp")
            at = lax.rem(part + parts - step, parts) * shard_rows
            whole = lax.dynamic_update_slice(whole, block, (at, 0))
        weights.append(whole)

    order = [0]
    for bit in reversed(bits):
        order = order + [s ^ bit for s in order]

    home = residual[0, 0]
    rest = {}
    for s in order:
        block = lax.dynamic_slice(home, (0, (member ^ s) * wide), (seq, wide))
        rest[s] = swap(block, "dp", s) if s else block
    rest = jnp.concatenate([rest[s] for s in order], axis=0)

    types = jnp.arange(type_weight.shape[0], dtype=jnp.int32)
    matches = event_ids[0][:, None] == types[None, :]
    looked_up = jnp.sum(jnp.where(matches, type_weight[None, :], jnp.float32(0.0)), axis=-1)
    tok_w = jnp.where(jnp.arange(seq, dtype=jnp.int32) < length, looked_up, jnp.float32(0.0))
    tok_w = tok_w.reshape(1, seq)
    for bit in reversed(bits):
        tok_w = jnp.concatenate([tok_w, swap(tok_w, "dp", bit)], axis=0)
    tok_w = tok_w.reshape(-1, 1)

    q, k, v = queries[0, 0], keys[0, 0], values[0, 0]
    (attn_own,) = attention_call(forward_kernel, length, (q, k, v), 1, 2)
    attn = [attn_own]
    for bit in reversed(bits):
        attn = attn + [swap(a, "dp", bit) for a in attn]
    attn = jnp.concatenate(attn, axis=0)

    def team_sum(value):
        value = value.reshape((2,) * len(bits) + (-1,))
        for axis, bit in enumerate(bits):
            value = value + jnp.flip(swap(value, "dp", bit), axis)
        return value.reshape(team * seq, -1)

    my_gain = lax.dynamic_slice(gain[0], (member * wide,), (wide,))
    hidden, sent, gains = [], [], []
    for (low, high), weight in zip(chunks, weights):
        h = rest[:, low:high].astype(jnp.float32) + jnp.dot(attn, weight, preferred_element_type=jnp.float32)
        g = my_gain[None, low:high]
        hidden.append(h)
        gains.append(g)
        sent.append(swap((h * g).astype(jnp.bfloat16), "copy", 1))
    square = sum(jnp.sum(h * h, axis=-1, keepdims=True) for h in hidden)
    inv = lax.rsqrt(team_sum(square) / width + 1e-06)
    inv_other = swap(inv, "copy", 1)

    normed = [h * inv for h in hidden]
    diff = [n * g - p.astype(jnp.float32) * inv_other for n, g, p in zip(normed, gains, sent)]
    scaled = [2.0 * tok_w * d / (width * count) * g for d, g in zip(diff, gains)]
    square = sum(jnp.sum(d * d, axis=-1, keepdims=True) for d in diff)
    cross = sum(jnp.sum(n * s, axis=-1, keepdims=True) for n, s in zip(normed, scaled))
    both = team_sum(jnp.concatenate([square, cross], axis=1))
    loss = jnp.sum(tok_w[:seq] * both[:seq, :1]) / (width * count)
    mean = both[:, 1:] / width
    d_hidden = [(inv * (s - n * mean)).astype(jnp.bfloat16) for s, n in zip(scaled, normed)]

    d_attn = sum(
        lax.dot_general(d, w, (((1,), (1,)), ((), ())), preferred_element_type=jnp.float32)
        for d, w in zip(d_hidden, weights)
    ).astype(jnp.bfloat16)
    for bit in bits[:-1]:
        half = d_attn.shape[0] // 2
        d_attn = (d_attn[:half].astype(jnp.float32) + swap(d_attn[half:], "dp", bit).astype(jnp.float32)).astype(jnp.bfloat16)
    kept, got = d_attn[:seq], swap(d_attn[seq:], "dp", bits[-1])
    d_queries, d_keys, d_values = attention_call(backward_kernel, length, (q, k, v, kept, got), 3, 5)

    out = jnp.zeros((shard_rows, width), jnp.float32)
    for (low, high), d in zip(chunks, d_hidden):
        terms = lax.dot_general(attn, d, (((0,), (0,)), ((), ())), preferred_element_type=jnp.float32).astype(jnp.bfloat16)

        def term(step):
            at = lax.rem(part + parts - step, parts) * shard_rows
            return lax.dynamic_slice(terms, (at, 0), (shard_rows, high - low))

        total = term(1 % parts)
        for step in range(1, parts):
            got = ring_shift(total, "fsdp")
            total = (got.astype(jnp.float32) + term((step + 1) % parts).astype(jnp.float32)).astype(jnp.bfloat16)
        pieces = {0: total}
        for bit in reversed(bits):
            pieces.update({s ^ bit: swap(p, "dp", bit) for s, p in pieces.items()})
        for s, piece in pieces.items():
            out = lax.dynamic_update_slice(out, piece.astype(jnp.float32), (0, (member ^ s) * wide + low))
    return (
        loss.reshape(1, 1),
        d_queries[None, None],
        d_keys[None, None],
        d_values[None, None],
        out[None],
    )


def solution(mesh):
    whole = P("copy", ("dp", "fsdp"), None, None)
    in_specs = (
        whole,
        whole,
        whole,
        whole,
        P(("dp", "fsdp"), None),
        P(),
        P(),
        P("copy", "fsdp", None),
        P("copy", None),
    )
    out_specs = (P("copy", ("dp", "fsdp")), whole, whole, whole, P("copy", "fsdp", None))
    return jax.shard_map(body, mesh=mesh, in_specs=in_specs, out_specs=out_specs, check_vma=False)
```

```python
import functools
import math

import jax
import jax.numpy as jnp
from jax import lax
from jax.experimental import pallas as pl
from jax.experimental.pallas import tpu as pltpu
from jax.sharding import PartitionSpec as P

DH = 128
LANES = 128
NEG = -1e30
MIB = 1 << 20
SCALE = MIB


def cost(micros):
    return pl.CostEstimate(flops=0, bytes_accessed=int(micros * SCALE), transcendentals=0)


def vmem(blocks):
    size = sum(math.prod(shape) * jnp.dtype(kind).itemsize for shape, kind in blocks)
    return pltpu.CompilerParams(vmem_limit_bytes=min(2 * size + 6 * MIB, 60 * MIB))


def swap(value, axis, bit):
    return lax.ppermute(value, axis, [(i, i ^ bit) for i in range(lax.axis_size(axis))])


def bits_of(size):
    return [1 << j for j in range(size.bit_length() - 1)]


def head_probs(query, key, valid):
    scores = lax.dot_general(query, key, (((1,), (1,)), ((), ())), preferred_element_type=jnp.float32)
    scores = jnp.where(valid, scores * (DH**-0.5), NEG)
    top = jnp.max(scores, axis=-1, keepdims=True)
    exps = jnp.exp(scores - top)
    return exps * (1.0 / jnp.sum(exps, axis=-1, keepdims=True))


def valid_mask(seq, length):
    rows = lax.broadcasted_iota(jnp.int32, (seq, seq), 0)
    cols = lax.broadcasted_iota(jnp.int32, (seq, seq), 1)
    return (cols <= rows) & (cols < length)


def forward_kernel(length_ref, q_ref, k_ref, v_ref, out_ref):
    seq, wide = q_ref.shape
    valid = valid_mask(seq, length_ref[0])
    for head in range(wide // DH):
        at = slice(head * DH, (head + 1) * DH)
        probs = head_probs(q_ref[:, at], k_ref[:, at], valid).astype(jnp.bfloat16)
        out_ref[:, at] = jnp.dot(probs, v_ref[:, at], preferred_element_type=jnp.float32).astype(out_ref.dtype)


def backward_kernel(length_ref, q_ref, k_ref, v_ref, one_ref, two_ref, *refs):
    dq_ref, dk_ref, dv_ref = refs[-3:]
    seq, wide = q_ref.shape
    valid = valid_mask(seq, length_ref[0])
    for head in range(wide // DH):
        at = slice(head * DH, (head + 1) * DH)
        query, key, value = q_ref[:, at], k_ref[:, at], v_ref[:, at]
        probs = head_probs(query, key, valid)
        d_attn = (one_ref[:, at].astype(jnp.float32) + two_ref[:, at].astype(jnp.float32)).astype(jnp.bfloat16)
        dv_ref[:, at] = lax.dot_general(
            probs.astype(jnp.bfloat16), d_attn, (((0,), (0,)), ((), ())), preferred_element_type=jnp.float32
        ).astype(dv_ref.dtype)
        dprob = lax.dot_general(d_attn, value, (((1,), (1,)), ((), ())), preferred_element_type=jnp.float32)
        delta = jnp.sum(dprob * probs, axis=-1, keepdims=True)
        ds = (probs * (dprob - delta) * (DH**-0.5)).astype(jnp.bfloat16)
        dq_ref[:, at] = jnp.dot(ds, key, preferred_element_type=jnp.float32).astype(dq_ref.dtype)
        dk_ref[:, at] = lax.dot_general(
            ds, query, (((0,), (0,)), ((), ())), preferred_element_type=jnp.float32
        ).astype(dk_ref.dtype)


def partial_kernel(at_ref, *refs):
    count = (len(refs) - 1) // 2
    total = 0.0
    for attn_ref, weight_ref in zip(refs[:count], refs[count:-1]):
        total = total + jnp.dot(attn_ref[...], weight_ref[...], preferred_element_type=jnp.float32)
    refs[-1][...] = total


def hidden_kernel(pieces, before, at_ref, attn_ref, gain_ref, *refs):
    rest = refs[:pieces]
    weights = refs[pieces + before : -3]
    hidden_ref, sent_ref, square_ref = refs[-3:]
    weight = weights[0][...]
    for other in weights[1:]:
        weight = weight + other[...]
    n = rest[0].shape[0]
    for i in range(pieces):
        at = slice(i * n, (i + 1) * n)
        hidden = rest[i][...].astype(jnp.float32) + jnp.dot(attn_ref[at], weight, preferred_element_type=jnp.float32)
        if before:
            hidden = hidden + refs[pieces][at]
        hidden_ref[at] = hidden
        sent_ref[at] = (hidden * gain_ref[...]).astype(sent_ref.dtype)
        square_ref[i] = to_lanes(jnp.sum(hidden * hidden, axis=-1, keepdims=True))


def to_lanes(column):
    return jnp.transpose(jnp.broadcast_to(column, (column.shape[0], LANES)))[:1]


def to_column(row):
    return jnp.transpose(jnp.broadcast_to(row, (LANES, row.shape[1])))[:, :1]


def matched(hidden, sent, gain, inv, inv_other, weight):
    normed = hidden * inv
    diff = normed * gain - sent.astype(jnp.float32) * inv_other
    return normed, diff, weight * diff * gain


def match_kernel(hidden_ref, sent_ref, gain_ref, inv_ref, other_ref, weight_ref, out_ref):
    n = inv_ref.shape[-1]
    for i in range(inv_ref.shape[0]):
        at = slice(i * n, (i + 1) * n)
        inv, other, weight = to_column(inv_ref[i]), to_column(other_ref[i]), to_column(weight_ref[i])
        normed, diff, scaled = matched(hidden_ref[at], sent_ref[at], gain_ref[...], inv, other, weight)
        out_ref[i, :1] = to_lanes(jnp.sum(diff * diff, axis=-1, keepdims=True))
        out_ref[i, 1:] = to_lanes(jnp.sum(normed * scaled, axis=-1, keepdims=True))


def d_hidden_kernel(halves, at_ref, attn_ref, gain_ref, inv_ref, other_ref, weight_ref, mean_ref, *refs):
    n = inv_ref.shape[-1]
    deep = inv_ref.shape[0] // halves
    total = 0.0
    for i in range(inv_ref.shape[0]):
        half, at = i // deep, slice(i % deep * n, (i % deep + 1) * n)
        inv, other, weight = to_column(inv_ref[i]), to_column(other_ref[i]), to_column(weight_ref[i])
        hidden, sent = refs[half][at], refs[halves + half][at]
        normed, _, scaled = matched(hidden, sent, gain_ref[...], inv, other, weight)
        d_hidden = (inv * (scaled - normed * to_column(mean_ref[i]))).astype(jnp.bfloat16)
        refs[2 * halves + half][at] = d_hidden
        total = total + lax.dot_general(
            attn_ref[i * n : (i + 1) * n], d_hidden, (((0,), (0,)), ((), ())), preferred_element_type=jnp.float32
        )
    refs[-1][...] = total.astype(refs[-1].dtype)


def terms_kernel(at_ref, attn_ref, *refs):
    total, at = 0.0, 0
    for d_ref in refs[:-1]:
        n = d_ref.shape[0]
        total = total + lax.dot_general(
            attn_ref[at : at + n], d_ref[...], (((0,), (0,)), ((), ())), preferred_element_type=jnp.float32
        )
        at += n
    refs[-1][...] = total.astype(refs[-1].dtype)


def d_attn_kernel(d_ref, weight_ref, out_ref):
    out_ref[...] = lax.dot_general(
        d_ref[...], weight_ref[...], (((1,), (1,)), ((), ())), preferred_element_type=jnp.float32
    ).astype(out_ref.dtype)


def assemble_kernel(wide, places, member_ref, *refs):
    for ref, other in zip(refs[:-1], places):
        at = pl.multiple_of((member_ref[0] ^ other) * wide, LANES)
        refs[-1][:, pl.ds(at, wide)] = ref[...].astype(refs[-1].dtype)


ANY = pl.BlockSpec(memory_space=pl.ANY)


def small_call(kernel, indices, ins, outs, into=None, micros=1.0, grid=1):
    out = pl.pallas_call(
        kernel,
        grid_spec=pltpu.PrefetchScalarGridSpec(
            num_scalar_prefetch=1,
            grid=(grid,),
            in_specs=[pl.BlockSpec(b, m) for _, b, m in ins] + [ANY] * (into is not None),
            out_specs=[pl.BlockSpec(b, m) for _, _, b, m in outs],
        ),
        out_shape=[jax.ShapeDtypeStruct(shape, d) for shape, d, _, _ in outs],
        input_output_aliases={} if into is None else {1 + len(ins): 0},
        cost_estimate=cost(micros),
        compiler_params=vmem([(b, a.dtype) for a, b, _ in ins] + [(b, d) for _, d, b, _ in outs]),
    )(jnp.stack([jnp.int32(i) for i in indices]), *[a for a, _, _ in ins], *(() if into is None else (into,)))
    return out


ORIGIN = lambda i, at: (0, 0)
DOWN = lambda i, at: (at[0], 0)


def split_kernel(at_ref, in_ref, *outs):
    for i, out in enumerate(outs):
        out[...] = in_ref[:, pl.ds(pl.multiple_of(at_ref[i], LANES), out.shape[1])]


def cut_columns(array, places, widths):
    if any(w % LANES for w in widths):
        return [lax.dynamic_slice(array, (0, p), (array.shape[0], w)) for p, w in zip(places, widths)]
    n = array.shape[0]
    outs = [((n, w), array.dtype, (n, w), ORIGIN) for w in widths]
    return small_call(split_kernel, places, [(array, array.shape, ORIGIN)], outs)


def copy_kernel(at_ref, in_ref, *refs):
    refs[-1][...] = in_ref[...]


def place_rows(whole, piece, index):
    new = isinstance(whole, tuple)
    shape = whole if new else whole.shape
    outs = [(shape, piece.dtype, piece.shape, DOWN)]
    return small_call(copy_kernel, [index], [(piece, piece.shape, ORIGIN)], outs, None if new else whole)[0]


def take_rows(array, index, rows):
    block = (rows, array.shape[1])
    return small_call(copy_kernel, [index], [(array, block, DOWN)], [(block, array.dtype, block, ORIGIN)])[0]


def stack_kernel(across, at_ref, *refs):
    n = refs[0].shape[0]
    column = 0
    for i, ref in enumerate(refs[:-1]):
        row, wide = i // across * n, ref.shape[1]
        refs[-1][row : row + n, column : column + wide] = ref[...]
        column = (column + wide) % refs[-1].shape[1]


def stack_blocks(columns):
    n = columns[0][0].shape[0]
    shape = (n * len(columns[0]), sum(c[0].shape[1] for c in columns))
    pieces = [p for row in zip(*columns) for p in row]
    ins = [(p, p.shape, ORIGIN) for p in pieces]
    kernel = functools.partial(stack_kernel, len(columns))
    return small_call(kernel, [0], ins, [(shape, pieces[0].dtype, shape, ORIGIN)])[0]


def whole_kernel(at_ref, *refs):
    n = refs[0].shape[0]
    count = at_ref.shape[0]
    for i in range(count):
        block = refs[i][...]
        if i == count - 1 and len(refs) - 1 > count:
            block = block + refs[count][...]
        refs[-1][pl.ds(pl.multiple_of(at_ref[i] * n, 16), n)] = block


def stack_rows(pieces):
    return stack_blocks([pieces])


def add_kernel(at_ref, *refs):
    total = sum(ref[...].astype(jnp.float32) for ref in refs[:-1])
    refs[-1][...] = total.astype(refs[-1].dtype)


def sum_terms(got, terms, index):
    block = got[0].shape
    ins = [(g, block, ORIGIN) for g in got] + [(terms, block, DOWN)]
    return small_call(add_kernel, [index], ins, [(block, terms.dtype, block, ORIGIN)])[0]


def add_term(got, terms, index):
    return sum_terms([got], terms, index)


def fold_kernel(near_ref, far_ref, kept_ref, sent_ref):
    half = kept_ref.shape[0]
    total = near_ref[...].astype(jnp.float32) + far_ref[...].astype(jnp.float32)
    total = total.astype(kept_ref.dtype)
    kept_ref[...] = total[:half]
    sent_ref[...] = total[half:]


def fold(near, far, first, last, group):
    rows = near.shape[0]
    n = (last - first) * group
    there = pl.BlockSpec((rows, group), lambda i: (0, i + first))
    here = pl.BlockSpec((rows // 2, group), lambda i: (0, i))
    return pl.pallas_call(
        fold_kernel,
        grid=(last - first,),
        in_specs=[there] * 2,
        out_specs=[here] * 2,
        out_shape=[jax.ShapeDtypeStruct((rows // 2, n), near.dtype)] * 2,
        cost_estimate=cost(1.0),
        compiler_params=vmem([((rows, group), near.dtype)] * 3),
    )(near, far)


def call(micros, kernel, grid, ins, outs):
    return pl.pallas_call(
        kernel,
        grid=grid,
        in_specs=[pl.BlockSpec(b, m) for _, b, m in ins],
        out_specs=[pl.BlockSpec(b, m) for _, _, b, m in outs],
        out_shape=[jax.ShapeDtypeStruct(s, d) for s, d, _, _ in outs],
        cost_estimate=cost(micros),
        compiler_params=vmem([(b, a.dtype) for a, b, _ in ins] + [(b, d) for _, d, b, _ in outs]),
    )(*[a for a, _, _ in ins])


def attention_call(micros, kernel, length, arrays, moved, outs, first, number, group, into=None):
    seq = arrays[0].shape[0]
    there = pl.BlockSpec((seq, group), lambda i, *_: (0, i + first))
    here = pl.BlockSpec((seq, group), lambda i, *_: (0, i))
    alone = into is None
    into = into or ()
    shape = jax.ShapeDtypeStruct((seq, group * number) if alone else arrays[0].shape, jnp.bfloat16)
    given = 1 + len(arrays) + len(moved)
    return pl.pallas_call(
        kernel,
        grid_spec=pltpu.PrefetchScalarGridSpec(
            num_scalar_prefetch=1,
            grid=(number,),
            in_specs=[there] * len(arrays) + [here] * len(moved) + [pl.BlockSpec(memory_space=pl.ANY)] * len(into),
            out_specs=[here if alone else there] * outs,
        ),
        out_shape=[shape] * outs,
        input_output_aliases={given + i: i for i in range(len(into))},
        cost_estimate=cost(micros),
        compiler_params=vmem([((seq, group), jnp.bfloat16)] * (given - 1 + outs)),
    )(length.reshape(1), *arrays, *moved, *into)


def group_width(heads_width):
    heads = heads_width // DH
    return DH * max(g for g in (4, 2, 1) if heads % g == 0)


def tie(*values):
    return lax.optimization_barrier(values)


def split(values, *counts):
    lists, at = [], 0
    for count in counts:
        lists.append(list(values[at : at + count]))
        at += count
    return *lists, list(values[at:])


def send(value, axis, pairs):
    return lax.ppermute(value, axis, pairs)


LINE = 4
ENDS_OUT = [(2, 3), (1, 0)]
ENDS_IN = [(0, 1), (3, 2)]
MIDDLE = [(1, 2), (2, 1)]


def body(queries, keys, values, residual, event_ids, lengths, type_weight, w_out, gain):
    seq, heads_width = queries.shape[2:]
    width = residual.shape[3]
    parts = lax.axis_size("fsdp")
    team = lax.axis_size("dp")
    bits = bits_of(team)
    rows = team * seq
    shard_rows = w_out.shape[1]
    part = lax.axis_index("fsdp")
    member = lax.axis_index("dp")
    own = lax.axis_index(("dp", "fsdp"))
    length = lengths[own]
    count = jnp.sum(lengths).astype(jnp.float32)
    wide = width // team
    line = parts == LINE
    f32, bf16 = jnp.float32, jnp.bfloat16
    group = group_width(heads_width)
    steps = heads_width // group
    middle = -(-steps // 2)
    cuts = [(0, middle), (middle, steps)] if steps > 1 else [(0, steps)]
    q, k, v = queries[0, 0], keys[0, 0], values[0, 0]

    order = [0]
    for bit in reversed(bits):
        order = order + [s ^ bit for s in order]

    (block,) = cut_columns(w_out[0], [member * wide], [wide])
    mine = cut_columns(residual[0, 0], [(member ^ s) * wide for s in order], [wide] * team)
    block, *mine = tie(block, *mine)
    others = [1, 2] if line else list(range(1, parts))
    came = [swap(block, "fsdp", s) for s in others]

    types = jnp.arange(type_weight.shape[0], dtype=jnp.int32)
    matches = event_ids[0][:, None] == types[None, :]
    looked_up = jnp.sum(jnp.where(matches, type_weight[None, :], f32(0.0)), axis=-1)
    tok_w = jnp.where(jnp.arange(seq, dtype=jnp.int32) < length, looked_up, f32(0.0))
    tok_w = tok_w.reshape(1, 1, seq)
    for bit in reversed(bits):
        tok_w = jnp.concatenate([tok_w, swap(tok_w, "dp", bit)], axis=0)

    attn = []
    for first, last in cuts:
        attn += attention_call(1.5 * (last - first), forward_kernel, length, (q, k, v), (), 1, first, last - first, group)
    far = [swap(a, "dp", bits[-1]) for a in attn]
    tok_w, block, *rest = tie(tok_w, block, *came, *mine, *attn, *far)
    came, mine, attn, far = split(rest, len(others), team, len(cuts))

    last = [send(block, "fsdp", MIDDLE), send(came[1], "fsdp", ENDS_OUT)] if line else []
    rest = [swap(piece, "dp", s) if s else piece for s, piece in zip(order, mine)]
    found = [[a, b] for a, b in zip(attn, far)]
    for bit in reversed(bits[:-1]):
        found = [f + [swap(x, "dp", bit) for x in f] for f in found]
    attn = stack_blocks(found)

    row_at = lambda i: (i, 0)
    fixed = lambda i, *_: (0, 0)
    halves = 2
    tall = rows // halves
    deep = team // halves
    blocks, spots = [block, *came], [part, *[part ^ s for s in others]]
    before = []
    if line:
        picks = [(attn, (tall, shard_rows), lambda i, at, k=k: (i, at[k])) for k in range(len(blocks))]
        before = small_call(
            partial_kernel,
            spots,
            picks + [(b, b.shape, fixed) for b in blocks],
            [((rows, wide), f32, (tall, wide), lambda i, at: (i, 0))],
            micros=4.0,
            grid=halves,
        )
    attn, *tied = tie(attn, *before, *rest, *last)
    before, rest, last = split(tied, len(before), team)

    def whole_weight(blocks, last):
        ins = [(b, b.shape, fixed) for b in blocks + last]
        outs = [((heads_width, wide), bf16, (heads_width, wide), fixed)]
        return small_call(whole_kernel, spots + ([part ^ 3] if last else []), ins, outs, micros=2.0)[0]

    if not line:
        weight = whole_weight(blocks, last)

    def team_sum(value):
        shape = value.shape
        value = value.reshape((2,) * len(bits) + shape[1:])
        for axis, bit in enumerate(bits):
            value = value + jnp.flip(swap(value, "dp", bit), axis)
        return value.reshape(shape)

    my_gain = lax.dynamic_slice(gain[0], (member * wide,), (wide,))[None]
    gain_in = (my_gain, (1, wide), fixed)
    final = last if line else [weight]
    columns = shard_rows if line else heads_width

    def half_hidden(half):
        at = lambda i, at: (half, 0)
        return small_call(
            functools.partial(hidden_kernel, deep, len(before)),
            [part ^ 3 if line else 0],
            [(attn, (tall, columns), lambda i, at: (half, at[0])), gain_in]
            + [(r, (seq, wide), fixed) for r in rest[half * deep : (half + 1) * deep]]
            + [(b, (tall, wide), at) for b in before]
            + [(w, w.shape, fixed) for w in final],
            [
                ((tall, wide), f32, (tall, wide), fixed),
                ((tall, wide), bf16, (tall, wide), fixed),
                ((deep, 1, seq), f32, (deep, 1, seq), lambda i, at: (0, 0, 0)),
            ],
            micros=2.0,
        )

    hidden, sent, square = [list(x) for x in zip(*[half_hidden(half) for half in range(halves)])]
    first_sent = swap(sent[0], "copy", 1)
    inv = lax.rsqrt(team_sum(jnp.concatenate(square, axis=0)) / width + 1e-06)
    inv_other = swap(inv, "copy", 1)
    inv_late, sent_late = tie(inv, sent[1])
    second_sent = swap(sent_late, "copy", 1)
    row_scale = 2.0 * tok_w / (width * count)
    if line:
        *tied, _ = tie(*blocks, *last, sent_late)
        blocks, last = split(tied, len(blocks))
        weight = whole_weight(blocks, last)

    def match(half, sent):
        stat = (deep, 1, seq)
        stats = [(x, stat, lambda i: (half, 0, 0)) for x in (inv, inv_other, row_scale)]
        return call(
            2.0,
            match_kernel,
            (1,),
            [(hidden[half], (tall, wide), fixed), (sent, (tall, wide), fixed), gain_in] + stats,
            [((deep, 2, seq), f32, (deep, 2, seq), lambda i: (0, 0, 0))],
        )[0]

    both = [match(0, first_sent)]
    both[0], second_sent, weight = tie(both[0], second_sent, weight)
    both.append(match(1, second_sent))
    both = team_sum(jnp.concatenate(both, axis=0))
    loss = jnp.sum(tok_w[0] * both[0, :1]) / (width * count)
    mean = both[:, 1:] / width

    stats = [(x, (team, 1, seq), lambda i, at: (0, 0, 0)) for x in (inv, inv_other, row_scale, mean)]
    *d_hidden, terms = small_call(
        functools.partial(d_hidden_kernel, halves),
        [part ^ 3 if line else 0],
        [(attn, (rows, columns), lambda i, at: (0, at[0])), gain_in]
        + stats
        + [(x, (tall, wide), fixed) for x in (*hidden, first_sent, second_sent)],
        [((tall, wide), bf16, (tall, wide), fixed)] * halves + [((columns, wide), bf16, (columns, wide), fixed)],
        micros=4.0,
    )
    across = next(w for w in (512, 256, 128, heads_width) if heads_width % w == 0)
    terms, *d_hidden = tie(terms, *d_hidden)
    if line:
        got = [send(terms, "fsdp", MIDDLE), send(terms, "fsdp", ENDS_IN)]
    else:
        got = [swap(take_rows(terms, part ^ s, shard_rows), "fsdp", s) for s in range(1, parts)]

    def d_attn_rows(half):
        return call(
            3.0,
            d_attn_kernel,
            (heads_width // across,),
            [(d_hidden[half], (tall, wide), fixed), (weight, (across, wide), row_at)],
            [((tall, heads_width), bf16, (tall, across), lambda i: (0, i))],
        )[0]

    far = d_attn_rows(1)
    far, *d_hidden = tie(far, *d_hidden)
    far = swap(far, "dp", bits[0])
    if line:
        (terms,) = small_call(
            terms_kernel,
            [part ^ 1, part ^ 2, part],
            [(attn, (rows, shard_rows), lambda i, at: (0, at[i]))] + [(d, (tall, wide), fixed) for d in d_hidden],
            [((3 * shard_rows, wide), bf16, (shard_rows, wide), lambda i, at: (i, 0))],
            micros=4.0,
            grid=3,
        )
    near = d_attn_rows(0)
    for bit in bits[1:-1]:
        near, far = fold(near, far, 0, steps, group)
        far = swap(far, "dp", bit)
    kept, far = zip(*[fold(near, far, first, last, group) for first, last in cuts])
    kept, far = list(kept), list(far)
    tied = tie(terms, *got, *kept, *far)
    terms, got = tied[0], list(tied[1 : 1 + len(got)])
    kept, far = tied[1 + len(got) : 1 + len(got) + len(cuts)], tied[1 + len(got) + len(cuts) :]

    if line:
        near_by = swap(take_rows(terms, 0, shard_rows), "fsdp", 1)
        beyond = swap(add_term(got[1], terms, 1), "fsdp", 2)
        got = [got[0], near_by, beyond]
    far = [swap(f, "dp", bits[-1]) for f in far]
    grads = ()
    for (first, last), *back in zip(cuts, kept, far):
        grads = attention_call(
            1.5 * (last - first) + 1.0, backward_kernel, length, (q, k, v), back, 3, first, last - first, group, grads
        )
    *got, d_queries, d_keys, d_values = tie(*got, *grads)

    total = sum_terms(got, terms, 2 if line else part)
    pieces = {0: total}
    for bit in reversed(bits):
        pieces.update({s ^ bit: swap(p, "dp", bit) for s, p in pieces.items()})
    placed = [pieces[s] for s in order]
    if wide % LANES == 0:
        tall = next(t for t in (128, 64, 32, 16, shard_rows) if shard_rows % t == 0)
        out = pl.pallas_call(
            functools.partial(assemble_kernel, wide, order),
            grid_spec=pltpu.PrefetchScalarGridSpec(
                num_scalar_prefetch=1,
                grid=(shard_rows // tall,),
                in_specs=[pl.BlockSpec((tall, wide), lambda i, *_: (i, 0))] * team,
                out_specs=pl.BlockSpec((tall, width), lambda i, *_: (i, 0)),
            ),
            out_shape=jax.ShapeDtypeStruct((shard_rows, width), f32),
            cost_estimate=cost(1.0),
            compiler_params=vmem([((tall, wide), bf16)] * team + [((tall, width), f32)]),
        )(member.reshape(1), *placed)
    else:
        out = jnp.zeros((shard_rows, width), f32)
        for piece, s in zip(placed, order):
            out = lax.dynamic_update_slice(out, piece.astype(f32), (0, (member ^ s) * wide))
    return (
        loss.reshape(1, 1),
        d_queries[None, None],
        d_keys[None, None],
        d_values[None, None],
        out[None],
    )


def solution(mesh):
    whole = P("copy", ("dp", "fsdp"), None, None)
    in_specs = (
        whole,
        whole,
        whole,
        whole,
        P(("dp", "fsdp"), None),
        P(),
        P(),
        P("copy", "fsdp", None),
        P("copy", None),
    )
    out_specs = (P("copy", ("dp", "fsdp")), whole, whole, whole, P("copy", "fsdp", None))
    return jax.shard_map(body, mesh=mesh, in_specs=in_specs, out_specs=out_specs, check_vma=False)
```

```python
import functools
import math

import jax
import jax.numpy as jnp
from jax import lax
from jax.experimental import pallas as pl
from jax.experimental.pallas import tpu as pltpu
from jax.sharding import PartitionSpec as P

DH = 128
LANES = 128
NEG = -1e30
MIB = 1 << 20
VALUES = 6
SCALE = MIB


def cost(micros):
    return pl.CostEstimate(flops=0, bytes_accessed=int(micros * SCALE), transcendentals=0)


def vmem(blocks, times=2):
    size = sum(math.prod(shape) * jnp.dtype(kind).itemsize for shape, kind in blocks)
    return pltpu.CompilerParams(vmem_limit_bytes=min(times * size + VALUES * MIB, 60 * MIB))


def spec(block, index, shape):
    if block == shape:
        return pl.BlockSpec(block, index, pipeline_mode=pl.Buffered(1))
    return pl.BlockSpec(block, index)


def room(ins, outs):
    once = [(b, a.dtype) for a, b, _ in ins if b == a.shape]
    twice = [(b, a.dtype) for a, b, _ in ins if b != a.shape] + [(b, d) for _, d, b, _ in outs]
    size = sum(math.prod(shape) * jnp.dtype(kind).itemsize for shape, kind in once + twice + twice)
    return pltpu.CompilerParams(vmem_limit_bytes=min(size + VALUES * MIB, 60 * MIB))


def swap(value, axis, bit):
    return lax.ppermute(value, axis, [(i, i ^ bit) for i in range(lax.axis_size(axis))])


def bits_of(size):
    return [1 << j for j in range(size.bit_length() - 1)]


def head_probs(query, key, valid):
    scores = lax.dot_general(query, key, (((1,), (1,)), ((), ())), preferred_element_type=jnp.float32)
    scores = jnp.where(valid, scores * (DH**-0.5), NEG)
    top = jnp.max(scores, axis=-1, keepdims=True)
    exps = jnp.exp(scores - top)
    return exps * (1.0 / jnp.sum(exps, axis=-1, keepdims=True))


def valid_mask(seq, length):
    rows = lax.broadcasted_iota(jnp.int32, (seq, seq), 0)
    cols = lax.broadcasted_iota(jnp.int32, (seq, seq), 1)
    return (cols <= rows) & (cols < length)


def forward_kernel(length_ref, q_ref, k_ref, v_ref, out_ref):
    seq, wide = q_ref.shape
    valid = valid_mask(seq, length_ref[0])
    for head in range(wide // DH):
        at = slice(head * DH, (head + 1) * DH)
        probs = head_probs(q_ref[:, at], k_ref[:, at], valid).astype(jnp.bfloat16)
        out_ref[:, at] = jnp.dot(probs, v_ref[:, at], preferred_element_type=jnp.float32).astype(out_ref.dtype)


def backward_kernel(length_ref, q_ref, k_ref, v_ref, one_ref, two_ref, *refs):
    dq_ref, dk_ref, dv_ref = refs[-3:]
    seq, wide = q_ref.shape
    valid = valid_mask(seq, length_ref[0])
    for head in range(wide // DH):
        at = slice(head * DH, (head + 1) * DH)
        query, key, value = q_ref[:, at], k_ref[:, at], v_ref[:, at]
        probs = head_probs(query, key, valid)
        d_attn = (one_ref[:, at].astype(jnp.float32) + two_ref[:, at].astype(jnp.float32)).astype(jnp.bfloat16)
        dv_ref[:, at] = lax.dot_general(
            probs.astype(jnp.bfloat16), d_attn, (((0,), (0,)), ((), ())), preferred_element_type=jnp.float32
        ).astype(dv_ref.dtype)
        dprob = lax.dot_general(d_attn, value, (((1,), (1,)), ((), ())), preferred_element_type=jnp.float32)
        delta = jnp.sum(dprob * probs, axis=-1, keepdims=True)
        ds = (probs * (dprob - delta) * (DH**-0.5)).astype(jnp.bfloat16)
        dq_ref[:, at] = jnp.dot(ds, key, preferred_element_type=jnp.float32).astype(dq_ref.dtype)
        dk_ref[:, at] = lax.dot_general(
            ds, query, (((0,), (0,)), ((), ())), preferred_element_type=jnp.float32
        ).astype(dk_ref.dtype)


def hidden_kernel(team, low, gathered, *refs):
    if gathered:
        pairs, refs, attn_ref = refs[: team // 2], refs[team // 2 : -1], refs[-1]
    else:
        attn_ref, refs = refs[0], refs[1:]
    weight_ref, gain_ref, *rest = refs[: 2 + team]
    hidden_ref, sent_ref, square_ref = refs[2 + team :]
    n = rest[0].shape[0]

    def gather(i):
        attn_ref[...] = pairs[i][...]

    def finish(i):
        for j in range(2):
            at = slice(j * n, (j + 1) * n)
            hidden = rest[2 * i + j][:, low : low + pair.shape[1]].astype(jnp.float32) + pair[at]
            hidden_ref[at] = hidden
            sent_ref[at] = (hidden * gain_ref[...]).astype(sent_ref.dtype)
            square_ref[j] = to_lanes(jnp.sum(hidden * hidden, axis=-1, keepdims=True))

    for i in range(team // 2 if gathered else 0):
        pl.when(pl.program_id(0) == i)(functools.partial(gather, i))
    pair = jnp.dot(attn_ref[...], weight_ref[...], preferred_element_type=jnp.float32)
    for i in range(team // 2):
        pl.when(pl.program_id(0) == i)(functools.partial(finish, i))


def to_lanes(column):
    return jnp.transpose(jnp.broadcast_to(column, (column.shape[0], LANES)))[:1]


def to_column(row):
    return jnp.transpose(jnp.broadcast_to(row, (LANES, row.shape[1])))[:, :1]


def matched(hidden, sent, gain, inv, inv_other, weight):
    normed = hidden * inv
    diff = normed * gain - sent.astype(jnp.float32) * inv_other
    return normed, diff, weight * diff * gain


def match_kernel(hidden_ref, sent_ref, gain_ref, inv_ref, other_ref, weight_ref, *refs):
    n = inv_ref.shape[-1]
    for i in range(inv_ref.shape[0]):
        at = slice(i * n, (i + 1) * n)
        inv, other, weight = to_column(inv_ref[i]), to_column(other_ref[i]), to_column(weight_ref[i])
        normed, diff, scaled = matched(hidden_ref[at], sent_ref[at], gain_ref[...], inv, other, weight)
        square = to_lanes(jnp.sum(diff * diff, axis=-1, keepdims=True))
        cross = to_lanes(jnp.sum(normed * scaled, axis=-1, keepdims=True))
        if len(refs) > 1:
            square, cross = square + refs[0][i, :1], cross + refs[0][i, 1:]
        refs[-1][i, :1] = square
        refs[-1][i, 1:] = cross


def d_hidden_kernel(lows, at_ref, attn_ref, inv_ref, other_ref, weight_ref, mean_ref, *refs):
    d_ref, terms_ref, total_ref = refs[-3:]
    n, count = inv_ref.shape[-1], len(lows)
    for i in range(inv_ref.shape[0]):
        at = slice(i * n, (i + 1) * n)
        inv, other, weight = to_column(inv_ref[i]), to_column(other_ref[i]), to_column(weight_ref[i])
        mean = to_column(mean_ref[i])
        for low, hidden_ref, sent_ref, gain_ref in zip(lows, refs, refs[count:], refs[2 * count :]):
            normed, _, scaled = matched(hidden_ref[at], sent_ref[at], gain_ref[...], inv, other, weight)
            d_hidden = (inv * (scaled - normed * mean)).astype(d_ref.dtype)
            d_ref[at, low : low + d_hidden.shape[1]] = d_hidden
    terms = lax.dot_general(attn_ref[...], d_ref[...], (((0,), (0,)), ((), ())), preferred_element_type=jnp.float32)
    step, last = pl.program_id(0), pl.num_programs(0) - 1

    @pl.when(step == 0)
    def _():
        total_ref[...] = terms

    @pl.when((step > 0) & (step < last))
    def _():
        total_ref[...] += terms

    @pl.when(step == last)
    def _():
        terms_ref[...] = (total_ref[...] + terms).astype(terms_ref.dtype)


def terms_kernel(lows, at_ref, attn_ref, d_ref, *outs):
    terms = lax.dot_general(
        attn_ref[...], d_ref[...], (((0,), (0,)), ((), ())), preferred_element_type=jnp.float32
    ).astype(jnp.bfloat16)
    for low, out in zip(lows, outs):
        out[...] = terms[:, low : low + out.shape[1]]


def d_attn_kernel(lows, d_ref, *refs):
    outs = refs[len(lows) :]
    total = 0.0
    for low, weight_ref in zip(lows, refs):
        total = total + lax.dot_general(
            d_ref[:, low : low + weight_ref.shape[1]],
            weight_ref[...],
            (((1,), (1,)), ((), ())),
            preferred_element_type=jnp.float32,
        )
    total = total.astype(outs[0].dtype)
    n = outs[0].shape[1]
    for i, out in enumerate(outs):
        out[...] = total[:, i * n : (i + 1) * n]


def assemble_kernel(wide, places, member_ref, *refs):
    for ref, (other, low) in zip(refs[:-1], places):
        at = pl.multiple_of((member_ref[0] ^ other) * wide + low, LANES)
        refs[-1][:, pl.ds(at, ref.shape[1])] = ref[...].astype(refs[-1].dtype)


ANY = pl.BlockSpec(memory_space=pl.ANY)


def small_call(kernel, indices, ins, outs, into=None, micros=1.0, grid=1, scratch=()):
    out = pl.pallas_call(
        kernel,
        grid_spec=pltpu.PrefetchScalarGridSpec(
            num_scalar_prefetch=1,
            grid=(grid,),
            in_specs=[spec(b, m, a.shape) for a, b, m in ins] + [ANY] * (into is not None),
            out_specs=[pl.BlockSpec(b, m) for _, _, b, m in outs],
            scratch_shapes=list(scratch),
        ),
        out_shape=[jax.ShapeDtypeStruct(shape, d) for shape, d, _, _ in outs],
        input_output_aliases={} if into is None else {1 + len(ins): 0},
        cost_estimate=cost(micros),
        compiler_params=room(ins, outs),
    )(jnp.stack([jnp.int32(i) for i in indices]), *[a for a, _, _ in ins], *(() if into is None else (into,)))
    return out


ORIGIN = lambda i, at: (0, 0)
DOWN = lambda i, at: (at[0], 0)


def split_kernel(count, at_ref, in_ref, *outs):
    for i in range(0, len(outs), count):
        at = at_ref[i // count]
        for out in outs[i : i + count]:
            n = out.shape[1]
            out[...] = in_ref[:, pl.ds(at if isinstance(at, int) else pl.multiple_of(at, LANES), n)]
            at = at + n


def cut_columns(array, places, widths):
    n = array.shape[0]
    if any(w % LANES for w in widths):
        return [lax.dynamic_slice(array, (0, p), (n, w)) for p in places for w in widths]
    outs = [((n, w), array.dtype, (n, w), ORIGIN) for _ in places for w in widths]
    return small_call(
        functools.partial(split_kernel, len(widths)), places, [(array, array.shape, ORIGIN)], outs
    )


def copy_kernel(at_ref, in_ref, *refs):
    refs[-1][...] = in_ref[...]


def place_rows(whole, piece, index):
    new = isinstance(whole, tuple)
    shape = whole if new else whole.shape
    outs = [(shape, piece.dtype, piece.shape, DOWN)]
    return small_call(copy_kernel, [index], [(piece, piece.shape, ORIGIN)], outs, None if new else whole)[0]


def take_rows(array, index, rows):
    block = (rows, array.shape[1])
    return small_call(copy_kernel, [index], [(array, block, DOWN)], [(block, array.dtype, block, ORIGIN)])[0]


def stack_kernel(across, at_ref, *refs):
    n, column = refs[0].shape[0], 0
    for i, ref in enumerate(refs[:-1]):
        row = i // across * n
        refs[-1][row : row + n, column : column + ref.shape[1]] = ref[...]
        column = (column + ref.shape[1]) % refs[-1].shape[1]


def stack_blocks(rows):
    n = rows[0][0].shape[0]
    shape = (n * len(rows), sum(x.shape[1] for x in rows[0]))
    pieces = [x for row in rows for x in row]
    ins = [(x, x.shape, ORIGIN) for x in pieces]
    kernel = functools.partial(stack_kernel, len(rows[0]))
    return small_call(kernel, [0], ins, [(shape, pieces[0].dtype, shape, ORIGIN)])[0]


def whole_kernel(low, count, at_ref, *refs):
    out = refs[-1]
    n, wide = refs[0].shape[0], out.shape[1]
    for i in range(count):
        block = refs[i][:, low : low + wide]
        if i == count - 1 and len(refs) - 1 > count:
            block = block + refs[count][:, low : low + wide]
        out[pl.ds(pl.multiple_of(at_ref[i] * n, 16), n)] = block


def add_kernel(low, at_ref, *refs):
    out_ref = refs[-1]
    total = 0.0
    for ref in refs[:-1]:
        n = out_ref.shape[1]
        part = ref[...] if ref.shape[1] == n else ref[:, low : low + n]
        total = total + part.astype(jnp.float32)
    out_ref[...] = total.astype(out_ref.dtype)


def sum_terms(got, low, terms, index):
    block = (got[0].shape[0], terms.shape[1])
    ins = [(g, g.shape, ORIGIN) for g in got] + [(terms, block, DOWN)]
    kernel = functools.partial(add_kernel, low)
    return small_call(kernel, [index], ins, [(block, terms.dtype, block, ORIGIN)])[0]


def fold_kernel(pieces, *refs):
    kept_ref, sent_ref = refs[2 * pieces :]
    half = kept_ref.shape[0]
    at = 0
    for near_ref, far_ref in zip(refs[:pieces], refs[pieces : 2 * pieces]):
        n = far_ref.shape[1]
        total = near_ref[...].astype(jnp.float32) + far_ref[...].astype(jnp.float32)
        total = total.astype(kept_ref.dtype)
        kept_ref[:, at : at + n] = total[:half]
        sent_ref[:, at : at + n] = total[half:]
        at += n


def fold(near, far):
    n, wide = near[0].shape[0], sum(x.shape[1] for x in near)
    ins = [(x, x.shape, lambda i: (0, 0)) for x in (*near, *far)]
    outs = [((n // 2, wide), near[0].dtype, (n // 2, wide), lambda i: (0, 0))] * 2
    return call(1.0, functools.partial(fold_kernel, len(near)), (1,), ins, outs)


def call(micros, kernel, grid, ins, outs):
    return pl.pallas_call(
        kernel,
        grid=grid,
        in_specs=[spec(b, m, a.shape) for a, b, m in ins],
        out_specs=[pl.BlockSpec(b, m) for _, _, b, m in outs],
        out_shape=[jax.ShapeDtypeStruct(s, d) for s, d, _, _ in outs],
        cost_estimate=cost(micros),
        compiler_params=room(ins, outs),
    )(*[a for a, _, _ in ins])


def attention_call(micros, kernel, length, arrays, moved, outs, first, number, group, into=None):
    seq = arrays[0].shape[0]
    there = pl.BlockSpec((seq, group), lambda i, *_: (0, i + first))
    here = pl.BlockSpec((seq, group), lambda i, *_: (0, i))
    alone = into is None
    into = into or ()
    shape = jax.ShapeDtypeStruct((seq, group * number) if alone else arrays[0].shape, jnp.bfloat16)
    given = 1 + len(arrays) + len(moved)
    return pl.pallas_call(
        kernel,
        grid_spec=pltpu.PrefetchScalarGridSpec(
            num_scalar_prefetch=1,
            grid=(number,),
            in_specs=[there] * len(arrays) + [here] * len(moved) + [pl.BlockSpec(memory_space=pl.ANY)] * len(into),
            out_specs=[here if alone else there] * outs,
        ),
        out_shape=[shape] * outs,
        input_output_aliases={given + i: i for i in range(len(into))},
        cost_estimate=cost(micros),
        compiler_params=vmem([((seq, group), jnp.bfloat16)] * (given - 1 + outs)),
    )(length.reshape(1), *arrays, *moved, *into)


def group_width(heads_width):
    heads = heads_width // DH
    return DH * max(g for g in (4, 2, 1) if heads % g == 0)


def tie(*values):
    return lax.optimization_barrier(values)


def split(values, *counts):
    lists, at = [], 0
    for count in counts:
        lists.append(list(values[at : at + count]))
        at += count
    return *lists, list(values[at:])


def send(value, axis, pairs):
    return lax.ppermute(value, axis, pairs)


LINE = 4
ENDS_OUT = [(2, 3), (1, 0)]
ENDS_IN = [(0, 1), (3, 2)]
MIDDLE = [(1, 2), (2, 1)]


def body(queries, keys, values, residual, event_ids, lengths, type_weight, w_out, gain):
    seq, heads_width = queries.shape[2:]
    width = residual.shape[3]
    parts = lax.axis_size("fsdp")
    team = lax.axis_size("dp")
    bits = bits_of(team)
    rows = team * seq
    shard_rows = w_out.shape[1]
    part = lax.axis_index("fsdp")
    member = lax.axis_index("dp")
    own = lax.axis_index(("dp", "fsdp"))
    length = lengths[own]
    count = jnp.sum(lengths).astype(jnp.float32)
    wide = width // team
    line = parts == LINE and shard_rows % LANES == 0
    two = line and wide % LANES == 0 and wide > LANES
    cut = -(-wide * 3 // (5 * LANES)) * LANES
    chunks = [(0, cut), (cut, wide)] if two else [(0, wide)]
    f32, bf16 = jnp.float32, jnp.bfloat16
    group = group_width(heads_width)
    steps = heads_width // group
    ends = sorted({0, 2 * steps // 5, 4 * steps // 5, steps})
    cuts = list(zip(ends[:-1], ends[1:]))
    q, k, v = queries[0, 0], keys[0, 0], values[0, 0]

    row_at = lambda i: (i, 0)
    fixed = lambda i, *_: (0, 0)
    fixed3 = lambda i, *_: (0, 0, 0)
    stat_at = lambda i, *_: (i, 0, 0)
    lows = [low for low, _ in chunks]
    sizes = [high - low for low, high in chunks]

    order = [0]
    for bit in reversed(bits):
        order = order + [s ^ bit for s in order]

    column = (w_out[0], (shard_rows, wide), lambda i, at: (0, at[0]))
    if wide % LANES == 0:
        (block,) = small_call(copy_kernel, [member], [column], [((shard_rows, wide), bf16, (shard_rows, wide), ORIGIN)])
    else:
        (block,) = cut_columns(w_out[0], [member * wide], [wide])
    others = [1, 2] if line else list(range(1, parts))
    came = [swap(block, "fsdp", s) for s in others]

    attn = []
    middle = max(1, 2 * steps // 5)
    for first, final in [(0, middle), (middle, steps)] if steps > 1 else [(0, steps)]:
        attn += attention_call(
            1.5 * (final - first), forward_kernel, length, (q, k, v), (), 1, first, final - first, group
        )
    far = [swap(a, "dp", bits[-1]) for a in attn]
    home, _ = tie(residual[0, 0], attn[-1])
    mine = cut_columns(home, [(member ^ s) * wide for s in order], [wide])
    if team == 4:
        mine = [mine[0], mine[2], stack_blocks([[mine[1]], [mine[3]]])]
    tied = tie(*came, block, count, *attn, *far, *mine)
    came, (block, count), attn, far, mine = split(tied, len(others), 2, len(attn), len(attn))

    last = [send(block, "fsdp", MIDDLE), send(came[1], "fsdp", ENDS_OUT)] if line else []
    pairs = [stack_blocks([attn, far])]
    for bit in reversed(bits[:-1]):
        pairs = pairs + [swap(x, "dp", bit) for x in pairs]
    if team == 4:
        here, beside, across = mine
        across = swap(across, "dp", 2)
        rest = [across, swap(beside, "dp", 1), swap(take_rows(across, 1, seq), "dp", 1)]
        rest = [here, *rest]
    else:
        rest = [swap(piece, "dp", s) if s else piece for s, piece in zip(order, mine)]
    tied = tie(*last, *pairs, *rest)
    last, pairs, rest = split(tied, len(last), len(pairs))
    spots = [part, *[part ^ s for s in others], *([part ^ 3] if line else [])]
    shapes = [(heads_width, n) for n in sizes]

    def whole_weight(i):
        ins = [(b, b.shape, fixed) for b in [block, *came, *last]]
        kernel = functools.partial(whole_kernel, lows[i], len(spots))
        return small_call(kernel, spots, ins, [(shapes[i], bf16, shapes[i], fixed)], micros=2.0)[0]

    def team_sum(value):
        shape = value.shape
        value = value.reshape((2,) * len(bits) + shape[1:])
        for axis, bit in enumerate(bits):
            value = value + jnp.flip(swap(value, "dp", bit), axis)
        return value.reshape(shape)

    my_gain = lax.dynamic_slice(gain[0], (member * wide,), (wide,))[None]
    gains = [my_gain[:, low:high] for low, high in chunks]
    tall = rows // 2

    hidden, sent, square, partner, weights = [], [], [], [], []
    for i, n in enumerate(sizes):
        weights.append(whole_weight(i))
        ins = [(a, a.shape, fixed) for a in (weights[i], gains[i])] + [(a, (seq, wide), fixed) for a in rest]
        outs = [
            ((rows, n), f32, (2 * seq, n), row_at),
            ((rows, n), bf16, (2 * seq, n), row_at),
            ((team, 1, seq), f32, (2, 1, seq), stat_at),
        ]
        whole = ((rows, heads_width), bf16, (2 * seq, heads_width), row_at)
        if i:
            ins = [(attn, whole[2], row_at), *ins]
        else:
            ins = [(a, a.shape, fixed) for a in pairs] + ins
            outs.append(whole)
        kernel = functools.partial(hidden_kernel, team, lows[i], i == 0)
        h, x, sq, *new = call(2.0, kernel, (team // 2,), ins, outs)
        attn = new[0] if new else attn
        if i + 1 < len(chunks):
            partner.append(swap(x, "copy", 1))
        hidden.append(h)
        sent.append(x)
        square.append(sq)
    inv = lax.rsqrt(team_sum(sum(square)) / width + 1e-06)
    inv_other = swap(inv, "copy", 1)
    partner.append(swap(sent[-1], "copy", 1))

    types = jnp.arange(type_weight.shape[0], dtype=jnp.int32)
    ids, _ = tie(event_ids, x)
    matches = ids[0][:, None] == types[None, :]
    looked_up = jnp.sum(jnp.where(matches, type_weight[None, :], f32(0.0)), axis=-1)
    tok_w = jnp.where(jnp.arange(seq, dtype=jnp.int32) < length, looked_up, f32(0.0))
    tok_w = tok_w.reshape(1, 1, seq)
    for bit in reversed(bits):
        tok_w = jnp.concatenate([tok_w, swap(tok_w, "dp", bit)], axis=0)
    row_scale = 2.0 * tok_w / (width * count)
    stats = [inv, inv_other, row_scale]

    both = []
    for i in range(len(chunks)):
        n = sizes[i]
        (found,) = call(
            3.0,
            match_kernel,
            (team // 2,),
            [(hidden[i], (2 * seq, n), row_at), (partner[i], (2 * seq, n), row_at), (gains[i], (1, n), fixed)]
            + [(a, (2, *a.shape[1:]), stat_at) for a in (*stats, *both[-1:])],
            [((team, 2, seq), f32, (2, 2, seq), stat_at)],
        )
        if i + 1 < len(chunks):
            found, partner[i + 1] = tie(found, partner[i + 1])
        both.append(found)
    both = team_sum(both[-1])
    loss = jnp.sum(tok_w[0] * both[0, :1]) / (width * count)
    mean = both[:, 1:] / width

    columns = shard_rows if line else heads_width
    d_hidden, terms = small_call(
        functools.partial(d_hidden_kernel, lows),
        [part ^ 3 if line else 0],
        [(attn, (2 * seq, columns), lambda i, at: (i, at[0]))]
        + [(x, (2, 1, seq), stat_at) for x in (*stats, mean)]
        + [(x, (2 * seq, x.shape[1]), lambda i, at: (i, 0)) for x in (*hidden, *partner)]
        + [(x, x.shape, fixed) for x in gains],
        [((rows, wide), bf16, (2 * seq, wide), lambda i, at: (i, 0)), ((columns, wide), bf16, (columns, wide), fixed)],
        grid=team // 2,
        scratch=[pltpu.VMEM((columns, wide), f32)],
        micros=4.0,
    )
    if line:
        early = [send(terms, "fsdp", MIDDLE), send(terms, "fsdp", ENDS_IN)]
        terms = small_call(
            functools.partial(terms_kernel, lows),
            [part ^ 1, part ^ 2, part],
            [(attn, (rows, shard_rows), lambda i, at: (0, at[i])), (d_hidden, (rows, wide), fixed)],
            [((3 * shard_rows, n), bf16, (shard_rows, n), lambda i, at: (i, 0)) for n in sizes],
            micros=4.0,
            grid=3,
        )
    else:
        early = [swap(take_rows(terms, part ^ s, shard_rows), "fsdp", s) for s in range(1, parts)]
        terms = [terms]

    across, each = group, 1

    def d_attn_rows(half, d_hidden):
        return call(
            3.0,
            functools.partial(d_attn_kernel, lows),
            (1,),
            [(d_hidden, (tall, wide), lambda i: (half, 0))] + [(w, w.shape, fixed) for w in weights],
            [((tall, across), bf16, (tall, across), fixed)] * (heads_width // across),
        )

    far = [swap(x, "dp", bits[0]) for x in d_attn_rows(1, d_hidden)]
    near = d_attn_rows(0, d_hidden)
    for bit in bits[1:-1]:
        near, far = zip(*[fold([x], [y]) for x, y in zip(near, far)])
        far = [swap(x, "dp", bit) for x in far]
    folded = [fold(near[each * first : each * final], far[each * first : each * final]) for first, final in cuts]
    kept, passed = zip(*folded)
    tied = tie(*early, *terms, *kept, *passed)
    early, terms, kept, passed, _ = split(tied, len(early), len(chunks), len(cuts), len(cuts))

    def late_sends(i):
        if not line:
            return []
        beyond = sum_terms([early[1]], lows[i], terms[i], 1)
        return [swap(beyond, "fsdp", 2), swap(take_rows(terms[i], 0, shard_rows), "fsdp", 1)]

    def team_pieces(i, got):
        got = early[:1] + got if line else early
        total = sum_terms(got, lows[i], terms[i], 2 if line else part)
        pieces = {0: total}
        for bit in reversed(bits):
            pieces.update({s ^ bit: swap(p, "dp", bit) for s, p in pieces.items()})
        return [pieces[s] for s in order]

    def back(j, grads):
        first, last = cuts[j]
        arrays = (q, k, v), (kept[j], passed[j])
        micros = 1.5 * (last - first) + 1.0
        return attention_call(micros, backward_kernel, length, *arrays, 3, first, last - first, group, grads)

    got = late_sends(0)
    passed = [swap(x, "dp", bits[-1]) for x in passed]
    grads = back(0, ())
    early_parts = passed
    tied = tie(*got, *grads, *terms, *early, loss, *early_parts)
    got, grads, terms, early, (loss,), early_parts = split(tied, len(got), 3, len(chunks), len(early), 1)
    passed = [*early_parts, *passed[len(early_parts) :]]

    placed = []
    for i in range(1, len(chunks)):
        late = late_sends(i)
        placed += team_pieces(i - 1, got)
        if i == 1:
            for j in range(1, len(cuts)):
                grads = back(j, grads)
        tied = tie(*late, *grads)
        got, grads, _ = split(tied, len(late), 3)
    placed += team_pieces(len(chunks) - 1, got)
    if len(chunks) == 1:
        for j in range(1, len(cuts)):
            grads = back(j, grads)
    d_queries, d_keys, d_values = grads
    places = [(s, low) for low in lows for s in order]

    if wide % LANES == 0:
        tall = next(t for t in (128, 64, 32, 16, shard_rows) if shard_rows % t == 0)
        out = pl.pallas_call(
            functools.partial(assemble_kernel, wide, places),
            grid_spec=pltpu.PrefetchScalarGridSpec(
                num_scalar_prefetch=1,
                grid=(shard_rows // tall,),
                in_specs=[pl.BlockSpec((tall, p.shape[1]), lambda i, *_: (i, 0)) for p in placed],
                out_specs=pl.BlockSpec((tall, width), lambda i, *_: (i, 0)),
            ),
            out_shape=jax.ShapeDtypeStruct((shard_rows, width), f32),
            cost_estimate=cost(1.0),
            compiler_params=vmem([((tall, width), bf16), ((tall, width), f32)]),
        )(member.reshape(1), *placed)
    else:
        out = jnp.zeros((shard_rows, width), f32)
        for piece, (s, low) in zip(placed, places):
            out = lax.dynamic_update_slice(out, piece.astype(f32), (0, (member ^ s) * wide + low))
    return (
        loss.reshape(1, 1),
        d_queries[None, None],
        d_keys[None, None],
        d_values[None, None],
        out[None],
    )


def solution(mesh):
    whole = P("copy", ("dp", "fsdp"), None, None)
    in_specs = (
        whole,
        whole,
        whole,
        whole,
        P(("dp", "fsdp"), None),
        P(),
        P(),
        P("copy", "fsdp", None),
        P("copy", None),
    )
    out_specs = (P("copy", ("dp", "fsdp")), whole, whole, whole, P("copy", "fsdp", None))
    return jax.shard_map(body, mesh=mesh, in_specs=in_specs, out_specs=out_specs, check_vma=False)
```

```python
import functools
import math

import jax
import jax.numpy as jnp
from jax import lax
from jax.experimental import pallas as pl
from jax.experimental.pallas import tpu as pltpu
from jax.sharding import PartitionSpec as P

DH = 128
LANES = 128
NEG = -1e30
MIB = 1 << 20
VALUES = 6
SCALE = MIB


def cost(micros):
    return pl.CostEstimate(flops=0, bytes_accessed=int(micros * SCALE), transcendentals=0)


def vmem(blocks, times=2):
    size = sum(math.prod(shape) * jnp.dtype(kind).itemsize for shape, kind in blocks)
    return pltpu.CompilerParams(vmem_limit_bytes=min(times * size + VALUES * MIB, 60 * MIB))


def spec(block, index, shape):
    if block == shape:
        return pl.BlockSpec(block, index, pipeline_mode=pl.Buffered(1))
    return pl.BlockSpec(block, index)


def room(ins, outs):
    once = [(b, a.dtype) for a, b, _ in ins if b == a.shape]
    twice = [(b, a.dtype) for a, b, _ in ins if b != a.shape] + [(b, d) for _, d, b, _ in outs]
    size = sum(math.prod(shape) * jnp.dtype(kind).itemsize for shape, kind in once + twice + twice)
    return pltpu.CompilerParams(vmem_limit_bytes=min(size + VALUES * MIB, 60 * MIB))


def swap(value, axis, bit):
    return lax.ppermute(value, axis, [(i, i ^ bit) for i in range(lax.axis_size(axis))])


def bits_of(size):
    return [1 << j for j in range(size.bit_length() - 1)]


def head_probs(query, key, valid):
    scores = lax.dot_general(query, key, (((1,), (1,)), ((), ())), preferred_element_type=jnp.float32)
    scores = jnp.where(valid, scores * (DH**-0.5), NEG)
    top = jnp.max(scores, axis=-1, keepdims=True)
    exps = jnp.exp(scores - top)
    return exps * (1.0 / jnp.sum(exps, axis=-1, keepdims=True))


def valid_mask(seq, length):
    rows = lax.broadcasted_iota(jnp.int32, (seq, seq), 0)
    cols = lax.broadcasted_iota(jnp.int32, (seq, seq), 1)
    return (cols <= rows) & (cols < length)


def forward_kernel(length_ref, q_ref, k_ref, v_ref, out_ref):
    seq, wide = q_ref.shape
    valid = valid_mask(seq, length_ref[0])
    for head in range(wide // DH):
        at = slice(head * DH, (head + 1) * DH)
        probs = head_probs(q_ref[:, at], k_ref[:, at], valid).astype(jnp.bfloat16)
        out_ref[:, at] = jnp.dot(probs, v_ref[:, at], preferred_element_type=jnp.float32).astype(out_ref.dtype)


def backward_kernel(length_ref, q_ref, k_ref, v_ref, one_ref, two_ref, *refs):
    dq_ref, dk_ref, dv_ref = refs[-3:]
    seq, wide = q_ref.shape
    valid = valid_mask(seq, length_ref[0])
    for head in range(wide // DH):
        at = slice(head * DH, (head + 1) * DH)
        query, key, value = q_ref[:, at], k_ref[:, at], v_ref[:, at]
        probs = head_probs(query, key, valid)
        d_attn = (one_ref[:, at].astype(jnp.float32) + two_ref[:, at].astype(jnp.float32)).astype(jnp.bfloat16)
        dv_ref[:, at] = lax.dot_general(
            probs.astype(jnp.bfloat16), d_attn, (((0,), (0,)), ((), ())), preferred_element_type=jnp.float32
        ).astype(dv_ref.dtype)
        dprob = lax.dot_general(d_attn, value, (((1,), (1,)), ((), ())), preferred_element_type=jnp.float32)
        delta = jnp.sum(dprob * probs, axis=-1, keepdims=True)
        ds = (probs * (dprob - delta) * (DH**-0.5)).astype(jnp.bfloat16)
        dq_ref[:, at] = jnp.dot(ds, key, preferred_element_type=jnp.float32).astype(dq_ref.dtype)
        dk_ref[:, at] = lax.dot_general(
            ds, query, (((0,), (0,)), ((), ())), preferred_element_type=jnp.float32
        ).astype(dk_ref.dtype)


def hidden_kernel(team, low, gathered, *refs):
    if gathered:
        count = sum(gathered)
        pieces, refs, attn_ref = refs[:count], refs[count:-1], refs[-1]
    else:
        attn_ref, refs = refs[0], refs[1:]
    weight_ref, gain_ref, *rest = refs[: 2 + team]
    hidden_ref, sent_ref, square_ref = refs[2 + team :]
    n = rest[0].shape[0]

    def gather(i):
        row, column = 0, 0
        for piece in pieces[sum(gathered[:i]) : sum(gathered[: i + 1])]:
            attn_ref[row : row + n, column : column + piece.shape[1]] = piece[...]
            column += piece.shape[1]
            if column == attn_ref.shape[1]:
                row, column = row + n, 0

    def finish(i):
        for j in range(2):
            at = slice(j * n, (j + 1) * n)
            hidden = rest[2 * i + j][:, low : low + pair.shape[1]].astype(jnp.float32) + pair[at]
            hidden_ref[at] = hidden
            sent_ref[at] = (hidden * gain_ref[...]).astype(sent_ref.dtype)
            square_ref[j] = to_lanes(jnp.sum(hidden * hidden, axis=-1, keepdims=True))

    for i in range(team // 2 if gathered else 0):
        pl.when(pl.program_id(0) == i)(functools.partial(gather, i))
    pair = jnp.dot(attn_ref[...], weight_ref[...], preferred_element_type=jnp.float32)
    for i in range(team // 2):
        pl.when(pl.program_id(0) == i)(functools.partial(finish, i))


def to_lanes(column):
    return jnp.transpose(jnp.broadcast_to(column, (column.shape[0], LANES)))[:1]


def to_column(row):
    return jnp.transpose(jnp.broadcast_to(row, (LANES, row.shape[1])))[:, :1]


def matched(hidden, sent, gain, inv, inv_other, weight):
    normed = hidden * inv
    diff = normed * gain - sent.astype(jnp.float32) * inv_other
    return normed, diff, weight * diff * gain


def match_kernel(hidden_ref, sent_ref, gain_ref, inv_ref, other_ref, weight_ref, *refs):
    n = inv_ref.shape[-1]
    for i in range(inv_ref.shape[0]):
        at = slice(i * n, (i + 1) * n)
        inv, other, weight = to_column(inv_ref[i]), to_column(other_ref[i]), to_column(weight_ref[i])
        normed, diff, scaled = matched(hidden_ref[at], sent_ref[at], gain_ref[...], inv, other, weight)
        square = to_lanes(jnp.sum(diff * diff, axis=-1, keepdims=True))
        cross = to_lanes(jnp.sum(normed * scaled, axis=-1, keepdims=True))
        if len(refs) > 1:
            square, cross = square + refs[0][i, :1], cross + refs[0][i, 1:]
        refs[-1][i, :1] = square
        refs[-1][i, 1:] = cross


def d_hidden_kernel(lows, at_ref, attn_ref, inv_ref, other_ref, weight_ref, mean_ref, *refs):
    d_ref, terms_ref, total_ref = refs[-3:]
    n, count = inv_ref.shape[-1], len(lows)
    for i in range(inv_ref.shape[0]):
        at = slice(i * n, (i + 1) * n)
        inv, other, weight = to_column(inv_ref[i]), to_column(other_ref[i]), to_column(weight_ref[i])
        mean = to_column(mean_ref[i])
        for low, hidden_ref, sent_ref, gain_ref in zip(lows, refs, refs[count:], refs[2 * count :]):
            normed, _, scaled = matched(hidden_ref[at], sent_ref[at], gain_ref[...], inv, other, weight)
            d_hidden = (inv * (scaled - normed * mean)).astype(d_ref.dtype)
            d_ref[at, low : low + d_hidden.shape[1]] = d_hidden
    terms = lax.dot_general(attn_ref[...], d_ref[...], (((0,), (0,)), ((), ())), preferred_element_type=jnp.float32)
    step, last = pl.program_id(0), pl.num_programs(0) - 1

    @pl.when(step == 0)
    def _():
        total_ref[...] = terms

    @pl.when((step > 0) & (step < last))
    def _():
        total_ref[...] += terms

    @pl.when(step == last)
    def _():
        terms_ref[...] = (total_ref[...] + terms).astype(terms_ref.dtype)


def terms_kernel(lows, at_ref, attn_ref, d_ref, *outs):
    terms = lax.dot_general(
        attn_ref[...], d_ref[...], (((0,), (0,)), ((), ())), preferred_element_type=jnp.float32
    ).astype(jnp.bfloat16)
    for low, out in zip(lows, outs):
        out[...] = terms[:, low : low + out.shape[1]]


def d_attn_kernel(lows, d_ref, *refs):
    outs = refs[len(lows) :]
    total = 0.0
    for low, weight_ref in zip(lows, refs):
        total = total + lax.dot_general(
            d_ref[:, low : low + weight_ref.shape[1]],
            weight_ref[...],
            (((1,), (1,)), ((), ())),
            preferred_element_type=jnp.float32,
        )
    total = total.astype(outs[0].dtype)
    n = outs[0].shape[1]
    for i, out in enumerate(outs):
        out[...] = total[:, i * n : (i + 1) * n]


def assemble_kernel(wide, places, member_ref, *refs):
    for ref, (other, low) in zip(refs[:-1], places):
        at = pl.multiple_of((member_ref[0] ^ other) * wide + low, LANES)
        refs[-1][:, pl.ds(at, ref.shape[1])] = ref[...].astype(refs[-1].dtype)


ANY = pl.BlockSpec(memory_space=pl.ANY)


def small_call(kernel, indices, ins, outs, into=None, micros=1.0, grid=1, scratch=()):
    out = pl.pallas_call(
        kernel,
        grid_spec=pltpu.PrefetchScalarGridSpec(
            num_scalar_prefetch=1,
            grid=(grid,),
            in_specs=[spec(b, m, a.shape) for a, b, m in ins] + [ANY] * (into is not None),
            out_specs=[pl.BlockSpec(b, m) for _, _, b, m in outs],
            scratch_shapes=list(scratch),
        ),
        out_shape=[jax.ShapeDtypeStruct(shape, d) for shape, d, _, _ in outs],
        input_output_aliases={} if into is None else {1 + len(ins): 0},
        cost_estimate=cost(micros),
        compiler_params=room(ins, outs),
    )(jnp.stack([jnp.int32(i) for i in indices]), *[a for a, _, _ in ins], *(() if into is None else (into,)))
    return out


ORIGIN = lambda i, at: (0, 0)
DOWN = lambda i, at: (at[0], 0)


def split_kernel(count, at_ref, in_ref, *outs):
    for i in range(0, len(outs), count):
        at = at_ref[i // count]
        for out in outs[i : i + count]:
            n = out.shape[1]
            out[...] = in_ref[:, pl.ds(at if isinstance(at, int) else pl.multiple_of(at, LANES), n)]
            at = at + n


def cut_columns(array, places, widths):
    n = array.shape[0]
    if any(w % LANES for w in widths):
        return [lax.dynamic_slice(array, (0, p), (n, w)) for p in places for w in widths]
    outs = [((n, w), array.dtype, (n, w), ORIGIN) for _ in places for w in widths]
    return small_call(
        functools.partial(split_kernel, len(widths)), places, [(array, array.shape, ORIGIN)], outs
    )


def copy_kernel(at_ref, in_ref, *refs):
    refs[-1][...] = in_ref[...]


def place_rows(whole, piece, index):
    new = isinstance(whole, tuple)
    shape = whole if new else whole.shape
    outs = [(shape, piece.dtype, piece.shape, DOWN)]
    return small_call(copy_kernel, [index], [(piece, piece.shape, ORIGIN)], outs, None if new else whole)[0]


def take_rows(array, index, rows):
    block = (rows, array.shape[1])
    return small_call(copy_kernel, [index], [(array, block, DOWN)], [(block, array.dtype, block, ORIGIN)])[0]


def stack_kernel(across, at_ref, *refs):
    n, column = refs[0].shape[0], 0
    for i, ref in enumerate(refs[:-1]):
        row = i // across * n
        refs[-1][row : row + n, column : column + ref.shape[1]] = ref[...]
        column = (column + ref.shape[1]) % refs[-1].shape[1]


def stack_blocks(rows):
    n = rows[0][0].shape[0]
    shape = (n * len(rows), sum(x.shape[1] for x in rows[0]))
    pieces = [x for row in rows for x in row]
    ins = [(x, x.shape, ORIGIN) for x in pieces]
    kernel = functools.partial(stack_kernel, len(rows[0]))
    return small_call(kernel, [0], ins, [(shape, pieces[0].dtype, shape, ORIGIN)])[0]


def whole_kernel(low, count, at_ref, *refs):
    out = refs[-1]
    n, wide = refs[0].shape[0], out.shape[1]
    for i in range(count):
        block = refs[i][:, low : low + wide]
        if i == count - 1 and len(refs) - 1 > count:
            block = block + refs[count][:, low : low + wide]
        out[pl.ds(pl.multiple_of(at_ref[i] * n, 16), n)] = block


def add_kernel(low, at_ref, *refs):
    out_ref = refs[-1]
    total = 0.0
    for ref in refs[:-1]:
        n = out_ref.shape[1]
        part = ref[...] if ref.shape[1] == n else ref[:, low : low + n]
        total = total + part.astype(jnp.float32)
    out_ref[...] = total.astype(out_ref.dtype)


def sum_terms(got, low, terms, index):
    block = (got[0].shape[0], terms.shape[1])
    ins = [(g, g.shape, ORIGIN) for g in got] + [(terms, block, DOWN)]
    kernel = functools.partial(add_kernel, low)
    return small_call(kernel, [index], ins, [(block, terms.dtype, block, ORIGIN)])[0]


def fold_kernel(pieces, *refs):
    kept_ref, sent_ref = refs[2 * pieces :]
    half = kept_ref.shape[0]
    at = 0
    for near_ref, far_ref in zip(refs[:pieces], refs[pieces : 2 * pieces]):
        n = far_ref.shape[1]
        total = near_ref[...].astype(jnp.float32) + far_ref[...].astype(jnp.float32)
        total = total.astype(kept_ref.dtype)
        kept_ref[:, at : at + n] = total[:half]
        sent_ref[:, at : at + n] = total[half:]
        at += n


def fold(near, far):
    n, wide = near[0].shape[0], sum(x.shape[1] for x in near)
    ins = [(x, x.shape, lambda i: (0, 0)) for x in (*near, *far)]
    outs = [((n // 2, wide), near[0].dtype, (n // 2, wide), lambda i: (0, 0))] * 2
    return call(1.0, functools.partial(fold_kernel, len(near)), (1,), ins, outs)


def call(micros, kernel, grid, ins, outs):
    return pl.pallas_call(
        kernel,
        grid=grid,
        in_specs=[spec(b, m, a.shape) for a, b, m in ins],
        out_specs=[pl.BlockSpec(b, m) for _, _, b, m in outs],
        out_shape=[jax.ShapeDtypeStruct(s, d) for s, d, _, _ in outs],
        cost_estimate=cost(micros),
        compiler_params=room(ins, outs),
    )(*[a for a, _, _ in ins])


def attention_call(micros, kernel, length, arrays, moved, outs, first, number, group, into=None):
    seq = arrays[0].shape[0]
    there = pl.BlockSpec((seq, group), lambda i, *_: (0, i + first))
    here = pl.BlockSpec((seq, group), lambda i, *_: (0, i))
    alone = into is None
    into = into or ()
    shape = jax.ShapeDtypeStruct((seq, group * number) if alone else arrays[0].shape, jnp.bfloat16)
    given = 1 + len(arrays) + len(moved)
    return pl.pallas_call(
        kernel,
        grid_spec=pltpu.PrefetchScalarGridSpec(
            num_scalar_prefetch=1,
            grid=(number,),
            in_specs=[there] * len(arrays) + [here] * len(moved) + [pl.BlockSpec(memory_space=pl.ANY)] * len(into),
            out_specs=[here if alone else there] * outs,
        ),
        out_shape=[shape] * outs,
        input_output_aliases={given + i: i for i in range(len(into))},
        cost_estimate=cost(micros),
        compiler_params=vmem([((seq, group), jnp.bfloat16)] * (given - 1 + outs)),
    )(length.reshape(1), *arrays, *moved, *into)


def group_width(heads_width):
    heads = heads_width // DH
    return DH * max(g for g in (4, 2, 1) if heads % g == 0)


def tie(*values):
    return lax.optimization_barrier(values)


def split(values, *counts):
    lists, at = [], 0
    for count in counts:
        lists.append(list(values[at : at + count]))
        at += count
    return *lists, list(values[at:])


def send(value, axis, pairs):
    return lax.ppermute(value, axis, pairs)


LINE = 4
ENDS_OUT = [(2, 3), (1, 0)]
ENDS_IN = [(0, 1), (3, 2)]
MIDDLE = [(1, 2), (2, 1)]


def body(queries, keys, values, residual, event_ids, lengths, type_weight, w_out, gain):
    seq, heads_width = queries.shape[2:]
    width = residual.shape[3]
    parts = lax.axis_size("fsdp")
    team = lax.axis_size("dp")
    bits = bits_of(team)
    rows = team * seq
    shard_rows = w_out.shape[1]
    part = lax.axis_index("fsdp")
    member = lax.axis_index("dp")
    own = lax.axis_index(("dp", "fsdp"))
    length = lengths[own]
    count = jnp.sum(lengths).astype(jnp.float32)
    wide = width // team
    line = parts == LINE and shard_rows % LANES == 0
    two = line and wide % LANES == 0 and wide > LANES
    cut = -(-wide * 2 // (5 * LANES)) * LANES
    chunks = [(0, cut), (cut, wide)] if two else [(0, wide)]
    back_cut = -(-wide * 3 // (5 * LANES)) * LANES
    back_chunks = [(0, back_cut), (back_cut, wide)] if two else [(0, wide)]
    f32, bf16 = jnp.float32, jnp.bfloat16
    group = group_width(heads_width)
    steps = heads_width // group
    ends = sorted({0, 2 * steps // 5, 4 * steps // 5, steps})
    cuts = list(zip(ends[:-1], ends[1:]))
    q, k, v = queries[0, 0], keys[0, 0], values[0, 0]

    row_at = lambda i: (i, 0)
    fixed = lambda i, *_: (0, 0)
    fixed3 = lambda i, *_: (0, 0, 0)
    stat_at = lambda i, *_: (i, 0, 0)
    lows = [low for low, _ in chunks]
    sizes = [high - low for low, high in chunks]

    order = [0]
    for bit in reversed(bits):
        order = order + [s ^ bit for s in order]

    column = (w_out[0], (shard_rows, wide), lambda i, at: (0, at[0]))
    if wide % LANES == 0:
        (block,) = small_call(copy_kernel, [member], [column], [((shard_rows, wide), bf16, (shard_rows, wide), ORIGIN)])
    else:
        (block,) = cut_columns(w_out[0], [member * wide], [wide])
    others = [1, 2] if line else list(range(1, parts))
    came = [swap(block, "fsdp", s) for s in others]

    attn = []
    middle = max(1, 2 * steps // 5)
    for first, final in [(0, middle), (middle, steps)] if steps > 1 else [(0, steps)]:
        attn += attention_call(
            1.5 * (final - first), forward_kernel, length, (q, k, v), (), 1, first, final - first, group
        )
    far = [swap(a, "dp", bits[-1]) for a in attn]
    if team == 4:
        attn.append(stack_blocks([attn]))
    home, _ = tie(residual[0, 0], attn[-1])
    mine = cut_columns(home, [(member ^ s) * wide for s in order], [wide])
    if team == 4:
        mine = [mine[0], mine[2], stack_blocks([[mine[1]], [mine[3]]])]
    own_parts = attn
    tied = tie(*came, block, count, *own_parts, *far, *mine)
    came, (block, count), own_parts, far, mine = split(tied, len(others), 2, len(own_parts), len(far))

    last = [send(block, "fsdp", MIDDLE), send(came[1], "fsdp", ENDS_OUT)] if line else []
    pairs = [[*own_parts[: len(far)], *far]]
    if team == 4:
        pairs.append([swap(x, "dp", 1) for x in (own_parts[-1], *far)])
    else:
        for bit in reversed(bits[:-1]):
            pairs = pairs + [[swap(x, "dp", bit) for x in pair] for pair in pairs]
    each = [len(pair) for pair in pairs]
    pairs = [x for pair in pairs for x in pair]
    if team == 4:
        here, beside, across = mine
        across = swap(across, "dp", 2)
        passed_on = swap(stack_blocks([[beside], [take_rows(across, 1, seq)]]), "dp", 1)
        rest = [here, across, passed_on]
    else:
        rest = [swap(piece, "dp", s) if s else piece for s, piece in zip(order, mine)]
    tied = tie(*last, *pairs, *rest)
    last, pairs, rest = split(tied, len(last), len(pairs))
    spots = [part, *[part ^ s for s in others], *([part ^ 3] if line else [])]
    shapes = [(heads_width, n) for n in sizes]

    def whole_weight(i, first):
        ins = [(b, b.shape, fixed) for b in [first, *came, *last]]
        kernel = functools.partial(whole_kernel, lows[i], len(spots))
        return small_call(kernel, spots, ins, [(shapes[i], bf16, shapes[i], fixed)], micros=2.0)[0]

    def team_sum(value):
        shape = value.shape
        value = value.reshape((2,) * len(bits) + shape[1:])
        for axis, bit in enumerate(bits):
            value = value + jnp.flip(swap(value, "dp", bit), axis)
        return value.reshape(shape)

    my_gain = lax.dynamic_slice(gain[0], (member * wide,), (wide,))[None]
    gains = [my_gain[:, low:high] for low, high in chunks]
    tall = rows // 2

    lower = lambda i, *_: (1, 0)
    rest_blocks = [(a, fixed) for a in rest]
    if team == 4:
        rest_blocks = [(rest[0], fixed), (rest[1], fixed), (rest[2], fixed), (rest[2], lower)]
    hidden, sent, square, partner, weights = [], [], [], [], []
    for i, n in enumerate(sizes):
        first = block
        if i:
            first, square[0] = tie(block, square[0])
        weights.append(whole_weight(i, first))
        ins = [(a, a.shape, fixed) for a in (weights[i], gains[i])] + [(a, (seq, wide), m) for a, m in rest_blocks]
        outs = [
            ((rows, n), f32, (2 * seq, n), row_at),
            ((rows, n), bf16, (2 * seq, n), row_at),
            ((team, 1, seq), f32, (2, 1, seq), stat_at),
        ]
        whole = ((rows, heads_width), bf16, (2 * seq, heads_width), row_at)
        if i:
            ins = [(attn, whole[2], row_at), *ins]
        else:
            ins = [(a, a.shape, fixed) for a in pairs] + ins
            outs.append(whole)
        kernel = functools.partial(hidden_kernel, team, lows[i], [] if i else each)
        h, x, sq, *new = call(2.0, kernel, (team // 2,), ins, outs)
        attn = new[0] if new else attn
        if i + 1 < len(chunks):
            partner.append(swap(x, "copy", 1))
        hidden.append(h)
        sent.append(x)
        square.append(sq)
    inv = lax.rsqrt(team_sum(sum(square)) / width + 1e-06)
    inv_other = swap(inv, "copy", 1)
    partner.append(swap(sent[-1], "copy", 1))

    types = jnp.arange(type_weight.shape[0], dtype=jnp.int32)
    ids, _ = tie(event_ids, x)
    matches = ids[0][:, None] == types[None, :]
    looked_up = jnp.sum(jnp.where(matches, type_weight[None, :], f32(0.0)), axis=-1)
    tok_w = jnp.where(jnp.arange(seq, dtype=jnp.int32) < length, looked_up, f32(0.0))
    tok_w = tok_w.reshape(1, 1, seq)
    for bit in reversed(bits):
        tok_w = jnp.concatenate([tok_w, swap(tok_w, "dp", bit)], axis=0)
    row_scale = 2.0 * tok_w / (width * count)
    stats = [inv, inv_other, row_scale]

    both = []
    for i in range(len(chunks)):
        n = sizes[i]
        (found,) = call(
            3.0,
            match_kernel,
            (team // 2,),
            [(hidden[i], (2 * seq, n), row_at), (partner[i], (2 * seq, n), row_at), (gains[i], (1, n), fixed)]
            + [(a, (2, *a.shape[1:]), stat_at) for a in (*stats, *both[-1:])],
            [((team, 2, seq), f32, (2, 2, seq), stat_at)],
        )
        if i + 1 < len(chunks):
            found, partner[i + 1] = tie(found, partner[i + 1])
        both.append(found)
    both = team_sum(both[-1])
    loss = jnp.sum(tok_w[0] * both[0, :1]) / (width * count)
    mean = both[:, 1:] / width

    back_lows = [low for low, _ in back_chunks]
    back_sizes = [high - low for low, high in back_chunks]
    columns = shard_rows if line else heads_width
    d_hidden, terms = small_call(
        functools.partial(d_hidden_kernel, lows),
        [part ^ 3 if line else 0],
        [(attn, (2 * seq, columns), lambda i, at: (i, at[0]))]
        + [(x, (2, 1, seq), stat_at) for x in (*stats, mean)]
        + [(x, (2 * seq, x.shape[1]), lambda i, at: (i, 0)) for x in (*hidden, *partner)]
        + [(x, x.shape, fixed) for x in gains],
        [((rows, wide), bf16, (2 * seq, wide), lambda i, at: (i, 0)), ((columns, wide), bf16, (columns, wide), fixed)],
        grid=team // 2,
        scratch=[pltpu.VMEM((columns, wide), f32)],
        micros=4.0,
    )
    if line:
        early = [send(terms, "fsdp", MIDDLE), send(terms, "fsdp", ENDS_IN)]
        terms = small_call(
            functools.partial(terms_kernel, back_lows),
            [part ^ 1, part ^ 2, part],
            [(attn, (rows, shard_rows), lambda i, at: (0, at[i])), (d_hidden, (rows, wide), fixed)],
            [((3 * shard_rows, n), bf16, (shard_rows, n), lambda i, at: (i, 0)) for n in back_sizes],
            micros=4.0,
            grid=3,
        )
    else:
        early = [swap(take_rows(terms, part ^ s, shard_rows), "fsdp", s) for s in range(1, parts)]
        terms = [terms]

    across, each = group, 1

    def d_attn_rows(half, d_hidden, first, count):
        n = across * count
        return call(
            0.6 * count,
            functools.partial(d_attn_kernel, lows),
            (1,),
            [(d_hidden, (tall, wide), lambda i: (half, 0))]
            + [(w, (n, w.shape[1]), lambda i: (first // count, 0)) for w in weights],
            [((tall, across), bf16, (tall, across), fixed)] * count,
        )

    def d_attn_parts(half, d_hidden):
        total = heads_width // across
        parts = [(0, 2), (2, 2), (4, 1)] if total == 5 else [(0, total)]
        return [x for first, count in parts for x in d_attn_rows(half, d_hidden, first, count)]

    far = [swap(x, "dp", bits[0]) for x in d_attn_parts(1, d_hidden)]
    near = d_attn_parts(0, d_hidden)
    for bit in bits[1:-1]:
        near, far = zip(*[fold([x], [y]) for x, y in zip(near, far)])
        far = [swap(x, "dp", bit) for x in far]
    folded = [fold(near[each * first : each * final], far[each * first : each * final]) for first, final in cuts]
    kept, passed = zip(*folded)
    passed = [swap(passed[0], "dp", bits[-1]), *passed[1:]]
    tied = tie(*early, *terms, *kept, *passed)
    early, terms, kept, passed, _ = split(tied, len(early), len(back_chunks), len(cuts), len(cuts))

    def late_sends(i):
        if not line:
            return []
        beyond = sum_terms([early[1]], back_lows[i], terms[i], 1)
        return [swap(beyond, "fsdp", 2), swap(take_rows(terms[i], 0, shard_rows), "fsdp", 1)]

    def team_pieces(i, got):
        got = early[:1] + got if line else early
        total = sum_terms(got, back_lows[i], terms[i], 2 if line else part)
        pieces = {0: total}
        for bit in reversed(bits):
            pieces.update({s ^ bit: swap(p, "dp", bit) for s, p in pieces.items()})
        return [pieces[s] for s in order]

    def back(j, grads):
        first, last = cuts[j]
        arrays = (q, k, v), (kept[j], passed[j])
        micros = 1.5 * (last - first) + 1.0
        return attention_call(micros, backward_kernel, length, *arrays, 3, first, last - first, group, grads)

    got = late_sends(0)
    passed = [passed[0], *[swap(x, "dp", bits[-1]) for x in passed[1:]]]
    grads = back(0, ())
    early_parts = passed
    tied = tie(*got, *grads, *terms, *early, loss, *early_parts)
    got, grads, terms, early, (loss,), early_parts = split(tied, len(got), 3, len(back_chunks), len(early), 1)
    passed = [*early_parts, *passed[len(early_parts) :]]

    placed = []
    for i in range(1, len(back_chunks)):
        late = late_sends(i)
        placed += team_pieces(i - 1, got)
        if i == 1:
            for j in range(1, len(cuts)):
                grads = back(j, grads)
        tied = tie(*late, *grads)
        got, grads, _ = split(tied, len(late), 3)
    placed += team_pieces(len(back_chunks) - 1, got)
    if len(back_chunks) == 1:
        for j in range(1, len(cuts)):
            grads = back(j, grads)
    d_queries, d_keys, d_values = grads
    places = [(s, low) for low in back_lows for s in order]

    if wide % LANES == 0:
        tall = next(t for t in (128, 64, 32, 16, shard_rows) if shard_rows % t == 0)
        out = pl.pallas_call(
            functools.partial(assemble_kernel, wide, places),
            grid_spec=pltpu.PrefetchScalarGridSpec(
                num_scalar_prefetch=1,
                grid=(shard_rows // tall,),
                in_specs=[pl.BlockSpec((tall, p.shape[1]), lambda i, *_: (i, 0)) for p in placed],
                out_specs=pl.BlockSpec((tall, width), lambda i, *_: (i, 0)),
            ),
            out_shape=jax.ShapeDtypeStruct((shard_rows, width), f32),
            cost_estimate=cost(1.0),
            compiler_params=vmem([((tall, width), bf16), ((tall, width), f32)]),
        )(member.reshape(1), *placed)
    else:
        out = jnp.zeros((shard_rows, width), f32)
        for piece, (s, low) in zip(placed, places):
            out = lax.dynamic_update_slice(out, piece.astype(f32), (0, (member ^ s) * wide + low))
    return (
        loss.reshape(1, 1),
        d_queries[None, None],
        d_keys[None, None],
        d_values[None, None],
        out[None],
    )


def solution(mesh):
    whole = P("copy", ("dp", "fsdp"), None, None)
    in_specs = (
        whole,
        whole,
        whole,
        whole,
        P(("dp", "fsdp"), None),
        P(),
        P(),
        P("copy", "fsdp", None),
        P("copy", None),
    )
    out_specs = (P("copy", ("dp", "fsdp")), whole, whole, whole, P("copy", "fsdp", None))
    return jax.shard_map(body, mesh=mesh, in_specs=in_specs, out_specs=out_specs, check_vma=False)
```

```python
import functools
import math

import jax
import jax.numpy as jnp
from jax import lax
from jax.experimental import pallas as pl
from jax.experimental.pallas import tpu as pltpu
from jax.sharding import PartitionSpec as P

DH = 128
LANES = 128
NEG = -1e30
MIB = 1 << 20
VALUES = 6
SCALE = MIB


def cost(micros):
    return pl.CostEstimate(flops=0, bytes_accessed=int(micros * SCALE), transcendentals=0)


def vmem(blocks, times=2):
    size = sum(math.prod(shape) * jnp.dtype(kind).itemsize for shape, kind in blocks)
    return pltpu.CompilerParams(vmem_limit_bytes=min(times * size + VALUES * MIB, 60 * MIB))


def spec(block, index, shape):
    if block == shape:
        return pl.BlockSpec(block, index, pipeline_mode=pl.Buffered(1))
    return pl.BlockSpec(block, index)


def room(ins, outs):
    once = [(b, a.dtype) for a, b, _ in ins if b == a.shape]
    twice = [(b, a.dtype) for a, b, _ in ins if b != a.shape] + [(b, d) for _, d, b, _ in outs]
    size = sum(math.prod(shape) * jnp.dtype(kind).itemsize for shape, kind in once + twice + twice)
    return pltpu.CompilerParams(vmem_limit_bytes=min(size + VALUES * MIB, 60 * MIB))


def swap(value, axis, bit):
    return lax.ppermute(value, axis, [(i, i ^ bit) for i in range(lax.axis_size(axis))])


def bits_of(size):
    return [1 << j for j in range(size.bit_length() - 1)]


def head_probs(query, key, valid):
    scores = lax.dot_general(query, key, (((1,), (1,)), ((), ())), preferred_element_type=jnp.float32)
    scores = jnp.where(valid, scores * (DH**-0.5), NEG)
    top = jnp.max(scores, axis=-1, keepdims=True)
    exps = jnp.exp(scores - top)
    return exps * (1.0 / jnp.sum(exps, axis=-1, keepdims=True))


def valid_mask(seq, length):
    rows = lax.broadcasted_iota(jnp.int32, (seq, seq), 0)
    cols = lax.broadcasted_iota(jnp.int32, (seq, seq), 1)
    return (cols <= rows) & (cols < length)


def forward_kernel(length_ref, q_ref, k_ref, v_ref, out_ref):
    seq, wide = q_ref.shape
    valid = valid_mask(seq, length_ref[0])
    for head in range(wide // DH):
        at = slice(head * DH, (head + 1) * DH)
        probs = head_probs(q_ref[:, at], k_ref[:, at], valid).astype(jnp.bfloat16)
        out_ref[:, at] = jnp.dot(probs, v_ref[:, at], preferred_element_type=jnp.float32).astype(out_ref.dtype)


def backward_kernel(length_ref, q_ref, k_ref, v_ref, one_ref, two_ref, *refs):
    dq_ref, dk_ref, dv_ref = refs[-3:]
    seq, wide = q_ref.shape
    valid = valid_mask(seq, length_ref[0])
    for head in range(wide // DH):
        at = slice(head * DH, (head + 1) * DH)
        query, key, value = q_ref[:, at], k_ref[:, at], v_ref[:, at]
        probs = head_probs(query, key, valid)
        d_attn = (one_ref[:, at].astype(jnp.float32) + two_ref[:, at].astype(jnp.float32)).astype(jnp.bfloat16)
        dv_ref[:, at] = lax.dot_general(
            probs.astype(jnp.bfloat16), d_attn, (((0,), (0,)), ((), ())), preferred_element_type=jnp.float32
        ).astype(dv_ref.dtype)
        dprob = lax.dot_general(d_attn, value, (((1,), (1,)), ((), ())), preferred_element_type=jnp.float32)
        delta = jnp.sum(dprob * probs, axis=-1, keepdims=True)
        ds = (probs * (dprob - delta) * (DH**-0.5)).astype(jnp.bfloat16)
        dq_ref[:, at] = jnp.dot(ds, key, preferred_element_type=jnp.float32).astype(dq_ref.dtype)
        dk_ref[:, at] = lax.dot_general(
            ds, query, (((0,), (0,)), ((), ())), preferred_element_type=jnp.float32
        ).astype(dk_ref.dtype)


def whole_kernel(low, count, at_ref, *refs):
    out = refs[-1]
    n, wide = refs[0].shape[0], out.shape[1]
    for i in range(count):
        block = refs[i][:, low : low + wide]
        if i == count - 1 and len(refs) - 1 > count:
            block = block + refs[count][:, low : low + wide]
        out[pl.ds(pl.multiple_of(at_ref[i] * n, 16), n)] = block


def hidden_kernel(team, low, gathered, blocks, at_ref, *refs):
    if gathered:
        pieces, refs, attn_ref = refs[: sum(gathered)], refs[sum(gathered) : -1], refs[-1]
    else:
        attn_ref, refs = refs[0], refs[1:]
    weights, (gain_ref, *rest) = refs[:blocks], refs[blocks : blocks + 1 + team]
    hidden_ref, sent_ref, square_ref, weight_ref = refs[blocks + 1 + team :]
    n = rest[0].shape[0]

    def gather(i):
        row, column = 0, 0
        for piece in pieces[sum(gathered[:i]) : sum(gathered[: i + 1])]:
            attn_ref[row : row + n, column : column + piece.shape[1]] = piece[...]
            column += piece.shape[1]
            if column == attn_ref.shape[1]:
                row, column = row + n, 0

    def finish(i):
        for j in range(2):
            at = slice(j * n, (j + 1) * n)
            hidden = rest[2 * i + j][:, low : low + pair.shape[1]].astype(jnp.float32) + pair[at]
            hidden_ref[at] = hidden
            sent_ref[at] = (hidden * gain_ref[...]).astype(sent_ref.dtype)
            square_ref[j] = to_lanes(jnp.sum(hidden * hidden, axis=-1, keepdims=True))

    for i in range(team // 2 if gathered else 0):
        pl.when(pl.program_id(0) == i)(functools.partial(gather, i))
    pl.when(pl.program_id(0) == 0)(functools.partial(whole_kernel, low, at_ref.shape[0], at_ref, *weights, weight_ref))
    pair = jnp.dot(attn_ref[...], weight_ref[...], preferred_element_type=jnp.float32)
    for i in range(team // 2):
        pl.when(pl.program_id(0) == i)(functools.partial(finish, i))


def to_lanes(column):
    return jnp.transpose(jnp.broadcast_to(column, (column.shape[0], LANES)))[:1]


def to_column(row):
    return jnp.transpose(jnp.broadcast_to(row, (LANES, row.shape[1])))[:, :1]


def matched(hidden, sent, gain, inv, inv_other, weight):
    normed = hidden * inv
    diff = normed * gain - sent.astype(jnp.float32) * inv_other
    return normed, diff, weight * diff * gain


def match_kernel(hidden_ref, sent_ref, gain_ref, inv_ref, other_ref, weight_ref, *refs):
    n = inv_ref.shape[-1]
    for i in range(inv_ref.shape[0]):
        at = slice(i * n, (i + 1) * n)
        inv, other, weight = to_column(inv_ref[i]), to_column(other_ref[i]), to_column(weight_ref[i])
        normed, diff, scaled = matched(hidden_ref[at], sent_ref[at], gain_ref[...], inv, other, weight)
        square = to_lanes(jnp.sum(diff * diff, axis=-1, keepdims=True))
        cross = to_lanes(jnp.sum(normed * scaled, axis=-1, keepdims=True))
        if len(refs) > 1:
            square, cross = square + refs[0][i, :1], cross + refs[0][i, 1:]
        refs[-1][i, :1] = square
        refs[-1][i, 1:] = cross


def d_hidden_kernel(lows, at_ref, attn_ref, inv_ref, other_ref, weight_ref, mean_ref, *refs):
    d_ref, terms_ref, total_ref = refs[-3:]
    n, count = inv_ref.shape[-1], len(lows)
    for i in range(inv_ref.shape[0]):
        at = slice(i * n, (i + 1) * n)
        inv, other, weight = to_column(inv_ref[i]), to_column(other_ref[i]), to_column(weight_ref[i])
        mean = to_column(mean_ref[i])
        for low, hidden_ref, sent_ref, gain_ref in zip(lows, refs, refs[count:], refs[2 * count :]):
            normed, _, scaled = matched(hidden_ref[at], sent_ref[at], gain_ref[...], inv, other, weight)
            d_hidden = (inv * (scaled - normed * mean)).astype(d_ref.dtype)
            d_ref[at, low : low + d_hidden.shape[1]] = d_hidden
    terms = lax.dot_general(attn_ref[...], d_ref[...], (((0,), (0,)), ((), ())), preferred_element_type=jnp.float32)
    step, last = pl.program_id(0), pl.num_programs(0) - 1

    @pl.when(step == 0)
    def _():
        total_ref[...] = terms

    @pl.when((step > 0) & (step < last))
    def _():
        total_ref[...] += terms

    @pl.when(step == last)
    def _():
        terms_ref[...] = (total_ref[...] + terms).astype(terms_ref.dtype)


def terms_kernel(lows, at_ref, attn_ref, d_ref, *outs):
    terms = lax.dot_general(
        attn_ref[...], d_ref[...], (((0,), (0,)), ((), ())), preferred_element_type=jnp.float32
    ).astype(jnp.bfloat16)
    for low, out in zip(lows, outs):
        out[...] = terms[:, low : low + out.shape[1]]


def d_attn_kernel(lows, d_ref, *refs):
    outs = refs[len(lows) :]
    total = 0.0
    for low, weight_ref in zip(lows, refs):
        total = total + lax.dot_general(
            d_ref[:, low : low + weight_ref.shape[1]],
            weight_ref[...],
            (((1,), (1,)), ((), ())),
            preferred_element_type=jnp.float32,
        )
    total = total.astype(outs[0].dtype)
    n = outs[0].shape[1]
    for i, out in enumerate(outs):
        out[...] = total[:, i * n : (i + 1) * n]


def part_kernel(wide, places, member_ref, *refs):
    pieces, out, (wide_ref, sems) = refs[: len(places)], refs[-3], refs[-2:]
    copies = []
    for i, (ref, (other, low)) in enumerate(zip(pieces, places)):
        n = ref.shape[1]
        wide_ref[i, :, :n] = ref[...].astype(wide_ref.dtype)
        at = pl.multiple_of((member_ref[0] ^ other) * wide + low, LANES)
        copies.append(pltpu.make_async_copy(wide_ref.at[i, :, pl.ds(0, n)], out.at[:, pl.ds(at, n)], sems.at[i]))
        copies[-1].start()
    for copy in copies:
        copy.wait()


def put_parts(pieces, places, wide, width, member, into):
    rows, n = pieces[0].shape
    shape = jax.ShapeDtypeStruct((rows, width), jnp.float32)
    given = 1 + len(pieces)
    return pl.pallas_call(
        functools.partial(part_kernel, wide, places),
        grid_spec=pltpu.PrefetchScalarGridSpec(
            num_scalar_prefetch=1,
            grid=(1,),
            in_specs=[spec(p.shape, lambda i, *_: (0, 0), p.shape) for p in pieces] + [ANY] * len(into),
            out_specs=ANY,
            scratch_shapes=[pltpu.VMEM((len(pieces), rows, n), jnp.float32), pltpu.SemaphoreType.DMA((len(pieces),))],
        ),
        out_shape=shape,
        input_output_aliases={given: 0} if into else {},
        cost_estimate=cost(2.0),
        compiler_params=pltpu.CompilerParams(vmem_limit_bytes=32 * MIB),
    )(member.reshape(1), *pieces, *into)


def assemble_kernel(wide, places, member_ref, *refs):
    for ref, (other, low) in zip(refs[:-1], places):
        at = pl.multiple_of((member_ref[0] ^ other) * wide + low, LANES)
        refs[-1][:, pl.ds(at, ref.shape[1])] = ref[...].astype(refs[-1].dtype)


ANY = pl.BlockSpec(memory_space=pl.ANY)


def small_call(kernel, indices, ins, outs, into=None, micros=1.0, grid=1, scratch=(), most=False):
    out = pl.pallas_call(
        kernel,
        grid_spec=pltpu.PrefetchScalarGridSpec(
            num_scalar_prefetch=1,
            grid=(grid,),
            in_specs=[spec(b, m, a.shape) for a, b, m in ins] + [ANY] * (into is not None),
            out_specs=[pl.BlockSpec(b, m) for _, _, b, m in outs],
            scratch_shapes=list(scratch),
        ),
        out_shape=[jax.ShapeDtypeStruct(shape, d) for shape, d, _, _ in outs],
        input_output_aliases={} if into is None else {1 + len(ins): 0},
        cost_estimate=cost(micros),
        compiler_params=pltpu.CompilerParams(vmem_limit_bytes=60 * MIB) if most else room(ins, outs),
    )(jnp.stack([jnp.int32(i) for i in indices]), *[a for a, _, _ in ins], *(() if into is None else (into,)))
    return out


ORIGIN = lambda i, at: (0, 0)
DOWN = lambda i, at: (at[0], 0)


def split_kernel(count, at_ref, in_ref, *outs):
    for i in range(0, len(outs), count):
        at = at_ref[i // count]
        for out in outs[i : i + count]:
            n = out.shape[1]
            out[...] = in_ref[:, pl.ds(at if isinstance(at, int) else pl.multiple_of(at, LANES), n)]
            at = at + n


def cut_columns(array, places, widths):
    n = array.shape[0]
    if any(w % LANES for w in widths):
        return [lax.dynamic_slice(array, (0, p), (n, w)) for p in places for w in widths]
    outs = [((n, w), array.dtype, (n, w), ORIGIN) for _ in places for w in widths]
    return small_call(
        functools.partial(split_kernel, len(widths)), places, [(array, array.shape, ORIGIN)], outs
    )


def copy_kernel(at_ref, in_ref, *refs):
    refs[-1][...] = in_ref[...]


def place_rows(whole, piece, index):
    new = isinstance(whole, tuple)
    shape = whole if new else whole.shape
    outs = [(shape, piece.dtype, piece.shape, DOWN)]
    return small_call(copy_kernel, [index], [(piece, piece.shape, ORIGIN)], outs, None if new else whole)[0]


def take_rows(array, index, rows):
    block = (rows, array.shape[1])
    return small_call(copy_kernel, [index], [(array, block, DOWN)], [(block, array.dtype, block, ORIGIN)])[0]


def stack_kernel(across, at_ref, *refs):
    n, column = refs[0].shape[0], 0
    for i, ref in enumerate(refs[:-1]):
        row = i // across * n
        refs[-1][row : row + n, column : column + ref.shape[1]] = ref[...]
        column = (column + ref.shape[1]) % refs[-1].shape[1]


def pairs_kernel(at_ref, *refs):
    n, row, column = refs[0].shape[0], 0, 0
    for ref in refs[:-1]:
        refs[-1][row : row + n, column : column + ref.shape[1]] = ref[...]
        column += ref.shape[1]
        if column == refs[-1].shape[1]:
            row, column = row + n, 0


def stack_pairs(pairs):
    pieces = [x for pair in pairs for x in pair]
    n, width = pieces[0].shape[0], sum(x.shape[1] for x in pairs[0]) // 2
    shape = (2 * n * len(pairs), width)
    ins = [(x, x.shape, ORIGIN) for x in pieces]
    return small_call(pairs_kernel, [0], ins, [(shape, pieces[0].dtype, shape, ORIGIN)])[0]


def stack_blocks(rows):
    n = rows[0][0].shape[0]
    shape = (n * len(rows), sum(x.shape[1] for x in rows[0]))
    pieces = [x for row in rows for x in row]
    ins = [(x, x.shape, ORIGIN) for x in pieces]
    kernel = functools.partial(stack_kernel, len(rows[0]))
    return small_call(kernel, [0], ins, [(shape, pieces[0].dtype, shape, ORIGIN)])[0]


def add_kernel(low, at_ref, *refs):
    out_ref = refs[-1]
    total = 0.0
    for ref in refs[:-1]:
        n = out_ref.shape[1]
        part = ref[...] if ref.shape[1] == n else ref[:, low : low + n]
        total = total + part.astype(jnp.float32)
    out_ref[...] = total.astype(out_ref.dtype)


def sum_terms(got, low, terms, index):
    block = (got[0].shape[0], terms.shape[1])
    ins = [(g, g.shape, ORIGIN) for g in got] + [(terms, block, DOWN)]
    kernel = functools.partial(add_kernel, low)
    return small_call(kernel, [index], ins, [(block, terms.dtype, block, ORIGIN)])[0]


def fold_kernel(pieces, *refs):
    kept_ref, sent_ref = refs[2 * pieces :]
    half = kept_ref.shape[0]
    at = 0
    for near_ref, far_ref in zip(refs[:pieces], refs[pieces : 2 * pieces]):
        n = far_ref.shape[1]
        total = near_ref[...].astype(jnp.float32) + far_ref[...].astype(jnp.float32)
        total = total.astype(kept_ref.dtype)
        kept_ref[:, at : at + n] = total[:half]
        sent_ref[:, at : at + n] = total[half:]
        at += n


def fold(near, far):
    n, wide = near[0].shape[0], sum(x.shape[1] for x in near)
    ins = [(x, x.shape, lambda i: (0, 0)) for x in (*near, *far)]
    outs = [((n // 2, wide), near[0].dtype, (n // 2, wide), lambda i: (0, 0))] * 2
    return call(1.0, functools.partial(fold_kernel, len(near)), (1,), ins, outs)


def call(micros, kernel, grid, ins, outs):
    return pl.pallas_call(
        kernel,
        grid=grid,
        in_specs=[spec(b, m, a.shape) for a, b, m in ins],
        out_specs=[pl.BlockSpec(b, m) for _, _, b, m in outs],
        out_shape=[jax.ShapeDtypeStruct(s, d) for s, d, _, _ in outs],
        cost_estimate=cost(micros),
        compiler_params=room(ins, outs),
    )(*[a for a, _, _ in ins])


def attention_call(micros, kernel, length, arrays, moved, outs, first, number, group, into=None):
    seq = arrays[0].shape[0]
    there = pl.BlockSpec((seq, group), lambda i, *_: (0, i + first))
    here = pl.BlockSpec((seq, group), lambda i, *_: (0, i))
    alone = into is None
    into = into or ()
    shape = jax.ShapeDtypeStruct((seq, group * number) if alone else arrays[0].shape, jnp.bfloat16)
    given = 1 + len(arrays) + len(moved)
    return pl.pallas_call(
        kernel,
        grid_spec=pltpu.PrefetchScalarGridSpec(
            num_scalar_prefetch=1,
            grid=(number,),
            in_specs=[there] * len(arrays) + [here] * len(moved) + [pl.BlockSpec(memory_space=pl.ANY)] * len(into),
            out_specs=[here if alone else there] * outs,
        ),
        out_shape=[shape] * outs,
        input_output_aliases={given + i: i for i in range(len(into))},
        cost_estimate=cost(micros),
        compiler_params=vmem([((seq, group), jnp.bfloat16)] * (given - 1 + outs)),
    )(length.reshape(1), *arrays, *moved, *into)


def group_width(heads_width):
    heads = heads_width // DH
    return DH * max(g for g in (4, 2, 1) if heads % g == 0)


def tie(*values):
    return lax.optimization_barrier(values)


def split(values, *counts):
    lists, at = [], 0
    for count in counts:
        lists.append(list(values[at : at + count]))
        at += count
    return *lists, list(values[at:])


def send(value, axis, pairs):
    return lax.ppermute(value, axis, pairs)


LINE = 4
ENDS_OUT = [(2, 3), (1, 0)]
ENDS_IN = [(0, 1), (3, 2)]
MIDDLE = [(1, 2), (2, 1)]


def body(queries, keys, values, residual, event_ids, lengths, type_weight, w_out, gain):
    seq, heads_width = queries.shape[2:]
    width = residual.shape[3]
    parts = lax.axis_size("fsdp")
    team = lax.axis_size("dp")
    bits = bits_of(team)
    rows = team * seq
    shard_rows = w_out.shape[1]
    part = lax.axis_index("fsdp")
    member = lax.axis_index("dp")
    own = lax.axis_index(("dp", "fsdp"))
    length = lengths[own]
    count = jnp.sum(lengths).astype(jnp.float32)
    wide = width // team
    line = parts == LINE and shard_rows % LANES == 0
    two = line and wide % LANES == 0 and wide > LANES
    cut = -(-wide * 2 // (5 * LANES)) * LANES
    chunks = [(0, cut), (cut, wide)] if two else [(0, wide)]
    back_cut = -(-wide * 3 // (5 * LANES)) * LANES
    back_chunks = [(0, back_cut), (back_cut, wide)] if two else [(0, wide)]
    f32, bf16 = jnp.float32, jnp.bfloat16
    group = group_width(heads_width)
    steps = heads_width // group
    ends = sorted({0, 2 * steps // 5, 4 * steps // 5, steps})
    cuts = list(zip(ends[:-1], ends[1:]))
    q, k, v = queries[0, 0], keys[0, 0], values[0, 0]

    row_at = lambda i, *_: (i, 0)
    fixed = lambda i, *_: (0, 0)
    fixed3 = lambda i, *_: (0, 0, 0)
    stat_at = lambda i, *_: (i, 0, 0)
    lows = [low for low, _ in chunks]
    sizes = [high - low for low, high in chunks]

    order = [0]
    for bit in reversed(bits):
        order = order + [s ^ bit for s in order]

    column = (w_out[0], (shard_rows, wide), lambda i, at: (0, at[0]))
    if wide % LANES == 0:
        (block,) = small_call(copy_kernel, [member], [column], [((shard_rows, wide), bf16, (shard_rows, wide), ORIGIN)], most=True)
    else:
        (block,) = cut_columns(w_out[0], [member * wide], [wide])
    others = [1, 2] if line else list(range(1, parts))
    came = [swap(block, "fsdp", s) for s in others]

    attn = []
    middle = max(1, 2 * steps // 5)
    for first, final in [(0, middle), (middle, steps)] if steps > 1 else [(0, steps)]:
        attn += attention_call(
            1.5 * (final - first), forward_kernel, length, (q, k, v), (), 1, first, final - first, group
        )
    far = [swap(a, "dp", bits[-1]) for a in attn]
    if team == 4:
        attn.append(stack_blocks([attn]))
    home, _ = tie(residual[0, 0], attn[-1])
    mine = cut_columns(home, [(member ^ s) * wide for s in order], [wide])
    if team == 4:
        mine = [mine[0], mine[2], stack_blocks([[mine[1]], [mine[3]]])]
    own_parts = attn
    tied = tie(*came, block, count, *own_parts, *far, *mine)
    came, (block, count), own_parts, far, mine = split(tied, len(others), 2, len(own_parts), len(far))

    last = [send(block, "fsdp", MIDDLE), send(came[1], "fsdp", ENDS_OUT)] if line else []
    pairs = [[*own_parts[: len(far)], *far]]
    if team == 4:
        pairs.append([swap(x, "dp", 1) for x in (own_parts[-1], *far)])
    else:
        for bit in reversed(bits[:-1]):
            pairs = pairs + [[swap(x, "dp", bit) for x in pair] for pair in pairs]
    pairs = [stack_pairs(pairs)]
    each = []
    if team == 4:
        here, beside, across = mine
        across = swap(across, "dp", 2)
        passed_on = swap(stack_blocks([[beside], [take_rows(across, 1, seq)]]), "dp", 1)
        rest = [here, across, passed_on]
    else:
        rest = [swap(piece, "dp", s) if s else piece for s, piece in zip(order, mine)]
    tied = tie(*last, *pairs, *rest)
    last, (attn,), rest = split(tied, len(last), 1)
    spots = [part, *[part ^ s for s in others], *([part ^ 3] if line else [])]
    shapes = [(heads_width, n) for n in sizes]

    used = [block, *came, *last]

    def team_sum(value):
        shape = value.shape
        value = value.reshape((2,) * len(bits) + shape[1:])
        for axis, bit in enumerate(bits):
            value = value + jnp.flip(swap(value, "dp", bit), axis)
        return value.reshape(shape)

    my_gain = lax.dynamic_slice(gain[0], (member * wide,), (wide,))[None]
    gains = [my_gain[:, low:high] for low, high in chunks]
    tall = rows // 2

    lower = lambda i, *_: (1, 0)
    rest_blocks = [(a, fixed) for a in rest]
    if team == 4:
        rest_blocks = [(rest[0], fixed), (rest[1], fixed), (rest[2], fixed), (rest[2], lower)]
    hidden, sent, square, partner, weights = [], [], [], [], []
    for i, n in enumerate(sizes):
        first = used
        if i:
            square[0], *first = tie(square[0], *used)
        ins = [(a, a.shape, fixed) for a in (*first, gains[i])] + [(a, (seq, wide), m) for a, m in rest_blocks]
        outs = [
            ((rows, n), f32, (2 * seq, n), row_at),
            ((rows, n), bf16, (2 * seq, n), row_at),
            ((team, 1, seq), f32, (2, 1, seq), stat_at),
            (shapes[i], bf16, shapes[i], fixed),
        ]
        whole = ((rows, heads_width), bf16, (2 * seq, heads_width), row_at)
        ins = [(attn, whole[2], row_at), *ins]
        kernel = functools.partial(hidden_kernel, team, lows[i], [] if i else each, len(used))
        h, x, sq, weight, *new = small_call(kernel, spots, ins, outs, micros=2.0, grid=team // 2)
        weights.append(weight)
        if i + 1 < len(chunks):
            partner.append(swap(x, "copy", 1))
        hidden.append(h)
        sent.append(x)
        square.append(sq)
    inv = lax.rsqrt(team_sum(sum(square)) / width + 1e-06)
    inv_other = swap(inv, "copy", 1)
    partner.append(swap(sent[-1], "copy", 1))

    types = jnp.arange(type_weight.shape[0], dtype=jnp.int32)
    ids, _ = tie(event_ids, x)
    matches = ids[0][:, None] == types[None, :]
    looked_up = jnp.sum(jnp.where(matches, type_weight[None, :], f32(0.0)), axis=-1)
    tok_w = jnp.where(jnp.arange(seq, dtype=jnp.int32) < length, looked_up, f32(0.0))
    tok_w = tok_w.reshape(1, 1, seq)
    for bit in reversed(bits):
        tok_w = jnp.concatenate([tok_w, swap(tok_w, "dp", bit)], axis=0)
    row_scale = 2.0 * tok_w / (width * count)
    stats = [inv, inv_other, row_scale]

    both = []
    for i in range(len(chunks)):
        n = sizes[i]
        (found,) = call(
            3.0,
            match_kernel,
            (team // 2,),
            [(hidden[i], (2 * seq, n), row_at), (partner[i], (2 * seq, n), row_at), (gains[i], (1, n), fixed)]
            + [(a, (2, *a.shape[1:]), stat_at) for a in (*stats, *both[-1:])],
            [((team, 2, seq), f32, (2, 2, seq), stat_at)],
        )
        if i + 1 < len(chunks):
            found, partner[i + 1] = tie(found, partner[i + 1])
        both.append(found)
    both = team_sum(both[-1])
    loss = jnp.sum(tok_w[0] * both[0, :1]) / (width * count)
    mean = both[:, 1:] / width

    back_lows = [low for low, _ in back_chunks]
    back_sizes = [high - low for low, high in back_chunks]
    columns = shard_rows if line else heads_width
    d_hidden, terms = small_call(
        functools.partial(d_hidden_kernel, lows),
        [part ^ 3 if line else 0],
        [(attn, (2 * seq, columns), lambda i, at: (i, at[0]))]
        + [(x, (2, 1, seq), stat_at) for x in (*stats, mean)]
        + [(x, (2 * seq, x.shape[1]), lambda i, at: (i, 0)) for x in (*hidden, *partner)]
        + [(x, x.shape, fixed) for x in gains],
        [((rows, wide), bf16, (2 * seq, wide), lambda i, at: (i, 0)), ((columns, wide), bf16, (columns, wide), fixed)],
        grid=team // 2,
        scratch=[pltpu.VMEM((columns, wide), f32)],
        micros=4.0,
    )
    if line:
        early = [send(terms, "fsdp", MIDDLE), send(terms, "fsdp", ENDS_IN)]
        terms = small_call(
            functools.partial(terms_kernel, back_lows),
            [part ^ 1, part ^ 2, part],
            [(attn, (rows, shard_rows), lambda i, at: (0, at[i])), (d_hidden, (rows, wide), fixed)],
            [((3 * shard_rows, n), bf16, (shard_rows, n), lambda i, at: (i, 0)) for n in back_sizes],
            micros=4.0,
            grid=3,
        )
    else:
        early = [swap(take_rows(terms, part ^ s, shard_rows), "fsdp", s) for s in range(1, parts)]
        terms = [terms]

    across, each = group, 1

    def d_attn_rows(half, d_hidden, first, count):
        n = across * count
        return call(
            0.6 * count,
            functools.partial(d_attn_kernel, lows),
            (1,),
            [(d_hidden, (tall, wide), lambda i: (half, 0))]
            + [(w, (n, w.shape[1]), lambda i: (first // count, 0)) for w in weights],
            [((tall, across), bf16, (tall, across), fixed)] * count,
        )

    def d_attn_parts(half, d_hidden):
        total = heads_width // across
        parts = [(0, 2), (2, 2), (4, 1)] if total == 5 else [(0, total)]
        return [x for first, count in parts for x in d_attn_rows(half, d_hidden, first, count)]

    far = [swap(x, "dp", bits[0]) for x in d_attn_parts(1, d_hidden)]
    near = d_attn_parts(0, d_hidden)
    for bit in bits[1:-1]:
        near, far = zip(*[fold([x], [y]) for x, y in zip(near, far)])
        far = [swap(x, "dp", bit) for x in far]
    folded = [fold(near[each * first : each * final], far[each * first : each * final]) for first, final in cuts]
    kept, passed = zip(*folded)
    passed = [swap(passed[0], "dp", bits[-1]), *passed[1:]]
    near_terms = [take_rows(x, 0, shard_rows) for x in terms] if line else []
    tied = tie(*early, *terms, *kept, *passed, *near_terms)
    early, terms, kept, passed, near_terms = split(tied, len(early), len(back_chunks), len(cuts), len(cuts))

    def late_sends(i):
        if not line:
            return []
        beyond = sum_terms([early[1]], back_lows[i], terms[i], 1)
        return [swap(beyond, "fsdp", 2), swap(near_terms[i], "fsdp", 1)]

    def team_pieces(i, got):
        got = early[:1] + got if line else early
        total = sum_terms(got, back_lows[i], terms[i], 2 if line else part)
        pieces = {0: total}
        for bit in reversed(bits):
            pieces.update({s ^ bit: swap(p, "dp", bit) for s, p in pieces.items()})
        return [pieces[s] for s in order]

    def back(j, grads):
        first, last = cuts[j]
        arrays = (q, k, v), (kept[j], passed[j])
        micros = 1.5 * (last - first) + 1.0
        return attention_call(micros, backward_kernel, length, *arrays, 3, first, last - first, group, grads)

    got = late_sends(0)
    passed = [passed[0], *[swap(x, "dp", bits[-1]) for x in passed[1:]]]
    grads = back(0, ())
    early_parts = passed
    tied = tie(*got, *grads, *terms, *early, *near_terms, loss, *early_parts)
    got, grads, terms, early, near_terms, (loss,), early_parts = split(
        tied, len(got), 3, len(back_chunks), len(early), len(near_terms), 1
    )
    passed = [*early_parts, *passed[len(early_parts) :]]

    placed = []
    for i in range(1, len(back_chunks)):
        late = late_sends(i)
        placed += team_pieces(i - 1, got)
        if i == 1:
            for j in range(1, len(cuts)):
                grads = back(j, grads)
        tied = tie(*late, *grads)
        got, grads, _ = split(tied, len(late), 3)
    placed += team_pieces(len(back_chunks) - 1, got)
    if len(back_chunks) == 1:
        for j in range(1, len(cuts)):
            grads = back(j, grads)
    d_queries, d_keys, d_values = grads
    places = [(s, low) for low in back_lows for s in order]

    if two:
        out = ()
        for i in range(0, len(placed), team):
            out = (put_parts(placed[i : i + team], places[i : i + team], wide, width, member, out),)
        (out,) = out
    elif wide % LANES == 0:
        tall = next(t for t in (128, 64, 32, 16, shard_rows) if shard_rows % t == 0)
        out = pl.pallas_call(
            functools.partial(assemble_kernel, wide, places),
            grid_spec=pltpu.PrefetchScalarGridSpec(
                num_scalar_prefetch=1,
                grid=(shard_rows // tall,),
                in_specs=[pl.BlockSpec((tall, p.shape[1]), lambda i, *_: (i, 0)) for p in placed],
                out_specs=pl.BlockSpec((tall, width), lambda i, *_: (i, 0)),
            ),
            out_shape=jax.ShapeDtypeStruct((shard_rows, width), f32),
            cost_estimate=cost(1.0),
            compiler_params=vmem([((tall, width), bf16), ((tall, width), f32)]),
        )(member.reshape(1), *placed)
    else:
        out = jnp.zeros((shard_rows, width), f32)
        for piece, (s, low) in zip(placed, places):
            out = lax.dynamic_update_slice(out, piece.astype(f32), (0, (member ^ s) * wide + low))
    return (
        loss.reshape(1, 1),
        d_queries[None, None],
        d_keys[None, None],
        d_values[None, None],
        out[None],
    )


def solution(mesh):
    whole = P("copy", ("dp", "fsdp"), None, None)
    in_specs = (
        whole,
        whole,
        whole,
        whole,
        P(("dp", "fsdp"), None),
        P(),
        P(),
        P("copy", "fsdp", None),
        P("copy", None),
    )
    out_specs = (P("copy", ("dp", "fsdp")), whole, whole, whole, P("copy", "fsdp", None))
    return jax.shard_map(body, mesh=mesh, in_specs=in_specs, out_specs=out_specs, check_vma=False)
```

```python
import functools
import math

import jax
import jax.numpy as jnp
from jax import lax
from jax.experimental import pallas as pl
from jax.experimental.pallas import tpu as pltpu
from jax.sharding import PartitionSpec as P

DH = 128
LANES = 128
NEG = -1e30
MIB = 1 << 20
VALUES = 6
SCALE = MIB


def cost(micros):
    return pl.CostEstimate(flops=0, bytes_accessed=int(micros * SCALE), transcendentals=0)


def vmem(blocks, times=2):
    size = sum(math.prod(shape) * jnp.dtype(kind).itemsize for shape, kind in blocks)
    return pltpu.CompilerParams(vmem_limit_bytes=min(times * size + VALUES * MIB, 60 * MIB))


def spec(block, index, shape):
    if block == shape:
        return pl.BlockSpec(block, index, pipeline_mode=pl.Buffered(1))
    return pl.BlockSpec(block, index)


def room(ins, outs):
    once = [(b, a.dtype) for a, b, _ in ins if b == a.shape]
    twice = [(b, a.dtype) for a, b, _ in ins if b != a.shape] + [(b, d) for _, d, b, _ in outs]
    size = sum(math.prod(shape) * jnp.dtype(kind).itemsize for shape, kind in once + twice + twice)
    return pltpu.CompilerParams(vmem_limit_bytes=min(size + VALUES * MIB, 60 * MIB))


def swap(value, axis, bit):
    return lax.ppermute(value, axis, [(i, i ^ bit) for i in range(lax.axis_size(axis))])


def bits_of(size):
    return [1 << j for j in range(size.bit_length() - 1)]


def head_probs(query, key, valid):
    scores = lax.dot_general(query, key, (((1,), (1,)), ((), ())), preferred_element_type=jnp.float32)
    scores = jnp.where(valid, scores * (DH**-0.5), NEG)
    top = jnp.max(scores, axis=-1, keepdims=True)
    exps = jnp.exp(scores - top)
    return exps * (1.0 / jnp.sum(exps, axis=-1, keepdims=True))


def valid_mask(seq, length):
    rows = lax.broadcasted_iota(jnp.int32, (seq, seq), 0)
    cols = lax.broadcasted_iota(jnp.int32, (seq, seq), 1)
    return (cols <= rows) & (cols < length)


def forward_kernel(length_ref, q_ref, k_ref, v_ref, out_ref):
    seq, wide = q_ref.shape
    valid = valid_mask(seq, length_ref[0])
    for head in range(wide // DH):
        at = slice(head * DH, (head + 1) * DH)
        probs = head_probs(q_ref[:, at], k_ref[:, at], valid).astype(jnp.bfloat16)
        out_ref[:, at] = jnp.dot(probs, v_ref[:, at], preferred_element_type=jnp.float32).astype(out_ref.dtype)


def backward_kernel(length_ref, q_ref, k_ref, v_ref, one_ref, two_ref, *refs):
    dq_ref, dk_ref, dv_ref = refs[-3:]
    seq, wide = q_ref.shape
    valid = valid_mask(seq, length_ref[0])
    for head in range(wide // DH):
        at = slice(head * DH, (head + 1) * DH)
        query, key, value = q_ref[:, at], k_ref[:, at], v_ref[:, at]
        probs = head_probs(query, key, valid)
        d_attn = (one_ref[:, at].astype(jnp.float32) + two_ref[:, at].astype(jnp.float32)).astype(jnp.bfloat16)
        dv_ref[:, at] = lax.dot_general(
            probs.astype(jnp.bfloat16), d_attn, (((0,), (0,)), ((), ())), preferred_element_type=jnp.float32
        ).astype(dv_ref.dtype)
        dprob = lax.dot_general(d_attn, value, (((1,), (1,)), ((), ())), preferred_element_type=jnp.float32)
        delta = jnp.sum(dprob * probs, axis=-1, keepdims=True)
        ds = (probs * (dprob - delta) * (DH**-0.5)).astype(jnp.bfloat16)
        dq_ref[:, at] = jnp.dot(ds, key, preferred_element_type=jnp.float32).astype(dq_ref.dtype)
        dk_ref[:, at] = lax.dot_general(
            ds, query, (((0,), (0,)), ((), ())), preferred_element_type=jnp.float32
        ).astype(dk_ref.dtype)


def whole_kernel(low, count, at_ref, *refs):
    out = refs[-1]
    n, wide = refs[0].shape[0], out.shape[1]
    for i in range(count):
        block = refs[i][...] if refs[i].shape[1] == wide else refs[i][:, low : low + wide]
        if i == count - 1 and len(refs) - 1 > count:
            block = block + (refs[count][...] if refs[count].shape[1] == wide else refs[count][:, low : low + wide])
        out[pl.ds(pl.multiple_of(at_ref[i] * n, 16), n)] = block


def hidden_kernel(team, low, gathered, blocks, at_ref, *refs):
    if gathered:
        pieces, refs, attn_ref = refs[: sum(gathered)], refs[sum(gathered) : -1], refs[-1]
    else:
        attn_ref, refs = refs[0], refs[1:]
    weights, (gain_ref, *rest) = refs[:blocks], refs[blocks : blocks + 1 + team]
    hidden_ref, sent_ref, square_ref, weight_ref = refs[blocks + 1 + team :]
    n = rest[0].shape[0]

    def gather(i):
        row, column = 0, 0
        for piece in pieces[sum(gathered[:i]) : sum(gathered[: i + 1])]:
            attn_ref[row : row + n, column : column + piece.shape[1]] = piece[...]
            column += piece.shape[1]
            if column == attn_ref.shape[1]:
                row, column = row + n, 0

    def finish(i):
        for j in range(2):
            at = slice(j * n, (j + 1) * n)
            there = rest[2 * i + j]
            there = there[...] if there.shape[1] == pair.shape[1] else there[:, low : low + pair.shape[1]]
            hidden = there.astype(jnp.float32) + pair[at]
            hidden_ref[at] = hidden
            sent_ref[at] = (hidden * gain_ref[...]).astype(sent_ref.dtype)
            square_ref[j] = to_lanes(jnp.sum(hidden * hidden, axis=-1, keepdims=True))

    for i in range(team // 2 if gathered else 0):
        pl.when(pl.program_id(0) == i)(functools.partial(gather, i))
    pl.when(pl.program_id(0) == 0)(functools.partial(whole_kernel, low, at_ref.shape[0], at_ref, *weights, weight_ref))
    pair = jnp.dot(attn_ref[...], weight_ref[...], preferred_element_type=jnp.float32)
    for i in range(team // 2):
        pl.when(pl.program_id(0) == i)(functools.partial(finish, i))


def to_lanes(column):
    return jnp.transpose(jnp.broadcast_to(column, (column.shape[0], LANES)))[:1]


def to_column(row):
    return jnp.transpose(jnp.broadcast_to(row, (LANES, row.shape[1])))[:, :1]


def matched(hidden, sent, gain, inv, inv_other, weight):
    normed = hidden * inv
    diff = normed * gain - sent.astype(jnp.float32) * inv_other
    return normed, diff, weight * diff * gain


def match_kernel(hidden_ref, sent_ref, gain_ref, inv_ref, other_ref, weight_ref, *refs):
    n = inv_ref.shape[-1]
    for i in range(inv_ref.shape[0]):
        at = slice(i * n, (i + 1) * n)
        inv, other, weight = to_column(inv_ref[i]), to_column(other_ref[i]), to_column(weight_ref[i])
        normed, diff, scaled = matched(hidden_ref[at], sent_ref[at], gain_ref[...], inv, other, weight)
        square = to_lanes(jnp.sum(diff * diff, axis=-1, keepdims=True))
        cross = to_lanes(jnp.sum(normed * scaled, axis=-1, keepdims=True))
        if len(refs) > 1:
            square, cross = square + refs[0][i, :1], cross + refs[0][i, 1:]
        refs[-1][i, :1] = square
        refs[-1][i, 1:] = cross


def d_hidden_kernel(lows, at_ref, attn_ref, inv_ref, other_ref, weight_ref, mean_ref, *refs):
    d_ref, terms_ref, total_ref = refs[-3:]
    n, count = inv_ref.shape[-1], len(lows)
    for i in range(inv_ref.shape[0]):
        at = slice(i * n, (i + 1) * n)
        inv, other, weight = to_column(inv_ref[i]), to_column(other_ref[i]), to_column(weight_ref[i])
        mean = to_column(mean_ref[i])
        for low, hidden_ref, sent_ref, gain_ref in zip(lows, refs, refs[count:], refs[2 * count :]):
            normed, _, scaled = matched(hidden_ref[at], sent_ref[at], gain_ref[...], inv, other, weight)
            d_hidden = (inv * (scaled - normed * mean)).astype(d_ref.dtype)
            d_ref[at, low : low + d_hidden.shape[1]] = d_hidden
    terms = lax.dot_general(attn_ref[...], d_ref[...], (((0,), (0,)), ((), ())), preferred_element_type=jnp.float32)
    step, last = pl.program_id(0), pl.num_programs(0) - 1

    @pl.when(step == 0)
    def _():
        total_ref[...] = terms

    @pl.when((step > 0) & (step < last))
    def _():
        total_ref[...] += terms

    @pl.when(step == last)
    def _():
        terms_ref[...] = (total_ref[...] + terms).astype(terms_ref.dtype)


def terms_kernel(lows, at_ref, attn_ref, d_ref, *outs):
    terms = lax.dot_general(
        attn_ref[...], d_ref[...], (((0,), (0,)), ((), ())), preferred_element_type=jnp.float32
    ).astype(jnp.bfloat16)
    for low, out in zip(lows, outs):
        out[...] = terms[:, low : low + out.shape[1]]


def d_attn_kernel(lows, d_ref, *refs):
    outs = refs[len(lows) :]
    total = 0.0
    for low, weight_ref in zip(lows, refs):
        total = total + lax.dot_general(
            d_ref[:, low : low + weight_ref.shape[1]],
            weight_ref[...],
            (((1,), (1,)), ((), ())),
            preferred_element_type=jnp.float32,
        )
    total = total.astype(outs[0].dtype)
    n = outs[0].shape[1]
    for i, out in enumerate(outs):
        out[...] = total[:, i * n : (i + 1) * n]


def part_kernel(wide, places, member_ref, *refs):
    pieces, out, (wide_ref, sems) = refs[: len(places)], refs[-3], refs[-2:]
    copies = []
    for i, (ref, (other, low)) in enumerate(zip(pieces, places)):
        n = ref.shape[1]
        wide_ref[i, :, :n] = ref[...].astype(wide_ref.dtype)
        at = pl.multiple_of((member_ref[0] ^ other) * wide + low, LANES)
        copies.append(pltpu.make_async_copy(wide_ref.at[i, :, pl.ds(0, n)], out.at[:, pl.ds(at, n)], sems.at[i]))
        copies[-1].start()
    for copy in copies:
        copy.wait()


def put_parts(pieces, places, wide, width, member, into):
    rows, n = pieces[0].shape
    shape = jax.ShapeDtypeStruct((rows, width), jnp.float32)
    given = 1 + len(pieces)
    return pl.pallas_call(
        functools.partial(part_kernel, wide, places),
        grid_spec=pltpu.PrefetchScalarGridSpec(
            num_scalar_prefetch=1,
            grid=(1,),
            in_specs=[spec(p.shape, lambda i, *_: (0, 0), p.shape) for p in pieces] + [ANY] * len(into),
            out_specs=ANY,
            scratch_shapes=[pltpu.VMEM((len(pieces), rows, n), jnp.float32), pltpu.SemaphoreType.DMA((len(pieces),))],
        ),
        out_shape=shape,
        input_output_aliases={given: 0} if into else {},
        cost_estimate=cost(2.0),
        compiler_params=pltpu.CompilerParams(vmem_limit_bytes=32 * MIB),
    )(member.reshape(1), *pieces, *into)


def assemble_kernel(wide, places, member_ref, *refs):
    for ref, (other, low) in zip(refs[:-1], places):
        at = pl.multiple_of((member_ref[0] ^ other) * wide + low, LANES)
        refs[-1][:, pl.ds(at, ref.shape[1])] = ref[...].astype(refs[-1].dtype)


ANY = pl.BlockSpec(memory_space=pl.ANY)


def small_call(kernel, indices, ins, outs, into=None, micros=1.0, grid=1, scratch=(), most=False):
    out = pl.pallas_call(
        kernel,
        grid_spec=pltpu.PrefetchScalarGridSpec(
            num_scalar_prefetch=1,
            grid=(grid,),
            in_specs=[spec(b, m, a.shape) for a, b, m in ins] + [ANY] * (into is not None),
            out_specs=[pl.BlockSpec(b, m) for _, _, b, m in outs],
            scratch_shapes=list(scratch),
        ),
        out_shape=[jax.ShapeDtypeStruct(shape, d) for shape, d, _, _ in outs],
        input_output_aliases={} if into is None else {1 + len(ins): 0},
        cost_estimate=cost(micros),
        compiler_params=pltpu.CompilerParams(vmem_limit_bytes=60 * MIB) if most else room(ins, outs),
    )(jnp.stack([jnp.int32(i) for i in indices]), *[a for a, _, _ in ins], *(() if into is None else (into,)))
    return out


ORIGIN = lambda i, at: (0, 0)
DOWN = lambda i, at: (at[0], 0)


def split_kernel(count, at_ref, in_ref, *outs):
    for i in range(0, len(outs), count):
        at = at_ref[i // count]
        for out in outs[i : i + count]:
            n = out.shape[1]
            out[...] = in_ref[:, pl.ds(at if isinstance(at, int) else pl.multiple_of(at, LANES), n)]
            at = at + n


def cut_columns(array, places, widths):
    n = array.shape[0]
    if any(w % LANES for w in widths):
        return [lax.dynamic_slice(array, (0, p), (n, w)) for p in places for w in widths]
    outs = [((n, w), array.dtype, (n, w), ORIGIN) for _ in places for w in widths]
    return small_call(
        functools.partial(split_kernel, len(widths)), places, [(array, array.shape, ORIGIN)], outs
    )


def copy_kernel(at_ref, in_ref, *refs):
    refs[-1][...] = in_ref[...]


def place_rows(whole, piece, index):
    new = isinstance(whole, tuple)
    shape = whole if new else whole.shape
    outs = [(shape, piece.dtype, piece.shape, DOWN)]
    return small_call(copy_kernel, [index], [(piece, piece.shape, ORIGIN)], outs, None if new else whole)[0]


def take_rows(array, index, rows):
    block = (rows, array.shape[1])
    return small_call(copy_kernel, [index], [(array, block, DOWN)], [(block, array.dtype, block, ORIGIN)])[0]


def stack_kernel(across, at_ref, *refs):
    n, column = refs[0].shape[0], 0
    for i, ref in enumerate(refs[:-1]):
        row = i // across * n
        refs[-1][row : row + n, column : column + ref.shape[1]] = ref[...]
        column = (column + ref.shape[1]) % refs[-1].shape[1]


def pairs_kernel(at_ref, *refs):
    n, row, column = refs[0].shape[0], 0, 0
    for ref in refs[:-1]:
        refs[-1][row : row + n, column : column + ref.shape[1]] = ref[...]
        column += ref.shape[1]
        if column == refs[-1].shape[1]:
            row, column = row + n, 0


def stack_pairs(pairs):
    pieces = [x for pair in pairs for x in pair]
    n, width = pieces[0].shape[0], sum(x.shape[1] for x in pairs[0]) // 2
    shape = (2 * n * len(pairs), width)
    ins = [(x, x.shape, ORIGIN) for x in pieces]
    return small_call(pairs_kernel, [0], ins, [(shape, pieces[0].dtype, shape, ORIGIN)])[0]


def stack_blocks(rows):
    n = rows[0][0].shape[0]
    shape = (n * len(rows), sum(x.shape[1] for x in rows[0]))
    pieces = [x for row in rows for x in row]
    ins = [(x, x.shape, ORIGIN) for x in pieces]
    kernel = functools.partial(stack_kernel, len(rows[0]))
    return small_call(kernel, [0], ins, [(shape, pieces[0].dtype, shape, ORIGIN)])[0]


def add_kernel(low, at_ref, *refs):
    out_ref = refs[-1]
    total = 0.0
    for ref in refs[:-1]:
        n = out_ref.shape[1]
        part = ref[...] if ref.shape[1] == n else ref[:, low : low + n]
        total = total + part.astype(jnp.float32)
    out_ref[...] = total.astype(out_ref.dtype)


def sum_terms(got, low, terms, index):
    block = (got[0].shape[0], terms.shape[1])
    ins = [(g, g.shape, ORIGIN) for g in got] + [(terms, block, DOWN)]
    kernel = functools.partial(add_kernel, low)
    return small_call(kernel, [index], ins, [(block, terms.dtype, block, ORIGIN)])[0]


def fold_kernel(pieces, *refs):
    kept_ref, sent_ref = refs[2 * pieces :]
    half = kept_ref.shape[0]
    at = 0
    for near_ref, far_ref in zip(refs[:pieces], refs[pieces : 2 * pieces]):
        n = far_ref.shape[1]
        total = near_ref[...].astype(jnp.float32) + far_ref[...].astype(jnp.float32)
        total = total.astype(kept_ref.dtype)
        kept_ref[:, at : at + n] = total[:half]
        sent_ref[:, at : at + n] = total[half:]
        at += n


def fold(near, far):
    n, wide = near[0].shape[0], sum(x.shape[1] for x in near)
    ins = [(x, x.shape, lambda i: (0, 0)) for x in (*near, *far)]
    outs = [((n // 2, wide), near[0].dtype, (n // 2, wide), lambda i: (0, 0))] * 2
    return call(1.0, functools.partial(fold_kernel, len(near)), (1,), ins, outs)


def call(micros, kernel, grid, ins, outs):
    return pl.pallas_call(
        kernel,
        grid=grid,
        in_specs=[spec(b, m, a.shape) for a, b, m in ins],
        out_specs=[pl.BlockSpec(b, m) for _, _, b, m in outs],
        out_shape=[jax.ShapeDtypeStruct(s, d) for s, d, _, _ in outs],
        cost_estimate=cost(micros),
        compiler_params=room(ins, outs),
    )(*[a for a, _, _ in ins])


def attention_call(micros, kernel, length, arrays, moved, outs, first, number, group, into=None):
    seq = arrays[0].shape[0]
    there = pl.BlockSpec((seq, group), lambda i, *_: (0, i + first))
    here = pl.BlockSpec((seq, group), lambda i, *_: (0, i))
    alone = into is None
    into = into or ()
    shape = jax.ShapeDtypeStruct((seq, group * number) if alone else arrays[0].shape, jnp.bfloat16)
    given = 1 + len(arrays) + len(moved)
    return pl.pallas_call(
        kernel,
        grid_spec=pltpu.PrefetchScalarGridSpec(
            num_scalar_prefetch=1,
            grid=(number,),
            in_specs=[there] * len(arrays) + [here] * len(moved) + [pl.BlockSpec(memory_space=pl.ANY)] * len(into),
            out_specs=[here if alone else there] * outs,
        ),
        out_shape=[shape] * outs,
        input_output_aliases={given + i: i for i in range(len(into))},
        cost_estimate=cost(micros),
        compiler_params=vmem([((seq, group), jnp.bfloat16)] * (given - 1 + outs)),
    )(length.reshape(1), *arrays, *moved, *into)


def group_width(heads_width):
    heads = heads_width // DH
    return DH * max(g for g in (4, 2, 1) if heads % g == 0)


def tie(*values):
    return lax.optimization_barrier(values)


def split(values, *counts):
    lists, at = [], 0
    for count in counts:
        lists.append(list(values[at : at + count]))
        at += count
    return *lists, list(values[at:])


def send(value, axis, pairs):
    return lax.ppermute(value, axis, pairs)


LINE = 4
ENDS_OUT = [(2, 3), (1, 0)]
ENDS_IN = [(0, 1), (3, 2)]
MIDDLE = [(1, 2), (2, 1)]


def body(queries, keys, values, residual, event_ids, lengths, type_weight, w_out, gain):
    seq, heads_width = queries.shape[2:]
    width = residual.shape[3]
    parts = lax.axis_size("fsdp")
    team = lax.axis_size("dp")
    bits = bits_of(team)
    rows = team * seq
    shard_rows = w_out.shape[1]
    part = lax.axis_index("fsdp")
    member = lax.axis_index("dp")
    own = lax.axis_index(("dp", "fsdp"))
    length = lengths[own]
    count = jnp.sum(lengths).astype(jnp.float32)
    wide = width // team
    line = parts == LINE and shard_rows % LANES == 0
    two = line and wide % LANES == 0 and wide > LANES
    cut = -(-wide * 2 // (5 * LANES)) * LANES
    chunks = [(0, cut), (cut, wide)] if two else [(0, wide)]
    back_cut = -(-wide * 3 // (5 * LANES)) * LANES
    back_chunks = [(0, back_cut), (back_cut, wide)] if two else [(0, wide)]
    f32, bf16 = jnp.float32, jnp.bfloat16
    group = group_width(heads_width)
    steps = heads_width // group
    ends = sorted({0, steps // 5, 3 * steps // 5, steps})
    cuts = list(zip(ends[:-1], ends[1:]))
    q, k, v = queries[0, 0], keys[0, 0], values[0, 0]

    row_at = lambda i, *_: (i, 0)
    fixed = lambda i, *_: (0, 0)
    fixed3 = lambda i, *_: (0, 0, 0)
    stat_at = lambda i, *_: (i, 0, 0)
    lows = [low for low, _ in chunks]
    sizes = [high - low for low, high in chunks]

    order = [0]
    for bit in reversed(bits):
        order = order + [s ^ bit for s in order]

    column = (w_out[0], (shard_rows, wide), lambda i, at: (0, at[0]))
    if wide % LANES == 0:
        (block,) = small_call(copy_kernel, [member], [column], [((shard_rows, wide), bf16, (shard_rows, wide), ORIGIN)], most=True)
    else:
        (block,) = cut_columns(w_out[0], [member * wide], [wide])
    others = [1, 2] if line else list(range(1, parts))
    came = [swap(block, "fsdp", s) for s in others]

    attn = []
    middle = max(1, 2 * steps // 5)
    for first, final in [(0, middle), (middle, steps)] if steps > 1 else [(0, steps)]:
        attn += attention_call(
            1.5 * (final - first), forward_kernel, length, (q, k, v), (), 1, first, final - first, group
        )
    far = [swap(a, "dp", bits[-1]) for a in attn]
    if team == 4:
        attn.append(stack_blocks([attn]))
    home, _ = tie(residual[0, 0], attn[-1])
    mine = cut_columns(home, [(member ^ s) * wide for s in order], [wide])
    if team == 4:
        mine = [mine[0], mine[2], stack_blocks([[mine[1]], [mine[3]]])]
    own_parts = attn
    tied = tie(*came, block, count, *own_parts, *far, *mine)
    came, (block, count), own_parts, far, mine = split(tied, len(others), 2, len(own_parts), len(far))

    last = [send(block, "fsdp", MIDDLE), send(came[1], "fsdp", ENDS_OUT)] if line else []
    pairs = [[*own_parts[: len(far)], *far]]
    if team == 4:
        pairs.append([swap(x, "dp", 1) for x in (own_parts[-1], *far)])
    else:
        for bit in reversed(bits[:-1]):
            pairs = pairs + [[swap(x, "dp", bit) for x in pair] for pair in pairs]
    pairs = [stack_pairs(pairs)]
    each = []
    if team == 4:
        here, beside, across = mine
        across = swap(across, "dp", 2)
        passed_on = swap(stack_blocks([[beside], [take_rows(across, 1, seq)]]), "dp", 1)
        rest = [here, across, passed_on]
    else:
        rest = [swap(piece, "dp", s) if s else piece for s, piece in zip(order, mine)]
    tied = tie(*last, *pairs, *rest)
    last, (attn,), rest = split(tied, len(last), 1)
    spots = [part, *[part ^ s for s in others], *([part ^ 3] if line else [])]
    shapes = [(heads_width, n) for n in sizes]

    used = [block, *came, *last]

    def team_sum(value):
        shape = value.shape
        value = value.reshape((2,) * len(bits) + shape[1:])
        for axis, bit in enumerate(bits):
            value = value + jnp.flip(swap(value, "dp", bit), axis)
        return value.reshape(shape)

    my_gain = lax.dynamic_slice(gain[0], (member * wide,), (wide,))[None]
    gains = [my_gain[:, low:high] for low, high in chunks]
    tall = rows // 2

    lower = lambda i, *_: (1, 0)
    rest_blocks = [(a, fixed) for a in rest]
    if team == 4:
        rest_blocks = [(rest[0], fixed), (rest[1], fixed), (rest[2], fixed), (rest[2], lower)]
    hidden, sent, square, partner, weights = [], [], [], [], []
    for i, n in enumerate(sizes):
        first = used
        if i:
            square[0], *first = tie(square[0], *used)
        narrow = i == 0 and two
        across = n if narrow else wide
        ins = [(a, (shard_rows, across) if line else a.shape, fixed) for a in first] + [(gains[i], (1, n), fixed)]
        ins += [(a, (seq, across), m) for a, m in rest_blocks]
        outs = [
            ((rows, n), f32, (2 * seq, n), row_at),
            ((rows, n), bf16, (2 * seq, n), row_at),
            ((team, 1, seq), f32, (2, 1, seq), stat_at),
            (shapes[i], bf16, shapes[i], fixed),
        ]
        whole = ((rows, heads_width), bf16, (2 * seq, heads_width), row_at)
        ins = [(attn, whole[2], row_at), *ins]
        kernel = functools.partial(hidden_kernel, team, lows[i], [] if i else each, len(used))
        h, x, sq, weight, *new = small_call(kernel, spots, ins, outs, micros=2.0, grid=team // 2)
        weights.append(weight)
        if i + 1 < len(chunks):
            partner.append(swap(x, "copy", 1))
        hidden.append(h)
        sent.append(x)
        square.append(sq)
    inv = lax.rsqrt(team_sum(sum(square)) / width + 1e-06)
    inv_other = swap(inv, "copy", 1)
    partner.append(swap(sent[-1], "copy", 1))

    types = jnp.arange(type_weight.shape[0], dtype=jnp.int32)
    ids, _ = tie(event_ids, x)
    matches = ids[0][:, None] == types[None, :]
    looked_up = jnp.sum(jnp.where(matches, type_weight[None, :], f32(0.0)), axis=-1)
    tok_w = jnp.where(jnp.arange(seq, dtype=jnp.int32) < length, looked_up, f32(0.0))
    tok_w = tok_w.reshape(1, 1, seq)
    for bit in reversed(bits):
        tok_w = jnp.concatenate([tok_w, swap(tok_w, "dp", bit)], axis=0)
    row_scale = 2.0 * tok_w / (width * count)
    stats = [inv, inv_other, row_scale]

    both = []
    for i in range(len(chunks)):
        n = sizes[i]
        (found,) = call(
            3.0,
            match_kernel,
            (team // 2,),
            [(hidden[i], (2 * seq, n), row_at), (partner[i], (2 * seq, n), row_at), (gains[i], (1, n), fixed)]
            + [(a, (2, *a.shape[1:]), stat_at) for a in (*stats, *both[-1:])],
            [((team, 2, seq), f32, (2, 2, seq), stat_at)],
        )
        if i + 1 < len(chunks):
            found, partner[i + 1] = tie(found, partner[i + 1])
        both.append(found)
    both = team_sum(both[-1])
    loss = jnp.sum(tok_w[0] * both[0, :1]) / (width * count)
    mean = both[:, 1:] / width

    back_lows = [low for low, _ in back_chunks]
    back_sizes = [high - low for low, high in back_chunks]
    columns = shard_rows if line else heads_width
    d_hidden, terms = small_call(
        functools.partial(d_hidden_kernel, lows),
        [part ^ 3 if line else 0],
        [(attn, (2 * seq, columns), lambda i, at: (i, at[0]))]
        + [(x, (2, 1, seq), stat_at) for x in (*stats, mean)]
        + [(x, (2 * seq, x.shape[1]), lambda i, at: (i, 0)) for x in (*hidden, *partner)]
        + [(x, x.shape, fixed) for x in gains],
        [((rows, wide), bf16, (2 * seq, wide), lambda i, at: (i, 0)), ((columns, wide), bf16, (columns, wide), fixed)],
        grid=team // 2,
        scratch=[pltpu.VMEM((columns, wide), f32)],
        micros=4.0,
    )
    if line:
        early = [send(terms, "fsdp", MIDDLE), send(terms, "fsdp", ENDS_IN)]
        terms = small_call(
            functools.partial(terms_kernel, back_lows),
            [part ^ 1, part ^ 2, part],
            [(attn, (rows, shard_rows), lambda i, at: (0, at[i])), (d_hidden, (rows, wide), fixed)],
            [((3 * shard_rows, n), bf16, (shard_rows, n), lambda i, at: (i, 0)) for n in back_sizes],
            micros=4.0,
            grid=3,
        )
    else:
        early = [swap(take_rows(terms, part ^ s, shard_rows), "fsdp", s) for s in range(1, parts)]
        terms = [terms]

    across, each = group, 1

    def d_attn_rows(half, d_hidden, first, count):
        n = across * count
        return call(
            0.6 * count,
            functools.partial(d_attn_kernel, lows),
            (1,),
            [(d_hidden, (tall, wide), lambda i: (half, 0))]
            + [(w, (n, w.shape[1]), lambda i: (first // count, 0)) for w in weights],
            [((tall, across), bf16, (tall, across), fixed)] * count,
        )

    def d_attn_parts(half, d_hidden):
        total = heads_width // across
        parts = [(0, 2), (2, 2), (4, 1)] if total == 5 else [(0, total)]
        return [x for first, count in parts for x in d_attn_rows(half, d_hidden, first, count)]

    far = [swap(x, "dp", bits[0]) for x in d_attn_parts(1, d_hidden)]
    near = d_attn_parts(0, d_hidden)
    for bit in bits[1:-1]:
        near, far = zip(*[fold([x], [y]) for x, y in zip(near, far)])
        far = [swap(x, "dp", bit) for x in far]
    folded = [fold(near[each * first : each * final], far[each * first : each * final]) for first, final in cuts]
    kept, passed = zip(*folded)
    passed = [swap(passed[0], "dp", bits[-1]), *passed[1:]]
    near_terms = [take_rows(x, 0, shard_rows) for x in terms] if line else []
    tied = tie(*early, *terms, *kept, *passed, *near_terms)
    early, terms, kept, passed, near_terms = split(tied, len(early), len(back_chunks), len(cuts), len(cuts))

    def late_sends(i):
        if not line:
            return []
        beyond = sum_terms([early[1]], back_lows[i], terms[i], 1)
        return [swap(beyond, "fsdp", 2), swap(near_terms[i], "fsdp", 1)]

    def team_pieces(i, got):
        got = early[:1] + got if line else early
        total = sum_terms(got, back_lows[i], terms[i], 2 if line else part)
        pieces = {0: total}
        for bit in reversed(bits):
            pieces.update({s ^ bit: swap(p, "dp", bit) for s, p in pieces.items()})
        return [pieces[s] for s in order]

    def back(j, grads):
        first, last = cuts[j]
        arrays = (q, k, v), (kept[j], passed[j])
        micros = 1.5 * (last - first) + 1.0
        return attention_call(micros, backward_kernel, length, *arrays, 3, first, last - first, group, grads)

    got = late_sends(0)
    passed = [passed[0], *[swap(x, "dp", bits[-1]) for x in passed[1:]]]
    grads = back(0, ())
    backed = max(1, len(cuts) - 1)
    for j in range(1, backed):
        grads = back(j, grads)
    early_parts = passed
    tied = tie(*got, *grads, *terms, *early, *near_terms, loss, *early_parts)
    got, grads, terms, early, near_terms, (loss,), early_parts = split(
        tied, len(got), 3, len(back_chunks), len(early), len(near_terms), 1
    )
    passed = [*early_parts, *passed[len(early_parts) :]]

    placed = []
    for i in range(1, len(back_chunks)):
        late = late_sends(i)
        placed += team_pieces(i - 1, got)
        if i == 1:
            for j in range(backed, len(cuts)):
                grads = back(j, grads)
        tied = tie(*late, *grads)
        got, grads, _ = split(tied, len(late), 3)
    placed += team_pieces(len(back_chunks) - 1, got)
    if len(back_chunks) == 1:
        for j in range(backed, len(cuts)):
            grads = back(j, grads)
    d_queries, d_keys, d_values = grads
    places = [(s, low) for low in back_lows for s in order]

    if two:
        out = ()
        for i in range(0, len(placed), team):
            out = (put_parts(placed[i : i + team], places[i : i + team], wide, width, member, out),)
        (out,) = out
    elif wide % LANES == 0:
        tall = next(t for t in (128, 64, 32, 16, shard_rows) if shard_rows % t == 0)
        out = pl.pallas_call(
            functools.partial(assemble_kernel, wide, places),
            grid_spec=pltpu.PrefetchScalarGridSpec(
                num_scalar_prefetch=1,
                grid=(shard_rows // tall,),
                in_specs=[pl.BlockSpec((tall, p.shape[1]), lambda i, *_: (i, 0)) for p in placed],
                out_specs=pl.BlockSpec((tall, width), lambda i, *_: (i, 0)),
            ),
            out_shape=jax.ShapeDtypeStruct((shard_rows, width), f32),
            cost_estimate=cost(1.0),
            compiler_params=vmem([((tall, width), bf16), ((tall, width), f32)]),
        )(member.reshape(1), *placed)
    else:
        out = jnp.zeros((shard_rows, width), f32)
        for piece, (s, low) in zip(placed, places):
            out = lax.dynamic_update_slice(out, piece.astype(f32), (0, (member ^ s) * wide + low))
    return (
        loss.reshape(1, 1),
        d_queries[None, None],
        d_keys[None, None],
        d_values[None, None],
        out[None],
    )


def solution(mesh):
    whole = P("copy", ("dp", "fsdp"), None, None)
    in_specs = (
        whole,
        whole,
        whole,
        whole,
        P(("dp", "fsdp"), None),
        P(),
        P(),
        P("copy", "fsdp", None),
        P("copy", None),
    )
    out_specs = (P("copy", ("dp", "fsdp")), whole, whole, whole, P("copy", "fsdp", None))
    return jax.shard_map(body, mesh=mesh, in_specs=in_specs, out_specs=out_specs, check_vma=False)
```

```python
import functools
import math

import jax
import jax.numpy as jnp
from jax import lax
from jax.experimental import pallas as pl
from jax.experimental.pallas import tpu as pltpu
from jax.sharding import PartitionSpec as P

DH = 128
LANES = 128
NEG = -1e30
MIB = 1 << 20
VALUES = 6
SCALE = MIB


def cost(micros):
    return pl.CostEstimate(flops=0, bytes_accessed=int(micros * SCALE), transcendentals=0)


def vmem(blocks, times=2):
    size = sum(math.prod(shape) * jnp.dtype(kind).itemsize for shape, kind in blocks)
    return pltpu.CompilerParams(vmem_limit_bytes=min(times * size + VALUES * MIB, 60 * MIB))


def spec(block, index, shape):
    if block == shape:
        return pl.BlockSpec(block, index, pipeline_mode=pl.Buffered(1))
    return pl.BlockSpec(block, index)


def room(ins, outs):
    once = [(b, a.dtype) for a, b, _ in ins if b == a.shape]
    twice = [(b, a.dtype) for a, b, _ in ins if b != a.shape] + [(b, d) for _, d, b, _ in outs]
    size = sum(math.prod(shape) * jnp.dtype(kind).itemsize for shape, kind in once + twice + twice)
    return pltpu.CompilerParams(vmem_limit_bytes=min(size + VALUES * MIB, 60 * MIB))


def swap(value, axis, bit):
    return lax.ppermute(value, axis, [(i, i ^ bit) for i in range(lax.axis_size(axis))])


def bits_of(size):
    return [1 << j for j in range(size.bit_length() - 1)]


def head_probs(query, key, valid):
    scores = lax.dot_general(query, key, (((1,), (1,)), ((), ())), preferred_element_type=jnp.float32)
    scores = jnp.where(valid, scores * (DH**-0.5), NEG)
    top = jnp.max(scores, axis=-1, keepdims=True)
    exps = jnp.exp(scores - top)
    return exps * (1.0 / jnp.sum(exps, axis=-1, keepdims=True))


def valid_mask(seq, length):
    rows = lax.broadcasted_iota(jnp.int32, (seq, seq), 0)
    cols = lax.broadcasted_iota(jnp.int32, (seq, seq), 1)
    return (cols <= rows) & (cols < length)


def forward_kernel(length_ref, q_ref, k_ref, v_ref, out_ref):
    seq, wide = q_ref.shape
    valid = valid_mask(seq, length_ref[0])
    for head in range(wide // DH):
        at = slice(head * DH, (head + 1) * DH)
        probs = head_probs(q_ref[:, at], k_ref[:, at], valid).astype(jnp.bfloat16)
        out_ref[:, at] = jnp.dot(probs, v_ref[:, at], preferred_element_type=jnp.float32).astype(out_ref.dtype)


def backward_kernel(length_ref, q_ref, k_ref, v_ref, one_ref, two_ref, *refs):
    dq_ref, dk_ref, dv_ref = refs[-3:]
    seq, wide = q_ref.shape
    valid = valid_mask(seq, length_ref[0])
    for head in range(wide // DH):
        at = slice(head * DH, (head + 1) * DH)
        query, key, value = q_ref[:, at], k_ref[:, at], v_ref[:, at]
        probs = head_probs(query, key, valid)
        d_attn = (one_ref[:, at].astype(jnp.float32) + two_ref[:, at].astype(jnp.float32)).astype(jnp.bfloat16)
        dv_ref[:, at] = lax.dot_general(
            probs.astype(jnp.bfloat16), d_attn, (((0,), (0,)), ((), ())), preferred_element_type=jnp.float32
        ).astype(dv_ref.dtype)
        dprob = lax.dot_general(d_attn, value, (((1,), (1,)), ((), ())), preferred_element_type=jnp.float32)
        delta = jnp.sum(dprob * probs, axis=-1, keepdims=True)
        ds = (probs * (dprob - delta) * (DH**-0.5)).astype(jnp.bfloat16)
        dq_ref[:, at] = jnp.dot(ds, key, preferred_element_type=jnp.float32).astype(dq_ref.dtype)
        dk_ref[:, at] = lax.dot_general(
            ds, query, (((0,), (0,)), ((), ())), preferred_element_type=jnp.float32
        ).astype(dk_ref.dtype)


def whole_kernel(low, count, at_ref, *refs):
    out = refs[-1]
    n, wide = refs[0].shape[0], out.shape[1]
    for i in range(count):
        block = refs[i][...] if refs[i].shape[1] == wide else refs[i][:, low : low + wide]
        if i == count - 1 and len(refs) - 1 > count:
            block = block + (refs[count][...] if refs[count].shape[1] == wide else refs[count][:, low : low + wide])
        out[pl.ds(pl.multiple_of(at_ref[i] * n, 16), n)] = block


def hidden_kernel(team, low, gathered, blocks, at_ref, *refs):
    if gathered:
        pieces, refs, attn_ref = refs[: sum(gathered)], refs[sum(gathered) : -1], refs[-1]
    else:
        attn_ref, refs = refs[0], refs[1:]
    weights, (gain_ref, *rest) = refs[:blocks], refs[blocks : blocks + 1 + team]
    hidden_ref, sent_ref, square_ref, weight_ref = refs[blocks + 1 + team :]
    n = rest[0].shape[0]

    def gather(i):
        row, column = 0, 0
        for piece in pieces[sum(gathered[:i]) : sum(gathered[: i + 1])]:
            attn_ref[row : row + n, column : column + piece.shape[1]] = piece[...]
            column += piece.shape[1]
            if column == attn_ref.shape[1]:
                row, column = row + n, 0

    def finish(i):
        for j in range(2):
            at = slice(j * n, (j + 1) * n)
            there = rest[2 * i + j]
            there = there[...] if there.shape[1] == pair.shape[1] else there[:, low : low + pair.shape[1]]
            hidden = there.astype(jnp.float32) + pair[at]
            hidden_ref[at] = hidden
            sent_ref[at] = (hidden * gain_ref[...]).astype(sent_ref.dtype)
            square_ref[j] = to_lanes(jnp.sum(hidden * hidden, axis=-1, keepdims=True))

    for i in range(team // 2 if gathered else 0):
        pl.when(pl.program_id(0) == i)(functools.partial(gather, i))
    pl.when(pl.program_id(0) == 0)(functools.partial(whole_kernel, low, at_ref.shape[0], at_ref, *weights, weight_ref))
    pair = jnp.dot(attn_ref[...], weight_ref[...], preferred_element_type=jnp.float32)
    for i in range(team // 2):
        pl.when(pl.program_id(0) == i)(functools.partial(finish, i))


def to_lanes(column):
    return jnp.transpose(jnp.broadcast_to(column, (column.shape[0], LANES)))[:1]


def to_column(row):
    return jnp.transpose(jnp.broadcast_to(row, (LANES, row.shape[1])))[:, :1]


def matched(hidden, sent, gain, inv, inv_other, weight):
    normed = hidden * inv
    diff = normed * gain - sent.astype(jnp.float32) * inv_other
    return normed, diff, weight * diff * gain


def match_kernel(hidden_ref, sent_ref, gain_ref, inv_ref, other_ref, weight_ref, *refs):
    n = inv_ref.shape[-1]
    for i in range(inv_ref.shape[0]):
        at = slice(i * n, (i + 1) * n)
        inv, other, weight = to_column(inv_ref[i]), to_column(other_ref[i]), to_column(weight_ref[i])
        normed, diff, scaled = matched(hidden_ref[at], sent_ref[at], gain_ref[...], inv, other, weight)
        square = to_lanes(jnp.sum(diff * diff, axis=-1, keepdims=True))
        cross = to_lanes(jnp.sum(normed * scaled, axis=-1, keepdims=True))
        if len(refs) > 1:
            square, cross = square + refs[0][i, :1], cross + refs[0][i, 1:]
        refs[-1][i, :1] = square
        refs[-1][i, 1:] = cross


def d_hidden_kernel(lows, at_ref, attn_ref, inv_ref, other_ref, weight_ref, mean_ref, *refs):
    d_ref, terms_ref, total_ref = refs[-3:]
    n, count = inv_ref.shape[-1], len(lows)
    for i in range(inv_ref.shape[0]):
        at = slice(i * n, (i + 1) * n)
        inv, other, weight = to_column(inv_ref[i]), to_column(other_ref[i]), to_column(weight_ref[i])
        mean = to_column(mean_ref[i])
        for low, hidden_ref, sent_ref, gain_ref in zip(lows, refs, refs[count:], refs[2 * count :]):
            normed, _, scaled = matched(hidden_ref[at], sent_ref[at], gain_ref[...], inv, other, weight)
            d_hidden = (inv * (scaled - normed * mean)).astype(d_ref.dtype)
            d_ref[at, low : low + d_hidden.shape[1]] = d_hidden
    terms = lax.dot_general(attn_ref[...], d_ref[...], (((0,), (0,)), ((), ())), preferred_element_type=jnp.float32)
    step, last = pl.program_id(0), pl.num_programs(0) - 1

    @pl.when(step == 0)
    def _():
        total_ref[...] = terms

    @pl.when((step > 0) & (step < last))
    def _():
        total_ref[...] += terms

    @pl.when(step == last)
    def _():
        terms_ref[...] = (total_ref[...] + terms).astype(terms_ref.dtype)


def terms_kernel(lows, at_ref, attn_ref, d_ref, *outs):
    terms = lax.dot_general(
        attn_ref[...], d_ref[...], (((0,), (0,)), ((), ())), preferred_element_type=jnp.float32
    ).astype(jnp.bfloat16)
    for low, out in zip(lows, outs):
        out[...] = terms[:, low : low + out.shape[1]]


def d_attn_kernel(lows, d_ref, *refs):
    outs = refs[len(lows) :]
    total = 0.0
    for low, weight_ref in zip(lows, refs):
        total = total + lax.dot_general(
            d_ref[:, low : low + weight_ref.shape[1]],
            weight_ref[...],
            (((1,), (1,)), ((), ())),
            preferred_element_type=jnp.float32,
        )
    total = total.astype(outs[0].dtype)
    n = outs[0].shape[1]
    for i, out in enumerate(outs):
        out[...] = total[:, i * n : (i + 1) * n]


def part_kernel(wide, places, member_ref, *refs):
    pieces, out, (wide_ref, sems) = refs[: len(places)], refs[-3], refs[-2:]
    copies = []
    for i, (ref, (other, low)) in enumerate(zip(pieces, places)):
        n = ref.shape[1]
        wide_ref[i, :, :n] = ref[...].astype(wide_ref.dtype)
        at = pl.multiple_of((member_ref[0] ^ other) * wide + low, LANES)
        copies.append(pltpu.make_async_copy(wide_ref.at[i, :, pl.ds(0, n)], out.at[:, pl.ds(at, n)], sems.at[i]))
        copies[-1].start()
    for copy in copies:
        copy.wait()


def put_parts(pieces, places, wide, width, member, into):
    rows, n = pieces[0].shape
    shape = jax.ShapeDtypeStruct((rows, width), jnp.float32)
    given = 1 + len(pieces)
    return pl.pallas_call(
        functools.partial(part_kernel, wide, places),
        grid_spec=pltpu.PrefetchScalarGridSpec(
            num_scalar_prefetch=1,
            grid=(1,),
            in_specs=[spec(p.shape, lambda i, *_: (0, 0), p.shape) for p in pieces] + [ANY] * len(into),
            out_specs=ANY,
            scratch_shapes=[pltpu.VMEM((len(pieces), rows, n), jnp.float32), pltpu.SemaphoreType.DMA((len(pieces),))],
        ),
        out_shape=shape,
        input_output_aliases={given: 0} if into else {},
        cost_estimate=cost(2.0),
        compiler_params=pltpu.CompilerParams(vmem_limit_bytes=32 * MIB),
    )(member.reshape(1), *pieces, *into)


def assemble_kernel(wide, places, member_ref, *refs):
    for ref, (other, low) in zip(refs[:-1], places):
        at = pl.multiple_of((member_ref[0] ^ other) * wide + low, LANES)
        refs[-1][:, pl.ds(at, ref.shape[1])] = ref[...].astype(refs[-1].dtype)


ANY = pl.BlockSpec(memory_space=pl.ANY)


def small_call(kernel, indices, ins, outs, into=None, micros=1.0, grid=1, scratch=(), most=False):
    out = pl.pallas_call(
        kernel,
        grid_spec=pltpu.PrefetchScalarGridSpec(
            num_scalar_prefetch=1,
            grid=(grid,),
            in_specs=[spec(b, m, a.shape) for a, b, m in ins] + [ANY] * (into is not None),
            out_specs=[pl.BlockSpec(b, m) for _, _, b, m in outs],
            scratch_shapes=list(scratch),
        ),
        out_shape=[jax.ShapeDtypeStruct(shape, d) for shape, d, _, _ in outs],
        input_output_aliases={} if into is None else {1 + len(ins): 0},
        cost_estimate=cost(micros),
        compiler_params=pltpu.CompilerParams(vmem_limit_bytes=60 * MIB) if most else room(ins, outs),
    )(jnp.stack([jnp.int32(i) for i in indices]), *[a for a, _, _ in ins], *(() if into is None else (into,)))
    return out


ORIGIN = lambda i, at: (0, 0)
DOWN = lambda i, at: (at[0], 0)


def split_kernel(count, at_ref, in_ref, *outs):
    for i in range(0, len(outs), count):
        at = at_ref[i // count]
        for out in outs[i : i + count]:
            n = out.shape[1]
            out[...] = in_ref[:, pl.ds(at if isinstance(at, int) else pl.multiple_of(at, LANES), n)]
            at = at + n


def cut_columns(array, places, widths):
    n = array.shape[0]
    if any(w % LANES for w in widths):
        return [lax.dynamic_slice(array, (0, p), (n, w)) for p in places for w in widths]
    outs = [((n, w), array.dtype, (n, w), ORIGIN) for _ in places for w in widths]
    return small_call(
        functools.partial(split_kernel, len(widths)), places, [(array, array.shape, ORIGIN)], outs
    )


def copy_kernel(at_ref, in_ref, *refs):
    refs[-1][...] = in_ref[...]


def place_rows(whole, piece, index):
    new = isinstance(whole, tuple)
    shape = whole if new else whole.shape
    outs = [(shape, piece.dtype, piece.shape, DOWN)]
    return small_call(copy_kernel, [index], [(piece, piece.shape, ORIGIN)], outs, None if new else whole)[0]


def take_rows(array, index, rows):
    block = (rows, array.shape[1])
    return small_call(copy_kernel, [index], [(array, block, DOWN)], [(block, array.dtype, block, ORIGIN)])[0]


def stack_kernel(across, at_ref, *refs):
    n, column = refs[0].shape[0], 0
    for i, ref in enumerate(refs[:-1]):
        row = i // across * n
        refs[-1][row : row + n, column : column + ref.shape[1]] = ref[...]
        column = (column + ref.shape[1]) % refs[-1].shape[1]


def pairs_kernel(at_ref, *refs):
    n, row, column = refs[0].shape[0], 0, 0
    for ref in refs[:-1]:
        refs[-1][row : row + n, column : column + ref.shape[1]] = ref[...]
        column += ref.shape[1]
        if column == refs[-1].shape[1]:
            row, column = row + n, 0


def stack_pairs(pairs):
    pieces = [x for pair in pairs for x in pair]
    n, width = pieces[0].shape[0], sum(x.shape[1] for x in pairs[0]) // 2
    shape = (2 * n * len(pairs), width)
    ins = [(x, x.shape, ORIGIN) for x in pieces]
    return small_call(pairs_kernel, [0], ins, [(shape, pieces[0].dtype, shape, ORIGIN)])[0]


def stack_blocks(rows):
    n = rows[0][0].shape[0]
    shape = (n * len(rows), sum(x.shape[1] for x in rows[0]))
    pieces = [x for row in rows for x in row]
    ins = [(x, x.shape, ORIGIN) for x in pieces]
    kernel = functools.partial(stack_kernel, len(rows[0]))
    return small_call(kernel, [0], ins, [(shape, pieces[0].dtype, shape, ORIGIN)])[0]


def add_kernel(low, at_ref, *refs):
    out_ref = refs[-1]
    total = 0.0
    for ref in refs[:-1]:
        n = out_ref.shape[1]
        part = ref[...] if ref.shape[1] == n else ref[:, low : low + n]
        total = total + part.astype(jnp.float32)
    out_ref[...] = total.astype(out_ref.dtype)


def sum_terms(got, low, terms, index):
    block = (got[0].shape[0], terms.shape[1])
    ins = [(g, g.shape, ORIGIN) for g in got] + [(terms, block, DOWN)]
    kernel = functools.partial(add_kernel, low)
    return small_call(kernel, [index], ins, [(block, terms.dtype, block, ORIGIN)])[0]


def fold_kernel(pieces, *refs):
    kept_ref, sent_ref = refs[2 * pieces :]
    half = kept_ref.shape[0]
    at = 0
    for near_ref, far_ref in zip(refs[:pieces], refs[pieces : 2 * pieces]):
        n = far_ref.shape[1]
        total = near_ref[...].astype(jnp.float32) + far_ref[...].astype(jnp.float32)
        total = total.astype(kept_ref.dtype)
        kept_ref[:, at : at + n] = total[:half]
        sent_ref[:, at : at + n] = total[half:]
        at += n


def fold(near, far):
    n, wide = near[0].shape[0], sum(x.shape[1] for x in near)
    ins = [(x, x.shape, lambda i: (0, 0)) for x in (*near, *far)]
    outs = [((n // 2, wide), near[0].dtype, (n // 2, wide), lambda i: (0, 0))] * 2
    return call(1.0, functools.partial(fold_kernel, len(near)), (1,), ins, outs)


def call(micros, kernel, grid, ins, outs):
    return pl.pallas_call(
        kernel,
        grid=grid,
        in_specs=[spec(b, m, a.shape) for a, b, m in ins],
        out_specs=[pl.BlockSpec(b, m) for _, _, b, m in outs],
        out_shape=[jax.ShapeDtypeStruct(s, d) for s, d, _, _ in outs],
        cost_estimate=cost(micros),
        compiler_params=room(ins, outs),
    )(*[a for a, _, _ in ins])


def attention_call(micros, kernel, length, arrays, moved, outs, first, number, group, into=None):
    seq = arrays[0].shape[0]
    there = pl.BlockSpec((seq, group), lambda i, *_: (0, i + first))
    here = pl.BlockSpec((seq, group), lambda i, *_: (0, i))
    alone = into is None
    into = into or ()
    shape = jax.ShapeDtypeStruct((seq, group * number) if alone else arrays[0].shape, jnp.bfloat16)
    given = 1 + len(arrays) + len(moved)
    return pl.pallas_call(
        kernel,
        grid_spec=pltpu.PrefetchScalarGridSpec(
            num_scalar_prefetch=1,
            grid=(number,),
            in_specs=[there] * len(arrays) + [here] * len(moved) + [pl.BlockSpec(memory_space=pl.ANY)] * len(into),
            out_specs=[here if alone else there] * outs,
        ),
        out_shape=[shape] * outs,
        input_output_aliases={given + i: i for i in range(len(into))},
        cost_estimate=cost(micros),
        compiler_params=vmem([((seq, group), jnp.bfloat16)] * (given - 1 + outs)),
    )(length.reshape(1), *arrays, *moved, *into)


def group_width(heads_width):
    heads = heads_width // DH
    return DH * max(g for g in (4, 2, 1) if heads % g == 0)


def tie(*values):
    return lax.optimization_barrier(values)


def split(values, *counts):
    lists, at = [], 0
    for count in counts:
        lists.append(list(values[at : at + count]))
        at += count
    return *lists, list(values[at:])


def send(value, axis, pairs):
    return lax.ppermute(value, axis, pairs)


LINE = 4
ENDS_OUT = [(2, 3), (1, 0)]
ENDS_IN = [(0, 1), (3, 2)]
MIDDLE = [(1, 2), (2, 1)]


def body(queries, keys, values, residual, event_ids, lengths, type_weight, w_out, gain):
    seq, heads_width = queries.shape[2:]
    width = residual.shape[3]
    parts = lax.axis_size("fsdp")
    team = lax.axis_size("dp")
    bits = bits_of(team)
    rows = team * seq
    shard_rows = w_out.shape[1]
    part = lax.axis_index("fsdp")
    member = lax.axis_index("dp")
    own = lax.axis_index(("dp", "fsdp"))
    length = lengths[own]
    count = jnp.sum(lengths).astype(jnp.float32)
    wide = width // team
    line = parts == LINE and shard_rows % LANES == 0
    two = line and wide % LANES == 0 and wide > LANES
    cut = -(-wide * 2 // (5 * LANES)) * LANES
    chunks = [(0, cut), (cut, wide)] if two else [(0, wide)]
    back_cut = -(-wide * 3 // (5 * LANES)) * LANES
    back_chunks = [(0, back_cut), (back_cut, wide)] if two else [(0, wide)]
    f32, bf16 = jnp.float32, jnp.bfloat16
    group = group_width(heads_width)
    steps = heads_width // group
    ends = sorted({0, steps // 5, 3 * steps // 5, steps})
    cuts = list(zip(ends[:-1], ends[1:]))
    q, k, v = queries[0, 0], keys[0, 0], values[0, 0]

    row_at = lambda i, *_: (i, 0)
    fixed = lambda i, *_: (0, 0)
    fixed3 = lambda i, *_: (0, 0, 0)
    stat_at = lambda i, *_: (i, 0, 0)
    lows = [low for low, _ in chunks]
    sizes = [high - low for low, high in chunks]

    order = [0]
    for bit in reversed(bits):
        order = order + [s ^ bit for s in order]

    column = (w_out[0], (shard_rows, wide), lambda i, at: (0, at[0]))
    if wide % LANES == 0:
        (block,) = small_call(copy_kernel, [member], [column], [((shard_rows, wide), bf16, (shard_rows, wide), ORIGIN)], most=True)
    else:
        (block,) = cut_columns(w_out[0], [member * wide], [wide])
    others = [1, 2] if line else list(range(1, parts))
    came = [swap(block, "fsdp", s) for s in others]

    attn = []
    middle = max(1, 2 * steps // 5)
    for first, final in [(0, middle), (middle, steps)] if steps > 1 else [(0, steps)]:
        attn += attention_call(
            1.5 * (final - first), forward_kernel, length, (q, k, v), (), 1, first, final - first, group
        )
    far = [swap(a, "dp", bits[-1]) for a in attn]
    if team == 4:
        attn.append(stack_blocks([attn]))
    home, _ = tie(residual[0, 0], attn[-1])
    mine = cut_columns(home, [(member ^ s) * wide for s in order], [wide])
    if team == 4:
        mine = [mine[0], mine[2], stack_blocks([[mine[1]], [mine[3]]])]
    own_parts = attn
    tied = tie(*came, block, count, *own_parts, *far, *mine)
    came, (block, count), own_parts, far, mine = split(tied, len(others), 2, len(own_parts), len(far))

    last = [send(block, "fsdp", MIDDLE), send(came[1], "fsdp", ENDS_OUT)] if line else []
    pairs = [[*own_parts[: len(far)], *far]]
    if team == 4:
        pairs.append([swap(x, "dp", 1) for x in (own_parts[-1], *far)])
    else:
        for bit in reversed(bits[:-1]):
            pairs = pairs + [[swap(x, "dp", bit) for x in pair] for pair in pairs]
    pairs = [stack_pairs(pairs)]
    each = []
    if team == 4:
        here, beside, across = mine
        across = swap(across, "dp", 2)
        passed_on = swap(stack_blocks([[beside], [take_rows(across, 1, seq)]]), "dp", 1)
        rest = [here, across, passed_on]
    else:
        rest = [swap(piece, "dp", s) if s else piece for s, piece in zip(order, mine)]
    tied = tie(*last, *pairs, *rest)
    last, (attn,), rest = split(tied, len(last), 1)
    spots = [part, *[part ^ s for s in others], *([part ^ 3] if line else [])]
    shapes = [(heads_width, n) for n in sizes]

    used = [block, *came, *last]

    def team_sum(value):
        shape = value.shape
        value = value.reshape((2,) * len(bits) + shape[1:])
        for axis, bit in enumerate(bits):
            value = value + jnp.flip(swap(value, "dp", bit), axis)
        return value.reshape(shape)

    my_gain = lax.dynamic_slice(gain[0], (member * wide,), (wide,))[None]
    gains = [my_gain[:, low:high] for low, high in chunks]
    tall = rows // 2

    lower = lambda i, *_: (1, 0)
    rest_blocks = [(a, fixed) for a in rest]
    if team == 4:
        rest_blocks = [(rest[0], fixed), (rest[1], fixed), (rest[2], fixed), (rest[2], lower)]
    hidden, sent, square, partner, weights = [], [], [], [], []
    for i, n in enumerate(sizes):
        first = used
        if i:
            square[0], *first = tie(square[0], *used)
        narrow = i == 0 and two
        across = n if narrow else wide
        ins = [(a, (shard_rows, across) if line else a.shape, fixed) for a in first] + [(gains[i], (1, n), fixed)]
        ins += [(a, (seq, across), m) for a, m in rest_blocks]
        outs = [
            ((rows, n), f32, (2 * seq, n), row_at),
            ((rows, n), bf16, (2 * seq, n), row_at),
            ((team, 1, seq), f32, (2, 1, seq), stat_at),
            (shapes[i], bf16, shapes[i], fixed),
        ]
        whole = ((rows, heads_width), bf16, (2 * seq, heads_width), row_at)
        ins = [(attn, whole[2], row_at), *ins]
        kernel = functools.partial(hidden_kernel, team, lows[i], [] if i else each, len(used))
        h, x, sq, weight, *new = small_call(kernel, spots, ins, outs, micros=2.0, grid=team // 2)
        weights.append(weight)
        if i + 1 < len(chunks):
            partner.append(swap(x, "copy", 1))
        hidden.append(h)
        sent.append(x)
        square.append(sq)
    inv = lax.rsqrt(team_sum(sum(square)) / width + 1e-06)
    inv_other = swap(inv, "copy", 1)
    partner.append(swap(sent[-1], "copy", 1))

    types = jnp.arange(type_weight.shape[0], dtype=jnp.int32)
    ids, _ = tie(event_ids, x)
    matches = ids[0][:, None] == types[None, :]
    looked_up = jnp.sum(jnp.where(matches, type_weight[None, :], f32(0.0)), axis=-1)
    tok_w = jnp.where(jnp.arange(seq, dtype=jnp.int32) < length, looked_up, f32(0.0))
    tok_w = tok_w.reshape(1, 1, seq)
    for bit in reversed(bits):
        tok_w = jnp.concatenate([tok_w, swap(tok_w, "dp", bit)], axis=0)
    row_scale = 2.0 * tok_w / (width * count)
    stats = [inv, inv_other, row_scale]

    both = []
    for i in range(len(chunks)):
        n = sizes[i]
        (found,) = call(
            3.0,
            match_kernel,
            (team // 2,),
            [(hidden[i], (2 * seq, n), row_at), (partner[i], (2 * seq, n), row_at), (gains[i], (1, n), fixed)]
            + [(a, (2, *a.shape[1:]), stat_at) for a in (*stats, *both[-1:])],
            [((team, 2, seq), f32, (2, 2, seq), stat_at)],
        )
        if i + 1 < len(chunks):
            found, partner[i + 1] = tie(found, partner[i + 1])
        both.append(found)
    both = team_sum(both[-1])
    loss = jnp.sum(tok_w[0] * both[0, :1]) / (width * count)
    mean = both[:, 1:] / width

    back_lows = [low for low, _ in back_chunks]
    back_sizes = [high - low for low, high in back_chunks]
    columns = shard_rows if line else heads_width
    d_hidden, terms = small_call(
        functools.partial(d_hidden_kernel, lows),
        [part ^ 3 if line else 0],
        [(attn, (2 * seq, columns), lambda i, at: (i, at[0]))]
        + [(x, (2, 1, seq), stat_at) for x in (*stats, mean)]
        + [(x, (2 * seq, x.shape[1]), lambda i, at: (i, 0)) for x in (*hidden, *partner)]
        + [(x, x.shape, fixed) for x in gains],
        [((rows, wide), bf16, (2 * seq, wide), lambda i, at: (i, 0)), ((columns, wide), bf16, (columns, wide), fixed)],
        grid=team // 2,
        scratch=[pltpu.VMEM((columns, wide), f32)],
        micros=4.0,
    )
    if line:
        early = [send(terms, "fsdp", MIDDLE), send(terms, "fsdp", ENDS_IN)]
        terms = small_call(
            functools.partial(terms_kernel, back_lows),
            [part ^ 1, part ^ 2, part],
            [(attn, (rows, shard_rows), lambda i, at: (0, at[i])), (d_hidden, (rows, wide), fixed)],
            [((3 * shard_rows, n), bf16, (shard_rows, n), lambda i, at: (i, 0)) for n in back_sizes],
            micros=4.0,
            grid=3,
        )
    else:
        early = [swap(take_rows(terms, part ^ s, shard_rows), "fsdp", s) for s in range(1, parts)]
        terms = [terms]

    across, each = group, 1

    def d_attn_rows(half, d_hidden, first, count):
        n = across * count
        return call(
            0.6 * count,
            functools.partial(d_attn_kernel, lows),
            (1,),
            [(d_hidden, (tall, wide), lambda i: (half, 0))]
            + [(w, (n, w.shape[1]), lambda i: (first // count, 0)) for w in weights],
            [((tall, across), bf16, (tall, across), fixed)] * count,
        )

    def d_attn_parts(half, d_hidden):
        total = heads_width // across
        parts = [(i, 1) for i in range(total)]
        return [x for first, count in parts for x in d_attn_rows(half, d_hidden, first, count)]

    far = [swap(x, "dp", bits[0]) for x in d_attn_parts(1, d_hidden)]
    near = d_attn_parts(0, d_hidden)
    for bit in bits[1:-1]:
        near, far = zip(*[fold([x], [y]) for x, y in zip(near, far)])
        far = [swap(x, "dp", bit) for x in far]
    folded = [fold(near[each * first : each * final], far[each * first : each * final]) for first, final in cuts]
    kept, passed = zip(*folded)
    passed = [swap(passed[0], "dp", bits[-1]), *passed[1:]]
    near_terms = [take_rows(x, 0, shard_rows) for x in terms] if line else []
    tied = tie(*early, *terms, *kept, *passed, *near_terms)
    early, terms, kept, passed, near_terms = split(tied, len(early), len(back_chunks), len(cuts), len(cuts))

    def late_sends(i):
        if not line:
            return []
        beyond = sum_terms([early[1]], back_lows[i], terms[i], 1)
        return [swap(beyond, "fsdp", 2), swap(near_terms[i], "fsdp", 1)]

    def team_pieces(i, got):
        got = early[:1] + got if line else early
        total = sum_terms(got, back_lows[i], terms[i], 2 if line else part)
        pieces = {0: total}
        for bit in reversed(bits):
            pieces.update({s ^ bit: swap(p, "dp", bit) for s, p in pieces.items()})
        return [pieces[s] for s in order]

    def back(j, grads):
        first, last = cuts[j]
        arrays = (q, k, v), (kept[j], passed[j])
        micros = 1.5 * (last - first) + 1.0
        return attention_call(micros, backward_kernel, length, *arrays, 3, first, last - first, group, grads)

    got = late_sends(0)
    passed = [passed[0], *[swap(x, "dp", bits[-1]) for x in passed[1:]]]
    grads = back(0, ())
    backed = max(1, len(cuts) - 1)
    for j in range(1, backed):
        grads = back(j, grads)
    early_parts = passed
    tied = tie(*got, *grads, *terms, *early, *near_terms, loss, *early_parts)
    got, grads, terms, early, near_terms, (loss,), early_parts = split(
        tied, len(got), 3, len(back_chunks), len(early), len(near_terms), 1
    )
    passed = [*early_parts, *passed[len(early_parts) :]]

    placed = []
    for i in range(1, len(back_chunks)):
        late = late_sends(i)
        placed += team_pieces(i - 1, got)
        if i == 1:
            for j in range(backed, len(cuts)):
                grads = back(j, grads)
        tied = tie(*late, *grads)
        got, grads, _ = split(tied, len(late), 3)
    placed += team_pieces(len(back_chunks) - 1, got)
    if len(back_chunks) == 1:
        for j in range(backed, len(cuts)):
            grads = back(j, grads)
    d_queries, d_keys, d_values = grads
    places = [(s, low) for low in back_lows for s in order]

    if two:
        out = ()
        for i in range(0, len(placed), team):
            out = (put_parts(placed[i : i + team], places[i : i + team], wide, width, member, out),)
        (out,) = out
    elif wide % LANES == 0:
        tall = next(t for t in (128, 64, 32, 16, shard_rows) if shard_rows % t == 0)
        out = pl.pallas_call(
            functools.partial(assemble_kernel, wide, places),
            grid_spec=pltpu.PrefetchScalarGridSpec(
                num_scalar_prefetch=1,
                grid=(shard_rows // tall,),
                in_specs=[pl.BlockSpec((tall, p.shape[1]), lambda i, *_: (i, 0)) for p in placed],
                out_specs=pl.BlockSpec((tall, width), lambda i, *_: (i, 0)),
            ),
            out_shape=jax.ShapeDtypeStruct((shard_rows, width), f32),
            cost_estimate=cost(1.0),
            compiler_params=vmem([((tall, width), bf16), ((tall, width), f32)]),
        )(member.reshape(1), *placed)
    else:
        out = jnp.zeros((shard_rows, width), f32)
        for piece, (s, low) in zip(placed, places):
            out = lax.dynamic_update_slice(out, piece.astype(f32), (0, (member ^ s) * wide + low))
    return (
        loss.reshape(1, 1),
        d_queries[None, None],
        d_keys[None, None],
        d_values[None, None],
        out[None],
    )


def solution(mesh):
    whole = P("copy", ("dp", "fsdp"), None, None)
    in_specs = (
        whole,
        whole,
        whole,
        whole,
        P(("dp", "fsdp"), None),
        P(),
        P(),
        P("copy", "fsdp", None),
        P("copy", None),
    )
    out_specs = (P("copy", ("dp", "fsdp")), whole, whole, whole, P("copy", "fsdp", None))
    return jax.shard_map(body, mesh=mesh, in_specs=in_specs, out_specs=out_specs, check_vma=False)
```

```python
import functools
import math

import jax
import jax.numpy as jnp
from jax import lax
from jax.experimental import pallas as pl
from jax.experimental.pallas import tpu as pltpu
from jax.sharding import PartitionSpec as P

DH = 128
LANES = 128
NEG = -1e30
MIB = 1 << 20
VALUES = 6
SCALE = MIB


def cost(micros):
    return pl.CostEstimate(flops=0, bytes_accessed=int(micros * SCALE), transcendentals=0)


def vmem(blocks, times=2):
    size = sum(math.prod(shape) * jnp.dtype(kind).itemsize for shape, kind in blocks)
    return pltpu.CompilerParams(vmem_limit_bytes=min(times * size + VALUES * MIB, 60 * MIB))


def spec(block, index, shape):
    if block == shape:
        return pl.BlockSpec(block, index, pipeline_mode=pl.Buffered(1))
    return pl.BlockSpec(block, index)


def room(ins, outs):
    once = [(b, a.dtype) for a, b, _ in ins if b == a.shape]
    twice = [(b, a.dtype) for a, b, _ in ins if b != a.shape] + [(b, d) for _, d, b, _ in outs]
    size = sum(math.prod(shape) * jnp.dtype(kind).itemsize for shape, kind in once + twice + twice)
    return pltpu.CompilerParams(vmem_limit_bytes=min(size + VALUES * MIB, 60 * MIB))


def swap(value, axis, bit):
    return lax.ppermute(value, axis, [(i, i ^ bit) for i in range(lax.axis_size(axis))])


def bits_of(size):
    return [1 << j for j in range(size.bit_length() - 1)]


def head_probs(query, key, valid):
    scores = lax.dot_general(query, key, (((1,), (1,)), ((), ())), preferred_element_type=jnp.float32)
    scores = jnp.where(valid, scores * (DH**-0.5), NEG)
    top = jnp.max(scores, axis=-1, keepdims=True)
    exps = jnp.exp(scores - top)
    return exps * (1.0 / jnp.sum(exps, axis=-1, keepdims=True))


def valid_mask(seq, length):
    rows = lax.broadcasted_iota(jnp.int32, (seq, seq), 0)
    cols = lax.broadcasted_iota(jnp.int32, (seq, seq), 1)
    return (cols <= rows) & (cols < length)


def forward_kernel(length_ref, q_ref, k_ref, v_ref, out_ref):
    seq, wide = q_ref.shape
    valid = valid_mask(seq, length_ref[0])
    for head in range(wide // DH):
        at = slice(head * DH, (head + 1) * DH)
        probs = head_probs(q_ref[:, at], k_ref[:, at], valid).astype(jnp.bfloat16)
        out_ref[:, at] = jnp.dot(probs, v_ref[:, at], preferred_element_type=jnp.float32).astype(out_ref.dtype)


def backward_kernel(length_ref, q_ref, k_ref, v_ref, one_ref, two_ref, *refs):
    dq_ref, dk_ref, dv_ref = refs[-3:]
    seq, wide = q_ref.shape
    valid = valid_mask(seq, length_ref[0])
    for head in range(wide // DH):
        at = slice(head * DH, (head + 1) * DH)
        query, key, value = q_ref[:, at], k_ref[:, at], v_ref[:, at]
        probs = head_probs(query, key, valid)
        d_attn = (one_ref[:, at].astype(jnp.float32) + two_ref[:, at].astype(jnp.float32)).astype(jnp.bfloat16)
        dv_ref[:, at] = lax.dot_general(
            probs.astype(jnp.bfloat16), d_attn, (((0,), (0,)), ((), ())), preferred_element_type=jnp.float32
        ).astype(dv_ref.dtype)
        dprob = lax.dot_general(d_attn, value, (((1,), (1,)), ((), ())), preferred_element_type=jnp.float32)
        delta = jnp.sum(dprob * probs, axis=-1, keepdims=True)
        ds = (probs * (dprob - delta) * (DH**-0.5)).astype(jnp.bfloat16)
        dq_ref[:, at] = jnp.dot(ds, key, preferred_element_type=jnp.float32).astype(dq_ref.dtype)
        dk_ref[:, at] = lax.dot_general(
            ds, query, (((0,), (0,)), ((), ())), preferred_element_type=jnp.float32
        ).astype(dk_ref.dtype)


def whole_kernel(low, count, at_ref, *refs):
    out = refs[-1]
    n, wide = refs[0].shape[0], out.shape[1]
    for i in range(count):
        block = refs[i][...] if refs[i].shape[1] == wide else refs[i][:, low : low + wide]
        if i == count - 1 and len(refs) - 1 > count:
            block = block + (refs[count][...] if refs[count].shape[1] == wide else refs[count][:, low : low + wide])
        out[pl.ds(pl.multiple_of(at_ref[i] * n, 16), n)] = block


def hidden_kernel(team, low, gathered, blocks, at_ref, *refs):
    if gathered:
        pieces, refs, attn_ref = refs[: sum(gathered)], refs[sum(gathered) : -1], refs[-1]
    else:
        attn_ref, refs = refs[0], refs[1:]
    weights, (gain_ref, *rest) = refs[:blocks], refs[blocks : blocks + 1 + team]
    hidden_ref, sent_ref, square_ref, weight_ref = refs[blocks + 1 + team :]
    n = rest[0].shape[0]

    def gather(i):
        row, column = 0, 0
        for piece in pieces[sum(gathered[:i]) : sum(gathered[: i + 1])]:
            attn_ref[row : row + n, column : column + piece.shape[1]] = piece[...]
            column += piece.shape[1]
            if column == attn_ref.shape[1]:
                row, column = row + n, 0

    def finish(i):
        for j in range(2):
            at = slice(j * n, (j + 1) * n)
            there = rest[2 * i + j]
            there = there[...] if there.shape[1] == pair.shape[1] else there[:, low : low + pair.shape[1]]
            hidden = there.astype(jnp.float32) + pair[at]
            hidden_ref[at] = hidden
            sent_ref[at] = (hidden * gain_ref[...]).astype(sent_ref.dtype)
            square_ref[j] = to_lanes(jnp.sum(hidden * hidden, axis=-1, keepdims=True))

    for i in range(team // 2 if gathered else 0):
        pl.when(pl.program_id(0) == i)(functools.partial(gather, i))
    pl.when(pl.program_id(0) == 0)(functools.partial(whole_kernel, low, at_ref.shape[0], at_ref, *weights, weight_ref))
    pair = jnp.dot(attn_ref[...], weight_ref[...], preferred_element_type=jnp.float32)
    for i in range(team // 2):
        pl.when(pl.program_id(0) == i)(functools.partial(finish, i))


def to_lanes(column):
    return jnp.transpose(jnp.broadcast_to(column, (column.shape[0], LANES)))[:1]


def to_column(row):
    return jnp.transpose(jnp.broadcast_to(row, (LANES, row.shape[1])))[:, :1]


def matched(hidden, sent, gain, inv, inv_other, weight):
    normed = hidden * inv
    diff = normed * gain - sent.astype(jnp.float32) * inv_other
    return normed, diff, weight * diff * gain


def match_kernel(hidden_ref, sent_ref, gain_ref, inv_ref, other_ref, weight_ref, *refs):
    n = inv_ref.shape[-1]
    for i in range(inv_ref.shape[0]):
        at = slice(i * n, (i + 1) * n)
        inv, other, weight = to_column(inv_ref[i]), to_column(other_ref[i]), to_column(weight_ref[i])
        normed, diff, scaled = matched(hidden_ref[at], sent_ref[at], gain_ref[...], inv, other, weight)
        square = to_lanes(jnp.sum(diff * diff, axis=-1, keepdims=True))
        cross = to_lanes(jnp.sum(normed * scaled, axis=-1, keepdims=True))
        if len(refs) > 1:
            square, cross = square + refs[0][i, :1], cross + refs[0][i, 1:]
        refs[-1][i, :1] = square
        refs[-1][i, 1:] = cross


def d_hidden_kernel(lows, at_ref, attn_ref, inv_ref, other_ref, weight_ref, mean_ref, *refs):
    d_ref, terms_ref, total_ref = refs[-3:]
    n, count = inv_ref.shape[-1], len(lows)
    for i in range(inv_ref.shape[0]):
        at = slice(i * n, (i + 1) * n)
        inv, other, weight = to_column(inv_ref[i]), to_column(other_ref[i]), to_column(weight_ref[i])
        mean = to_column(mean_ref[i])
        for low, hidden_ref, sent_ref, gain_ref in zip(lows, refs, refs[count:], refs[2 * count :]):
            normed, _, scaled = matched(hidden_ref[at], sent_ref[at], gain_ref[...], inv, other, weight)
            d_hidden = (inv * (scaled - normed * mean)).astype(d_ref.dtype)
            d_ref[at, low : low + d_hidden.shape[1]] = d_hidden
    terms = lax.dot_general(attn_ref[...], d_ref[...], (((0,), (0,)), ((), ())), preferred_element_type=jnp.float32)
    step, last = pl.program_id(0), pl.num_programs(0) - 1

    @pl.when(step == 0)
    def _():
        total_ref[...] = terms

    @pl.when((step > 0) & (step < last))
    def _():
        total_ref[...] += terms

    @pl.when(step == last)
    def _():
        terms_ref[...] = (total_ref[...] + terms).astype(terms_ref.dtype)


def terms_kernel(lows, at_ref, attn_ref, d_ref, *outs):
    terms = lax.dot_general(
        attn_ref[...], d_ref[...], (((0,), (0,)), ((), ())), preferred_element_type=jnp.float32
    ).astype(jnp.bfloat16)
    for low, out in zip(lows, outs):
        out[...] = terms[:, low : low + out.shape[1]]


def d_attn_kernel(lows, d_ref, *refs):
    outs = refs[len(lows) :]
    total = 0.0
    for low, weight_ref in zip(lows, refs):
        total = total + lax.dot_general(
            d_ref[:, low : low + weight_ref.shape[1]],
            weight_ref[...],
            (((1,), (1,)), ((), ())),
            preferred_element_type=jnp.float32,
        )
    total = total.astype(outs[0].dtype)
    n = outs[0].shape[1]
    for i, out in enumerate(outs):
        out[...] = total[:, i * n : (i + 1) * n]


def part_kernel(wide, places, member_ref, *refs):
    pieces, out, (wide_ref, sems) = refs[: len(places)], refs[-3], refs[-2:]
    copies = []
    for i, (ref, (other, low)) in enumerate(zip(pieces, places)):
        n = ref.shape[1]
        wide_ref[i, :, :n] = ref[...].astype(wide_ref.dtype)
        at = pl.multiple_of((member_ref[0] ^ other) * wide + low, LANES)
        copies.append(pltpu.make_async_copy(wide_ref.at[i, :, pl.ds(0, n)], out.at[:, pl.ds(at, n)], sems.at[i]))
        copies[-1].start()
    for copy in copies:
        copy.wait()


def put_parts(pieces, places, wide, width, member, into):
    rows, n = pieces[0].shape
    shape = jax.ShapeDtypeStruct((rows, width), jnp.float32)
    given = 1 + len(pieces)
    return pl.pallas_call(
        functools.partial(part_kernel, wide, places),
        grid_spec=pltpu.PrefetchScalarGridSpec(
            num_scalar_prefetch=1,
            grid=(1,),
            in_specs=[spec(p.shape, lambda i, *_: (0, 0), p.shape) for p in pieces] + [ANY] * len(into),
            out_specs=ANY,
            scratch_shapes=[pltpu.VMEM((len(pieces), rows, n), jnp.float32), pltpu.SemaphoreType.DMA((len(pieces),))],
        ),
        out_shape=shape,
        input_output_aliases={given: 0} if into else {},
        cost_estimate=cost(2.0),
        compiler_params=pltpu.CompilerParams(vmem_limit_bytes=32 * MIB),
    )(member.reshape(1), *pieces, *into)


def assemble_kernel(wide, places, member_ref, *refs):
    for ref, (other, low) in zip(refs[:-1], places):
        at = pl.multiple_of((member_ref[0] ^ other) * wide + low, LANES)
        refs[-1][:, pl.ds(at, ref.shape[1])] = ref[...].astype(refs[-1].dtype)


ANY = pl.BlockSpec(memory_space=pl.ANY)


def small_call(kernel, indices, ins, outs, into=None, micros=1.0, grid=1, scratch=(), most=False):
    out = pl.pallas_call(
        kernel,
        grid_spec=pltpu.PrefetchScalarGridSpec(
            num_scalar_prefetch=1,
            grid=(grid,),
            in_specs=[spec(b, m, a.shape) for a, b, m in ins] + [ANY] * (into is not None),
            out_specs=[pl.BlockSpec(b, m) for _, _, b, m in outs],
            scratch_shapes=list(scratch),
        ),
        out_shape=[jax.ShapeDtypeStruct(shape, d) for shape, d, _, _ in outs],
        input_output_aliases={} if into is None else {1 + len(ins): 0},
        cost_estimate=cost(micros),
        compiler_params=pltpu.CompilerParams(vmem_limit_bytes=60 * MIB) if most else room(ins, outs),
    )(jnp.stack([jnp.int32(i) for i in indices]), *[a for a, _, _ in ins], *(() if into is None else (into,)))
    return out


ORIGIN = lambda i, at: (0, 0)
DOWN = lambda i, at: (at[0], 0)


def split_kernel(count, at_ref, in_ref, *outs):
    for i in range(0, len(outs), count):
        at = at_ref[i // count]
        for out in outs[i : i + count]:
            n = out.shape[1]
            out[...] = in_ref[:, pl.ds(at if isinstance(at, int) else pl.multiple_of(at, LANES), n)]
            at = at + n


def cut_columns(array, places, widths):
    n = array.shape[0]
    if any(w % LANES for w in widths):
        return [lax.dynamic_slice(array, (0, p), (n, w)) for p in places for w in widths]
    outs = [((n, w), array.dtype, (n, w), ORIGIN) for _ in places for w in widths]
    return small_call(
        functools.partial(split_kernel, len(widths)), places, [(array, array.shape, ORIGIN)], outs
    )


def copy_kernel(at_ref, in_ref, *refs):
    refs[-1][...] = in_ref[...]


def place_rows(whole, piece, index):
    new = isinstance(whole, tuple)
    shape = whole if new else whole.shape
    outs = [(shape, piece.dtype, piece.shape, DOWN)]
    return small_call(copy_kernel, [index], [(piece, piece.shape, ORIGIN)], outs, None if new else whole)[0]


def take_rows(array, index, rows):
    block = (rows, array.shape[1])
    return small_call(copy_kernel, [index], [(array, block, DOWN)], [(block, array.dtype, block, ORIGIN)])[0]


def stack_kernel(across, at_ref, *refs):
    n, column = refs[0].shape[0], 0
    for i, ref in enumerate(refs[:-1]):
        row = i // across * n
        refs[-1][row : row + n, column : column + ref.shape[1]] = ref[...]
        column = (column + ref.shape[1]) % refs[-1].shape[1]


def pairs_kernel(at_ref, *refs):
    n, row, column = refs[0].shape[0], 0, 0
    for ref in refs[:-1]:
        refs[-1][row : row + n, column : column + ref.shape[1]] = ref[...]
        column += ref.shape[1]
        if column == refs[-1].shape[1]:
            row, column = row + n, 0


def stack_pairs(pairs):
    pieces = [x for pair in pairs for x in pair]
    n, width = pieces[0].shape[0], sum(x.shape[1] for x in pairs[0]) // 2
    shape = (2 * n * len(pairs), width)
    ins = [(x, x.shape, ORIGIN) for x in pieces]
    return small_call(pairs_kernel, [0], ins, [(shape, pieces[0].dtype, shape, ORIGIN)])[0]


def stack_blocks(rows):
    n = rows[0][0].shape[0]
    shape = (n * len(rows), sum(x.shape[1] for x in rows[0]))
    pieces = [x for row in rows for x in row]
    ins = [(x, x.shape, ORIGIN) for x in pieces]
    kernel = functools.partial(stack_kernel, len(rows[0]))
    return small_call(kernel, [0], ins, [(shape, pieces[0].dtype, shape, ORIGIN)])[0]


def add_kernel(low, at_ref, *refs):
    out_ref = refs[-1]
    total = 0.0
    for ref in refs[:-1]:
        n = out_ref.shape[1]
        part = ref[...] if ref.shape[1] == n else ref[:, low : low + n]
        total = total + part.astype(jnp.float32)
    out_ref[...] = total.astype(out_ref.dtype)


def sum_terms(got, low, terms, index):
    block = (got[0].shape[0], terms.shape[1])
    ins = [(g, g.shape, ORIGIN) for g in got] + [(terms, block, DOWN)]
    kernel = functools.partial(add_kernel, low)
    return small_call(kernel, [index], ins, [(block, terms.dtype, block, ORIGIN)])[0]


def fold_kernel(pieces, *refs):
    kept_ref, sent_ref = refs[2 * pieces :]
    half = kept_ref.shape[0]
    at = 0
    for near_ref, far_ref in zip(refs[:pieces], refs[pieces : 2 * pieces]):
        n = far_ref.shape[1]
        total = near_ref[...].astype(jnp.float32) + far_ref[...].astype(jnp.float32)
        total = total.astype(kept_ref.dtype)
        kept_ref[:, at : at + n] = total[:half]
        sent_ref[:, at : at + n] = total[half:]
        at += n


def fold(near, far):
    n, wide = near[0].shape[0], sum(x.shape[1] for x in near)
    ins = [(x, x.shape, lambda i: (0, 0)) for x in (*near, *far)]
    outs = [((n // 2, wide), near[0].dtype, (n // 2, wide), lambda i: (0, 0))] * 2
    return call(1.0, functools.partial(fold_kernel, len(near)), (1,), ins, outs)


def call(micros, kernel, grid, ins, outs):
    return pl.pallas_call(
        kernel,
        grid=grid,
        in_specs=[spec(b, m, a.shape) for a, b, m in ins],
        out_specs=[pl.BlockSpec(b, m) for _, _, b, m in outs],
        out_shape=[jax.ShapeDtypeStruct(s, d) for s, d, _, _ in outs],
        cost_estimate=cost(micros),
        compiler_params=room(ins, outs),
    )(*[a for a, _, _ in ins])


def attention_call(micros, kernel, length, arrays, moved, outs, first, number, group, into=None):
    seq = arrays[0].shape[0]
    there = pl.BlockSpec((seq, group), lambda i, *_: (0, i + first))
    here = pl.BlockSpec((seq, group), lambda i, *_: (0, i))
    alone = into is None
    into = into or ()
    shape = jax.ShapeDtypeStruct((seq, group * number) if alone else arrays[0].shape, jnp.bfloat16)
    given = 1 + len(arrays) + len(moved)
    return pl.pallas_call(
        kernel,
        grid_spec=pltpu.PrefetchScalarGridSpec(
            num_scalar_prefetch=1,
            grid=(number,),
            in_specs=[there] * len(arrays) + [here] * len(moved) + [pl.BlockSpec(memory_space=pl.ANY)] * len(into),
            out_specs=[here if alone else there] * outs,
        ),
        out_shape=[shape] * outs,
        input_output_aliases={given + i: i for i in range(len(into))},
        cost_estimate=cost(micros),
        compiler_params=vmem([((seq, group), jnp.bfloat16)] * (given - 1 + outs)),
    )(length.reshape(1), *arrays, *moved, *into)


def group_width(heads_width):
    heads = heads_width // DH
    return DH * max(g for g in (4, 2, 1) if heads % g == 0)


def tie(*values):
    return lax.optimization_barrier(values)


def split(values, *counts):
    lists, at = [], 0
    for count in counts:
        lists.append(list(values[at : at + count]))
        at += count
    return *lists, list(values[at:])


def send(value, axis, pairs):
    return lax.ppermute(value, axis, pairs)


LINE = 4
ENDS_OUT = [(2, 3), (1, 0)]
ENDS_IN = [(0, 1), (3, 2)]
MIDDLE = [(1, 2), (2, 1)]


def body(queries, keys, values, residual, event_ids, lengths, type_weight, w_out, gain):
    seq, heads_width = queries.shape[2:]
    width = residual.shape[3]
    parts = lax.axis_size("fsdp")
    team = lax.axis_size("dp")
    bits = bits_of(team)
    rows = team * seq
    shard_rows = w_out.shape[1]
    part = lax.axis_index("fsdp")
    member = lax.axis_index("dp")
    own = lax.axis_index(("dp", "fsdp"))
    length = lengths[own]
    count = jnp.sum(lengths).astype(jnp.float32)
    wide = width // team
    line = parts == LINE and shard_rows % LANES == 0
    two = line and wide % LANES == 0 and wide > LANES
    cut = -(-wide * 2 // (5 * LANES)) * LANES
    chunks = [(0, cut), (cut, wide)] if two else [(0, wide)]
    back_cut = -(-wide * 3 // (5 * LANES)) * LANES
    back_chunks = [(0, back_cut), (back_cut, wide)] if two else [(0, wide)]
    f32, bf16 = jnp.float32, jnp.bfloat16
    group = group_width(heads_width)
    steps = heads_width // group
    ends = sorted({0, steps // 5, 3 * steps // 5, steps})
    cuts = list(zip(ends[:-1], ends[1:]))
    q, k, v = queries[0, 0], keys[0, 0], values[0, 0]

    row_at = lambda i, *_: (i, 0)
    fixed = lambda i, *_: (0, 0)
    fixed3 = lambda i, *_: (0, 0, 0)
    stat_at = lambda i, *_: (i, 0, 0)
    lows = [low for low, _ in chunks]
    sizes = [high - low for low, high in chunks]

    order = [0]
    for bit in reversed(bits):
        order = order + [s ^ bit for s in order]

    column = (w_out[0], (shard_rows, wide), lambda i, at: (0, at[0]))
    if wide % LANES == 0:
        (block,) = small_call(copy_kernel, [member], [column], [((shard_rows, wide), bf16, (shard_rows, wide), ORIGIN)], most=True)
    else:
        (block,) = cut_columns(w_out[0], [member * wide], [wide])
    others = [1, 2] if line else list(range(1, parts))
    came = [swap(block, "fsdp", s) for s in others]

    attn = []
    middle = max(1, 2 * steps // 5)
    for first, final in [(0, middle), (middle, steps)] if steps > 1 else [(0, steps)]:
        attn += attention_call(
            1.5 * (final - first), forward_kernel, length, (q, k, v), (), 1, first, final - first, group
        )
    far = [swap(a, "dp", bits[-1]) for a in attn]
    if team == 4:
        attn.append(stack_blocks([attn]))
    home, _ = tie(residual[0, 0], attn[-1])
    mine = cut_columns(home, [(member ^ s) * wide for s in order], [wide])
    if team == 4:
        mine = [mine[0], mine[2], stack_blocks([[mine[1]], [mine[3]]])]
    own_parts = attn
    tied = tie(*came, block, count, *own_parts, *far, *mine)
    came, (block, count), own_parts, far, mine = split(tied, len(others), 2, len(own_parts), len(far))

    last = [send(block, "fsdp", MIDDLE), send(came[1], "fsdp", ENDS_OUT)] if line else []
    pairs = [[*own_parts[: len(far)], *far]]
    if team == 4:
        pairs.append([swap(x, "dp", 1) for x in (own_parts[-1], *far)])
    else:
        for bit in reversed(bits[:-1]):
            pairs = pairs + [[swap(x, "dp", bit) for x in pair] for pair in pairs]
    pairs = [stack_pairs(pairs)]
    each = []
    if team == 4:
        here, beside, across = mine
        across = swap(across, "dp", 2)
        passed_on = swap(stack_blocks([[beside], [take_rows(across, 1, seq)]]), "dp", 1)
        rest = [here, across, passed_on]
    else:
        rest = [swap(piece, "dp", s) if s else piece for s, piece in zip(order, mine)]
    (attn,) = pairs
    spots = [part, *[part ^ s for s in others], *([part ^ 3] if line else [])]
    shapes = [(heads_width, n) for n in sizes]

    used = [block, *came, *last]

    def team_sum(value):
        shape = value.shape
        value = value.reshape((2,) * len(bits) + shape[1:])
        for axis, bit in enumerate(bits):
            value = value + jnp.flip(swap(value, "dp", bit), axis)
        return value.reshape(shape)

    my_gain = lax.dynamic_slice(gain[0], (member * wide,), (wide,))[None]
    gains = [my_gain[:, low:high] for low, high in chunks]
    tall = rows // 2

    lower = lambda i, *_: (1, 0)
    rest_blocks = [(a, fixed) for a in rest]
    if team == 4:
        rest_blocks = [(rest[0], fixed), (rest[1], fixed), (rest[2], fixed), (rest[2], lower)]
    hidden, sent, square, partner, weights = [], [], [], [], []
    for i, n in enumerate(sizes):
        first = used
        if i:
            square[0], *first = tie(square[0], *used)
        narrow = i == 0 and two
        across = n if narrow else wide
        ins = [(a, (shard_rows, across) if line else a.shape, fixed) for a in first] + [(gains[i], (1, n), fixed)]
        ins += [(a, (seq, across), m) for a, m in rest_blocks]
        outs = [
            ((rows, n), f32, (2 * seq, n), row_at),
            ((rows, n), bf16, (2 * seq, n), row_at),
            ((team, 1, seq), f32, (2, 1, seq), stat_at),
            (shapes[i], bf16, shapes[i], fixed),
        ]
        whole = ((rows, heads_width), bf16, (2 * seq, heads_width), row_at)
        ins = [(attn, whole[2], row_at), *ins]
        kernel = functools.partial(hidden_kernel, team, lows[i], [] if i else each, len(used))
        h, x, sq, weight, *new = small_call(kernel, spots, ins, outs, micros=2.0, grid=team // 2)
        weights.append(weight)
        if i + 1 < len(chunks):
            partner.append(swap(x, "copy", 1))
        hidden.append(h)
        sent.append(x)
        square.append(sq)
    inv = lax.rsqrt(team_sum(sum(square)) / width + 1e-06)
    inv_other = swap(inv, "copy", 1)
    partner.append(swap(sent[-1], "copy", 1))

    types = jnp.arange(type_weight.shape[0], dtype=jnp.int32)
    ids, _ = tie(event_ids, x)
    matches = ids[0][:, None] == types[None, :]
    looked_up = jnp.sum(jnp.where(matches, type_weight[None, :], f32(0.0)), axis=-1)
    tok_w = jnp.where(jnp.arange(seq, dtype=jnp.int32) < length, looked_up, f32(0.0))
    tok_w = tok_w.reshape(1, 1, seq)
    for bit in reversed(bits):
        tok_w = jnp.concatenate([tok_w, swap(tok_w, "dp", bit)], axis=0)
    row_scale = 2.0 * tok_w / (width * count)
    stats = [inv, inv_other, row_scale]

    both = []
    for i in range(len(chunks)):
        n = sizes[i]
        (found,) = call(
            3.0,
            match_kernel,
            (team // 2,),
            [(hidden[i], (2 * seq, n), row_at), (partner[i], (2 * seq, n), row_at), (gains[i], (1, n), fixed)]
            + [(a, (2, *a.shape[1:]), stat_at) for a in (*stats, *both[-1:])],
            [((team, 2, seq), f32, (2, 2, seq), stat_at)],
        )
        if i + 1 < len(chunks):
            found, partner[i + 1] = tie(found, partner[i + 1])
        both.append(found)
    both = team_sum(both[-1])
    loss = jnp.sum(tok_w[0] * both[0, :1]) / (width * count)
    mean = both[:, 1:] / width

    back_lows = [low for low, _ in back_chunks]
    back_sizes = [high - low for low, high in back_chunks]
    columns = shard_rows if line else heads_width
    d_hidden, terms = small_call(
        functools.partial(d_hidden_kernel, lows),
        [part ^ 3 if line else 0],
        [(attn, (2 * seq, columns), lambda i, at: (i, at[0]))]
        + [(x, (2, 1, seq), stat_at) for x in (*stats, mean)]
        + [(x, (2 * seq, x.shape[1]), lambda i, at: (i, 0)) for x in (*hidden, *partner)]
        + [(x, x.shape, fixed) for x in gains],
        [((rows, wide), bf16, (2 * seq, wide), lambda i, at: (i, 0)), ((columns, wide), bf16, (columns, wide), fixed)],
        grid=team // 2,
        scratch=[pltpu.VMEM((columns, wide), f32)],
        micros=4.0,
    )
    if line:
        early = [send(terms, "fsdp", MIDDLE), send(terms, "fsdp", ENDS_IN)]
        terms = small_call(
            functools.partial(terms_kernel, back_lows),
            [part ^ 1, part ^ 2, part],
            [(attn, (rows, shard_rows), lambda i, at: (0, at[i])), (d_hidden, (rows, wide), fixed)],
            [((3 * shard_rows, n), bf16, (shard_rows, n), lambda i, at: (i, 0)) for n in back_sizes],
            micros=4.0,
            grid=3,
        )
    else:
        early = [swap(take_rows(terms, part ^ s, shard_rows), "fsdp", s) for s in range(1, parts)]
        terms = [terms]

    across, each = group, 1

    def d_attn_rows(half, d_hidden, first, count):
        n = across * count
        return call(
            0.6 * count,
            functools.partial(d_attn_kernel, lows),
            (1,),
            [(d_hidden, (tall, wide), lambda i: (half, 0))]
            + [(w, (n, w.shape[1]), lambda i: (first // count, 0)) for w in weights],
            [((tall, across), bf16, (tall, across), fixed)] * count,
        )

    def d_attn_parts(half, d_hidden):
        total = heads_width // across
        parts = [(i, 1) for i in range(total)]
        return [x for first, count in parts for x in d_attn_rows(half, d_hidden, first, count)]

    far = [swap(x, "dp", bits[0]) for x in d_attn_parts(1, d_hidden)]
    near = d_attn_parts(0, d_hidden)
    for bit in bits[1:-1]:
        near, far = zip(*[fold([x], [y]) for x, y in zip(near, far)])
        far = [swap(x, "dp", bit) for x in far]
    folded = [fold(near[each * first : each * final], far[each * first : each * final]) for first, final in cuts]
    kept, passed = zip(*folded)
    passed = [swap(passed[0], "dp", bits[-1]), *passed[1:]]
    near_terms = [take_rows(x, 0, shard_rows) for x in terms] if line else []
    tied = tie(*early, *terms, *kept, *passed, *near_terms)
    early, terms, kept, passed, near_terms = split(tied, len(early), len(back_chunks), len(cuts), len(cuts))

    def late_sends(i):
        if not line:
            return []
        beyond = sum_terms([early[1]], back_lows[i], terms[i], 1)
        return [swap(beyond, "fsdp", 2), swap(near_terms[i], "fsdp", 1)]

    def team_pieces(i, got):
        got = early[:1] + got if line else early
        total = sum_terms(got, back_lows[i], terms[i], 2 if line else part)
        pieces = {0: total}
        for bit in reversed(bits):
            pieces.update({s ^ bit: swap(p, "dp", bit) for s, p in pieces.items()})
        return [pieces[s] for s in order]

    def back(j, grads):
        first, last = cuts[j]
        arrays = (q, k, v), (kept[j], passed[j])
        micros = 1.5 * (last - first) + 1.0
        return attention_call(micros, backward_kernel, length, *arrays, 3, first, last - first, group, grads)

    got = late_sends(0)
    passed = [passed[0], *[swap(x, "dp", bits[-1]) for x in passed[1:]]]
    grads = back(0, ())
    backed = max(1, len(cuts) - 1)
    for j in range(1, backed):
        grads = back(j, grads)
    early_parts = passed
    tied = tie(*got, *grads, *terms, *early, *near_terms, loss, *early_parts)
    got, grads, terms, early, near_terms, (loss,), early_parts = split(
        tied, len(got), 3, len(back_chunks), len(early), len(near_terms), 1
    )
    passed = [*early_parts, *passed[len(early_parts) :]]

    placed = []
    for i in range(1, len(back_chunks)):
        late = late_sends(i)
        placed += team_pieces(i - 1, got)
        if i == 1:
            for j in range(backed, len(cuts)):
                grads = back(j, grads)
        tied = tie(*late, *grads)
        got, grads, _ = split(tied, len(late), 3)
    placed += team_pieces(len(back_chunks) - 1, got)
    if len(back_chunks) == 1:
        for j in range(backed, len(cuts)):
            grads = back(j, grads)
    d_queries, d_keys, d_values = grads
    places = [(s, low) for low in back_lows for s in order]

    if two:
        out = ()
        for i in range(0, len(placed), team):
            out = (put_parts(placed[i : i + team], places[i : i + team], wide, width, member, out),)
        (out,) = out
    elif wide % LANES == 0:
        tall = next(t for t in (128, 64, 32, 16, shard_rows) if shard_rows % t == 0)
        out = pl.pallas_call(
            functools.partial(assemble_kernel, wide, places),
            grid_spec=pltpu.PrefetchScalarGridSpec(
                num_scalar_prefetch=1,
                grid=(shard_rows // tall,),
                in_specs=[pl.BlockSpec((tall, p.shape[1]), lambda i, *_: (i, 0)) for p in placed],
                out_specs=pl.BlockSpec((tall, width), lambda i, *_: (i, 0)),
            ),
            out_shape=jax.ShapeDtypeStruct((shard_rows, width), f32),
            cost_estimate=cost(1.0),
            compiler_params=vmem([((tall, width), bf16), ((tall, width), f32)]),
        )(member.reshape(1), *placed)
    else:
        out = jnp.zeros((shard_rows, width), f32)
        for piece, (s, low) in zip(placed, places):
            out = lax.dynamic_update_slice(out, piece.astype(f32), (0, (member ^ s) * wide + low))
    return (
        loss.reshape(1, 1),
        d_queries[None, None],
        d_keys[None, None],
        d_values[None, None],
        out[None],
    )


def solution(mesh):
    whole = P("copy", ("dp", "fsdp"), None, None)
    in_specs = (
        whole,
        whole,
        whole,
        whole,
        P(("dp", "fsdp"), None),
        P(),
        P(),
        P("copy", "fsdp", None),
        P("copy", None),
    )
    out_specs = (P("copy", ("dp", "fsdp")), whole, whole, whole, P("copy", "fsdp", None))
    return jax.shard_map(body, mesh=mesh, in_specs=in_specs, out_specs=out_specs, check_vma=False)
```
